32 devices in a mesh: section: 2 (over x), seq: 4 (over y, core), tensor: 4 (over z).
Axes of the slice: x: 2, y: 2, z: 4, core: 2. Of those that a mesh axis runs over, the one named last changes fastest.
Arguments:
- block_input: bfloat16 [4, 4, 1024, 1280], P(None, 'tensor', 'seq'), may hold values from -6 to 6
- cotangent: bfloat16 [4, 4, 1024, 1280], P(None, 'tensor', 'seq'), may hold values from -6 to 6
- mask: int32 [4, 4, 1024], P(None, 'tensor', 'seq'), may hold values 0 or 1
- conv_in: bfloat16 [2, 1280, 640], P('section', None, 'tensor'), may hold values from -0.15625 to 0.15625
- bias_in: bfloat16 [2, 640], P('section', 'tensor'), may hold values from -2 to 2
- conv_mid: bfloat16 [2, 5, 640, 640], P('section', None, None, 'tensor'), may hold values from -0.109375 to 0.109375
- bias_mid: bfloat16 [2, 640], P('section', 'tensor'), may hold values from -2 to 2
- conv_out: bfloat16 [2, 640, 1280], P('section', 'tensor'), may hold values from -0.25 to 0.25
- bias_out: bfloat16 [2, 1280], P('section', 'tensor'), may hold values from -2 to 2
- gain_first: bfloat16 [2, 1280], P('section', 'tensor'), may hold values from 0.5 to 1.5
- shift_first: bfloat16 [2, 1280], P('section', 'tensor'), may hold values from -2 to 2
- gain_second: bfloat16 [2, 640], P('section', 'tensor'), may hold values from 0.5 to 1.5
- shift_second: bfloat16 [2, 640], P('section', 'tensor'), may hold values from -2 to 2
- gain_third: bfloat16 [2, 640], P('section', 'tensor'), may hold values from 0.5 to 1.5
- shift_third: bfloat16 [2, 640], P('section', 'tensor'), may hold values from -2 to 2
Outputs:
- block_out: bfloat16 [2, 4, 4, 1024, 1280], P('section', None, 'tensor', 'seq')
- input_grad: bfloat16 [2, 4, 4, 1024, 1280], P('section', None, 'tensor', 'seq')
- grad_conv_in: float32 [2, 1280, 640], P('section', None, 'tensor')
- grad_bias_in: float32 [2, 640], P('section', 'tensor')
- grad_conv_mid: float32 [2, 5, 640, 640], P('section', None, None, 'tensor')
- grad_bias_mid: float32 [2, 640], P('section', 'tensor')
- grad_conv_out: float32 [2, 640, 1280], P('section', 'tensor')
- grad_bias_out: float32 [2, 1280], P('section', 'tensor')
- grad_gain_first: float32 [2, 1280], P('section', 'tensor')
- grad_shift_first: float32 [2, 1280], P('section', 'tensor')
- grad_gain_second: float32 [2, 640], P('section', 'tensor')
- grad_shift_second: float32 [2, 640], P('section', 'tensor')
- grad_gain_third: float32 [2, 640], P('section', 'tensor')
- grad_shift_third: float32 [2, 640], P('section', 'tensor')
The draws below stay inside these ranges and needn't reach their ends.
All inputs are finite; a program needn't handle non-finite values. No bound on the sum of `mask` on one device may be relied on, other than what follows from the above.
Results may differ from the reference program's by a relative error of at most 0.012.
Values may be sent and summed in bfloat16 or wider, within the bound.
A program may use at most 256 MiB of HBM per device.

```python
import jax
import jax.numpy as jnp
from jax import lax

D = 1280
H = 640
KERNEL = 5
DILATION_BASE = 64
MICRO = 4
PROT = 4
LEN = 1024


def plant(drawn, rng, smallest, high):
    spot = [jax.random.randint(jax.random.fold_in(rng, axis), (), 0, length) for axis, length in enumerate(drawn.shape)]
    widest = drawn.shape.index(max(drawn.shape))
    next_to = spot[:widest] + [(spot[widest] + 1) % drawn.shape[widest]] + spot[widest + 1:]
    return drawn.at[tuple(spot)].set(smallest).at[tuple(next_to)].set(high)


def block_levels(key, extent, cuts, low, top_value):
    def one(axis_at, shards_of):
        heights = jax.random.uniform(jax.random.fold_in(jax.random.fold_in(key, 6), axis_at), (shards_of,), jnp.float32, low / len(cuts), top_value / len(cuts))
        return jnp.repeat(jnp.exp(heights), extent[axis_at] // shards_of).reshape((-1,) + (1,) * (len(extent) - axis_at - 1))

    loudness = one(*cuts[0])
    for cut in cuts[1:]:
        loudness = loudness * one(*cut)
    return loudness


def normal_values(rng, extent, deviation, bound, shards=(), held_as=jnp.bfloat16):
    values = deviation * jax.random.normal(rng, extent, jnp.float32)
    if shards:
        values = values * block_levels(rng, extent, shards, -0.22, 0.18)
    return jnp.clip(values, -bound, bound).astype(held_as)


def setup_inputs(seed: int = 0) -> dict:
    keys = jax.random.split(jax.random.key(seed), 16)
    return {
        "block_input": normal_values(keys[0], (MICRO, PROT, LEN, D), 1.0, 6.0, ((1, 4), (2, 4))),
        "cotangent": normal_values(keys[1], (MICRO, PROT, LEN, D), 1.0, 6.0, ((1, 4), (2, 4))),
        "mask": plant((jax.random.randint(keys[2], (MICRO, PROT, LEN), 0, 2) < 1).astype(jnp.int32), jax.random.fold_in(keys[2], 1), 0, 1),
        "conv_in": normal_values(keys[3], (2, D, H), D ** -0.5, 0.15625, ((0, 2), (2, 4))),
        "bias_in": normal_values(keys[4], (2, H), 0.3, 2.0, ((0, 2), (1, 4))),
        "conv_mid": normal_values(keys[5], (2, KERNEL, H, H), (KERNEL * H) ** -0.5, 0.109375, ((0, 2), (3, 4))),
        "bias_mid": normal_values(keys[6], (2, H), 0.3, 2.0, ((0, 2), (1, 4))),
        "conv_out": normal_values(keys[7], (2, H, D), H ** -0.5, 0.25, ((0, 2), (1, 4))),
        "bias_out": normal_values(keys[8], (2, D), 0.3, 2.0, ((0, 2), (1, 4))),
        "gain_first": jnp.clip(1.0 + 0.1 * jax.random.normal(keys[9], (2, D), jnp.float32), 0.5, 1.5).astype(jnp.bfloat16),
        "shift_first": normal_values(keys[10], (2, D), 0.3, 2.0, ((0, 2), (1, 4))),
        "gain_second": jnp.clip(1.0 + 0.1 * jax.random.normal(keys[11], (2, H), jnp.float32), 0.5, 1.5).astype(jnp.bfloat16),
        "shift_second": normal_values(keys[12], (2, H), 0.3, 2.0, ((0, 2), (1, 4))),
        "gain_third": jnp.clip(1.0 + 0.1 * jax.random.normal(keys[13], (2, H), jnp.float32), 0.5, 1.5).astype(jnp.bfloat16),
        "shift_third": normal_values(keys[14], (2, H), 0.3, 2.0, ((0, 2), (1, 4))),
    }


EPS = 1e-05

@jax.custom_vjp
def low(v):
    return lax.optimization_barrier(v.astype(jnp.bfloat16)).astype(jnp.float32)

@jax.custom_vjp
def low_back(v):
    return v

def low_keep(v):
    return (low(v), None)

def low_pass(kept, grad):
    return (grad,)

def back_keep(v):
    return (v, None)

def back_low(kept, grad):
    return (low(grad),)
low.defvjp(low_keep, low_pass)
low_back.defvjp(back_keep, back_low)

def layer_norm(value, gain, shift):
    mean = lax.optimization_barrier(jnp.mean(value, axis=-1, keepdims=True))
    spread = lax.optimization_barrier(jnp.mean(value * value, axis=-1, keepdims=True)) - mean * mean
    return (value - mean) * lax.rsqrt(spread + EPS) * gain + shift

def dilated(active, kernel, dilation_rate):
    length = active.shape[0]
    padded = jnp.pad(active, ((2 * dilation_rate, 2 * dilation_rate), (0, 0)))
    total = jnp.zeros((length, kernel.shape[2]), jnp.float32)
    for tap in range(KERNEL):
        rows = padded[tap * dilation_rate:tap * dilation_rate + length]
        total = total + jnp.dot(rows, kernel[tap], precision=lax.Precision.HIGHEST)
    return total

def residual_block(entry_values, block_parameters, dilation_rate):
    conv_in, bias_in, conv_mid, bias_mid, conv_out, bias_out, gain_first, shift_first, gain_second, shift_second, gain_third, shift_third = block_parameters
    entry_values = low_back(entry_values)
    active_one = low(jax.nn.gelu(layer_norm(entry_values, gain_first, shift_first), approximate=False))
    hidden_one = low_back(jnp.dot(active_one, conv_in, precision=lax.Precision.HIGHEST) + bias_in)
    active_two = low(jax.nn.gelu(layer_norm(hidden_one, gain_second, shift_second), approximate=False))
    hidden_two = low_back(dilated(active_two, conv_mid, dilation_rate) + bias_mid)
    active_three = low(jax.nn.gelu(layer_norm(hidden_two, gain_third, shift_third), approximate=False))
    return low(entry_values + (jnp.dot(active_three, conv_out, precision=lax.Precision.HIGHEST) + bias_out))

def reference(block_input, cotangent, mask, conv_in, bias_in, conv_mid, bias_mid, conv_out, bias_out, gain_first, shift_first, gain_second, shift_second, gain_third, shift_third):
    stacked = (conv_in, bias_in, conv_mid, bias_mid, conv_out, bias_out, gain_first, shift_first, gain_second, shift_second, gain_third, shift_third)
    first_params = tuple((member[0].astype(jnp.float32) for member in stacked))
    second_params = tuple((member[1].astype(jnp.float32) for member in stacked))
    entries = block_input.astype(jnp.float32).reshape(MICRO * PROT, LEN, D)
    upstreams = (cotangent.astype(jnp.float32) * mask[..., None].astype(jnp.float32)).reshape(MICRO * PROT, LEN, D)

    def first_block(entry_values, block_parameters):
        return residual_block(entry_values, block_parameters, DILATION_BASE)

    def second_block(entry_values, block_parameters):
        return residual_block(entry_values, block_parameters, 2 * DILATION_BASE)

    def protein(carry, member):
        entry_values, upstream = member
        middle, back_first = jax.vjp(first_block, entry_values, first_params)
        leaving, back_second = jax.vjp(second_block, middle, second_params)
        grad_middle, second_grads = back_second(upstream)
        grad_entry, first_grads = back_first(grad_middle)
        carry = (jax.tree.map(jnp.add, carry[0], first_grads), jax.tree.map(jnp.add, carry[1], second_grads))
        return (carry, (middle, leaving, grad_entry, grad_middle))
    zero_first = tuple((jnp.zeros_like(member) for member in first_params))
    zero_second = tuple((jnp.zeros_like(member) for member in second_params))
    sums, outputs = lax.scan(protein, (zero_first, zero_second), (entries, upstreams))
    middles, leavings, grad_entries, grad_middles = outputs
    shape = (MICRO, PROT, LEN, D)
    block_out = jnp.stack([middles.reshape(shape), leavings.reshape(shape)]).astype(jnp.bfloat16)
    input_grad = jnp.stack([grad_entries.reshape(shape), grad_middles.reshape(shape)]).astype(jnp.bfloat16)
    gradients = tuple((jnp.stack([first_part, second_part]) for first_part, second_part in zip(sums[0], sums[1])))
    return (block_out, input_grad, gradients[0], gradients[1], gradients[2], gradients[3], gradients[4], gradients[5], gradients[6], gradients[7], gradients[8], gradients[9], gradients[10], gradients[11])
```

```python
import functools

import jax
import jax.numpy as jnp
from jax import lax
from jax.experimental import pallas as pl
from jax.experimental.pallas import tpu as pltpu
from jax.sharding import PartitionSpec as P

DILATION_BASE = 64
EPS = 1e-05
ROOT_HALF = 0.7071067811865476
INVERSE_ROOT_TWO_PI = 0.3989422804014327
MESH = pl.DeviceIdType.MESH
f32 = jnp.float32
bf16 = jnp.bfloat16

MICRO = 4
LEN = 256
H = 640
ROWS = MICRO * LEN
SHARDS = 4
PART = H // SHARDS
HALF = PART // 2
BLOCKS = 9
TILE = 64
NN = (((1,), (0,)), ((), ()))
NT = (((1,), (1,)), ((), ()))
TN = (((0,), (0,)), ((), ()))
ORDER = (2, 3, 4, 5, 6, 7, 8, 0, 1)
E_AT, SX_AT, LV_AT, POOL_ROWS = 0, 2 * ROWS, 4 * ROWS, 6 * ROWS
KEEP_AT, GIVE_AT = 0, BLOCKS * SHARDS * HALF


def dot(a, b, dims):
    return lax.dot_general(a, b, dims, preferred_element_type=f32)


def loop(count, body):
    def step(i, carry):
        body(i)
        return carry

    lax.fori_loop(0, count, step, 0)


def row_stats(parts, width):
    mean = sum(jnp.sum(x, axis=-1, keepdims=True) for x in parts) / width
    spread = sum(jnp.sum(x * x, axis=-1, keepdims=True) for x in parts) / width - mean * mean
    return mean, lax.rsqrt(spread + EPS)


def gelu_slope(v):
    phi = 0.5 * (1.0 + lax.erf(v * ROOT_HALF))
    return phi, phi + v * (jnp.exp(-0.5 * v * v) * INVERSE_ROOT_TWO_PI)


def norm_back(ys, normeds, inverse, gains, width):
    scaled = [y * g for y, g in zip(ys, gains)]
    total = sum(jnp.sum(s, axis=-1, keepdims=True) for s in scaled) / width
    along = sum(jnp.sum(s * n, axis=-1, keepdims=True) for s, n in zip(scaled, normeds)) / width
    return [inverse * (s - total - n * along) for s, n in zip(scaled, normeds)]


def eights(x):
    return jnp.sum(x.reshape(x.shape[0] // 8, 8, x.shape[1]), axis=0)


def relay_kernel(fused, *refs):
    if fused:
        (xin, cot, mask, wsh, vsh, bo, ig, gout, vout) = refs[:9]
        rest = refs[9:]
    else:
        (xin, cot, mask, wfull, wother, v640_in, v1280_in, vx_in, bo, ig, gout, vout) = refs[:12]
        rest = refs[12:]
    (W, WX, POOL, A1, S1, A2, S2, N2, A3, S3, N3, U, GM, GH, XR, MU, IV1, IV2, IV3, MUX, IVX, MK, TG, V640, V1280, VX, AC, VS) = rest[:28]
    (l_in, l_w, o_bo, o_ig, x_s, x_r, ha_s, ha_r, hg_s, hg_r) = rest[28:38]
    if fused:
        (VG, CR, YR, ZR, YX, F, VR, vg_s, vg_r, gz_s, gz_r, gy_s, gy_r, gc_s, gc_r, wx_s, wx_r, wc_s, wc_r, rc_s, rc_r, ry_s, ry_r, rz_s, rz_r, fy_s, fy_r, fc_s, fc_r, vr_s, vr_r, o_g) = rest[38:]
    else:
        (o_g,) = rest[38:]

    sec = lax.axis_index("section")
    seq = lax.axis_index("seq")
    ten = lax.axis_index("tensor")
    y = seq // 2
    core = lax.rem(seq, 2)
    at_core = (sec, y * 2 + (1 - core), ten)
    at_y = (sec, (1 - y) * 2 + core, ten)
    at_diag = (sec, (1 - y) * 2 + (1 - core), ten)
    at_x = (1 - sec, seq, ten)
    up, down = (sec, seq, ten + 1), (sec, seq, ten - 1)
    behind, ahead = (sec, seq - 1, ten), (sec, seq + 1, ten)
    first = sec == 0

    def remote(src, dst, send, recv, where):
        return pltpu.make_async_remote_copy(src_ref=src, dst_ref=dst, send_sem=send, recv_sem=recv, device_id=where, device_id_type=MESH)

    def rows(base, m, r=0, n=LEN):
        return pl.ds(pl.multiple_of(base + m * LEN + r, 16), n)

    def load_in(m, h, ref, into):
        return pltpu.make_async_copy(ref.at[m, :, pl.ds(h * H, H)], into, l_in.at[m, h, 0 if ref is xin else 1])

    for m in range(MICRO):
        for h in range(2):
            load_in(m, h, xin, POOL.at[pl.ds(E_AT + h * ROWS + m * LEN, LEN), :]).start()
            load_in(m, h, cot, U.at[h, pl.ds(m * LEN, LEN), :]).start()
    if fused:
        own_w = pltpu.make_async_copy(wsh, W.at[:, pl.ds(pl.multiple_of(ten * PART, 16), PART), :], l_w.at[0])
        own_v = pltpu.make_async_copy(vsh, VG.at[sec, ten], l_w.at[1])
        own_w.start()
        own_v.start()
        partners = [at_core, at_y, at_diag]
        others = [(s, d) for s in range(2) for d in range(SHARDS) if s or d]
        partners += [(lax.rem(sec + s, 2), seq, lax.rem(ten + d, SHARDS)) for s, d in others]
    else:
        own_w = pltpu.make_async_copy(wfull, W, l_w.at[0])
        own_v = pltpu.make_async_copy(wother, WX, l_w.at[1])
        own_w.start()
        own_v.start()
        partners = [at_core, at_diag, at_x]

    barrier = pltpu.get_barrier_semaphore()
    for partner in partners:
        pl.semaphore_signal(barrier, inc=1, device_id=partner, device_id_type=MESH)
    pl.semaphore_wait(barrier, len(partners))

    def piece(ref, b, s, half):
        return ref.at[b, pl.ds(pl.multiple_of(s * PART + half * HALF, 16), HALF), :]

    def gz(b, s, to_up, src=None):
        spot = piece(W, b, s, core)
        return remote(spot if src is None else src, spot, gz_s.at[b, s, 0 if to_up else 1], gz_r.at[b, s], up if to_up else down)

    def gy(b, s):
        spot = piece(W, b, s, core)
        return remote(spot, spot, gy_s.at[b, s], gy_r.at[b, s], at_y)

    def gc(b, s, half):
        spot = piece(W, b, s, half)
        return remote(spot, spot, gc_s.at[b, s], gc_r.at[b, s], at_core)

    def gx():
        b = jnp.where(first, 2 + core, core)
        return remote(W.at[b], WX.at[core], wx_s.at[0], wx_r.at[0], at_x)

    def gxc(half):
        return remote(WX.at[half], WX.at[half], wc_s.at[0], wc_r.at[0], at_core)

    def gather():
        mine = lambda b: jnp.logical_or(b == BLOCKS - 1, lax.rem(b, 2) == y)
        own_v.wait()
        for i, (s, d) in enumerate(others):
            remote(VG.at[sec, ten], VG.at[sec, ten], vg_s.at[i], vg_r.at[i], (lax.rem(sec + s, 2), seq, lax.rem(ten + d, SHARDS))).start()

        def send_own(b):
            src = wsh.at[b, pl.ds(pl.multiple_of(core * HALF, 16), HALF), :]

            @pl.when(jnp.logical_and(mine(b), ten < SHARDS - 1))
            def _():
                gz(b, ten, True, src).start()

            @pl.when(jnp.logical_and(mine(b), ten > 0))
            def _():
                gz(b, ten, False, src).start()

        loop(BLOCKS, send_own)

        def step(k):
            for d in range(1, SHARDS):
                b = k - (d - 1)
                ok = jnp.logical_and(b >= 0, b < BLOCKS)
                for above in (False, True):
                    s = ten + d if above else ten - d
                    there = jnp.logical_and(ok, s < SHARDS if above else s >= 0)
                    onward = (ten > 0) if above else (ten < SHARDS - 1)

                    @pl.when(jnp.logical_and(there, mine(b)))
                    def _():
                        gz(b, s, True).wait_recv()

                        @pl.when(onward)
                        def _():
                            gz(b, s, not above).start()

                        @pl.when(b < BLOCKS - 1)
                        def _():
                            gy(b, s).start()

                        gc(b, s, core).start()

            for d in range(1, SHARDS):
                b = k - d
                ok = jnp.logical_and(b >= 0, b < BLOCKS)
                for above in (False, True):
                    s = ten + d if above else ten - d
                    there = jnp.logical_and(ok, s < SHARDS if above else s >= 0)

                    @pl.when(jnp.logical_and(there, jnp.logical_not(mine(b))))
                    def _():
                        gy(b, s).wait_recv()
                        gc(b, s, core).start()

            b = k - 4
            for s in range(SHARDS):

                @pl.when(jnp.logical_and(jnp.logical_and(b >= 0, b < BLOCKS), s != ten))
                def _():
                    gc(b, s, 1 - core).wait_recv()

            @pl.when(b == jnp.where(first, 2 + core, core))
            def _():
                gx().start()

        loop(BLOCKS + 4, step)

        def drain(b):
            for s in range(SHARDS):
                fromabove = s > ten

                @pl.when(jnp.logical_and(mine(b), jnp.logical_and(s <= ten, ten < SHARDS - 1)))
                def _():
                    gz(b, s, True).wait_send()

                @pl.when(jnp.logical_and(mine(b), jnp.logical_and(s >= ten, ten > 0)))
                def _():
                    gz(b, s, False).wait_send()

                @pl.when(s != ten)
                def _():
                    gc(b, s, core).wait_send()

                    @pl.when(jnp.logical_and(mine(b), b < BLOCKS - 1))
                    def _():
                        gy(b, s).wait_send()

        loop(BLOCKS, drain)
        gx().wait_recv()
        gxc(core).start()

    def vectors():
        for i, (s, d) in enumerate(others):
            remote(VG.at[sec, ten], VG.at[sec, ten], vg_s.at[i], vg_r.at[i], at_x).wait()
        line = lax.broadcasted_iota(jnp.int32, (2 * 128, H), 0)
        col = lax.broadcasted_iota(jnp.int32, (2 * 128, H), 1)

        def pick(offset):
            return jnp.where(col == line + offset, 1.0, 0.0).astype(bf16)

        narrow = jnp.zeros((16, H), f32)
        wide = [[jnp.zeros((16, H), f32) for _ in range(4)] for _ in range(2)]
        for s in range(SHARDS):
            inner = pick(s * PART)
            narrow = narrow + dot(VG[sec, s], inner, NN)
            for who in range(2):
                held = VG[sec if who == 0 else 1 - sec, s]
                for h in range(2):
                    for k in range(2):
                        put = pick(s * 2 * PART + k * PART - h * H)
                        wide[who][h * 2 + k] = wide[who][h * 2 + k] + dot(held, put, NN)
        V640[...] = narrow
        for who, into in ((0, V1280), (1, VX)):
            for h in range(2):
                into[h, 0:3, :] = wide[who][h * 2][6:9] + wide[who][h * 2 + 1][9:12]

    def halo(ref, sends, recvs, m, reach, start):
        fwd = remote(ref.at[m, pl.ds(2 * LEN - reach, reach), :], ref.at[m, pl.ds(LEN - reach, reach), :], sends.at[m, 0], recvs.at[m, 0], ahead)
        bwd = remote(ref.at[m, pl.ds(LEN, reach), :], ref.at[m, pl.ds(2 * LEN, reach), :], sends.at[m, 1], recvs.at[m, 1], behind)

        @pl.when(seq < 3)
        def _():
            fwd.start() if start else fwd.wait_send()

        @pl.when(seq > 0)
        def _():
            bwd.start() if start else bwd.wait_send()

        if not start:

            @pl.when(seq > 0)
            def _():
                fwd.wait_recv()

            @pl.when(seq < 3)
            def _():
                bwd.wait_recv()

    def x_send(m, src):
        return remote(src.at[rows(0, m), :], XR.at[rows(0, m), :], x_s.at[m], x_r.at[m], at_x)

    def stage_a(m, reach):
        def tile(i):
            r = i * TILE
            at = rows(0, m, r, TILE)
            x = [POOL[rows(E_AT + h * ROWS, m, r, TILE), :].astype(f32) for h in range(2)]
            mean, inverse = row_stats(x, 2 * H)
            MU[at, :] = mean
            IV1[at, :] = inverse
            for h in range(2):
                v = (x[h] - mean) * inverse * V1280[h, 1:2, :] + V1280[h, 2:3, :]
                phi, slope = gelu_slope(v)
                A1[h, at, :] = (v * phi).astype(bf16)
                S1[h, at, :] = slope.astype(bf16)

        loop(LEN // TILE, tile)
        here = rows(0, m)
        TG[0:LEN, :] = dot(A1[0, here, :], W[0], NT) + dot(A1[1, here, :], W[1], NT)

        def tile2(i):
            r = i * TILE
            at = rows(0, m, r, TILE)
            x = TG[pl.ds(r, TILE), :] + V640[0:1, :]
            mean, inverse = row_stats([x], H)
            normed = (x - mean) * inverse
            v = normed * V640[2:3, :] + V640[3:4, :]
            phi, slope = gelu_slope(v)
            A2[m, pl.ds(pl.multiple_of(LEN + r, 16), TILE), :] = (v * phi).astype(bf16)
            S2[at, :] = slope.astype(bf16)
            N2[at, :] = normed.astype(bf16)
            IV2[at, :] = inverse

        loop(LEN // TILE, tile2)
        halo(A2, ha_s, ha_r, m, reach, True)

    def stage_b(m, span, relay):
        halo(A2, ha_s, ha_r, m, 2 * span, False)
        TG[0:LEN, :] = sum(dot(A2[m, pl.ds(LEN + (t - 2) * span, LEN), :], W[4 + t], NT) for t in (2, 0, 1, 3, 4))

        def tile(i):
            r = i * TILE
            at = rows(0, m, r, TILE)
            x = TG[pl.ds(r, TILE), :] + V640[1:2, :]
            mean, inverse = row_stats([x], H)
            normed = (x - mean) * inverse
            v = normed * V640[4:5, :] + V640[5:6, :]
            phi, slope = gelu_slope(v)
            A3[at, :] = (v * phi).astype(bf16)
            S3[at, :] = slope.astype(bf16)
            N3[at, :] = normed.astype(bf16)
            IV3[at, :] = inverse

        loop(LEN // TILE, tile)
        if relay:
            x_send(m, A3).start()
        here = rows(0, m)
        for h in range(2):
            mixed = dot(A3[here, :], W[2 + h], NN) + V1280[h, 0:1, :]
            POOL[rows(LV_AT + h * ROWS, m), :] = (POOL[rows(E_AT + h * ROWS, m), :].astype(f32) + mixed).astype(bf16)
            out_bo(m, h).start()

    def out_bo(m, h):
        return pltpu.make_async_copy(POOL.at[rows(LV_AT + h * ROWS, m), :], bo.at[m, :, pl.ds(h * H, H)], o_bo.at[m, h])

    def out_ig(m, h):
        return pltpu.make_async_copy(S1.at[h, rows(0, m), :], ig.at[m, :, pl.ds(h * H, H)], o_ig.at[m, h])

    def stage_x(m):
        x_send(m, A3).wait_recv()
        for h in range(2):
            at = rows(E_AT + h * ROWS, m)
            mixed = dot(XR[rows(0, m), :], WX[h], NN) + VX[h, 0:1, :]
            POOL[at, :] = (POOL[at, :].astype(f32) + mixed).astype(bf16)

    def stage_n(m):
        def tile(i):
            r = i * TILE
            at = rows(0, m, r, TILE)
            x = [POOL[rows(LV_AT + h * ROWS, m, r, TILE), :].astype(f32) for h in range(2)]
            mean, inverse = row_stats(x, 2 * H)
            MUX[at, :] = mean
            IVX[at, :] = inverse
            for h in range(2):
                v = (x[h] - mean) * inverse * VX[h, 1:2, :] + VX[h, 2:3, :]
                POOL[rows(SX_AT + h * ROWS, m, r, TILE), :] = gelu_slope(v)[1].astype(bf16)

        loop(LEN // TILE, tile)

    def stage_q(m):
        x_send(m, GH).wait_recv()
        for h in range(2):
            TG[h * LEN : (h + 1) * LEN, :] = dot(XR[rows(0, m), :], WX[h], NN)

        def tile(i):
            r = i * TILE
            at = rows(0, m, r, TILE)
            mean, inverse = MUX[at, :], IVX[at, :]
            ys, normeds = [], []
            for h in range(2):
                slope = POOL[rows(SX_AT + h * ROWS, m, r, TILE), :].astype(f32)
                ys.append(TG[pl.ds(h * LEN + r, TILE), :] * slope)
                normeds.append((POOL[rows(LV_AT + h * ROWS, m, r, TILE), :].astype(f32) - mean) * inverse)
            grads = norm_back(ys, normeds, inverse, [VX[h, 1:2, :] for h in range(2)], 2 * H)
            for h in range(2):
                U[h, at, :] = (U[h, at, :].astype(f32) + grads[h]).astype(bf16)

        loop(LEN // TILE, tile)

    def stage_p1(m, reach):
        here = rows(0, m)
        TG[0:LEN, :] = dot(U[0, here, :], W[2], NT) + dot(U[1, here, :], W[3], NT)

        def tile(i):
            r = i * TILE
            at = rows(0, m, r, TILE)
            y_ = TG[pl.ds(r, TILE), :] * S3[at, :].astype(f32)
            normed = N3[at, :].astype(f32)
            (grad,) = norm_back([y_], [normed], IV3[at, :], [V640[4:5, :]], H)
            low = grad.astype(bf16)
            GM[m, pl.ds(pl.multiple_of(LEN + r, 16), TILE), :] = low
            AC[4] += eights(y_ * normed)
            AC[5] += eights(y_)
            AC[1] += eights(low.astype(f32))
            for h in range(2):
                AC[6 + h] += eights(U[h, at, :].astype(f32))

        loop(LEN // TILE, tile)
        halo(GM, hg_s, hg_r, m, reach, True)

    def stage_p2(m, span, relay):
        halo(GM, hg_s, hg_r, m, 2 * span, False)
        TG[0:LEN, :] = sum(dot(GM[m, pl.ds(LEN - (t - 2) * span, LEN), :], W[4 + t], NN) for t in (2, 0, 1, 3, 4))

        def tile(i):
            r = i * TILE
            at = rows(0, m, r, TILE)
            y_ = TG[pl.ds(r, TILE), :] * S2[at, :].astype(f32)
            normed = N2[at, :].astype(f32)
            (grad,) = norm_back([y_], [normed], IV2[at, :], [V640[2:3, :]], H)
            low = grad.astype(bf16)
            GH[at, :] = low
            AC[2] += eights(y_ * normed)
            AC[3] += eights(y_)
            AC[0] += eights(low.astype(f32))

        loop(LEN // TILE, tile)
        if relay:
            x_send(m, GH).start()

    def stage_p3(m):
        for h in range(2):
            TG[h * LEN : (h + 1) * LEN, :] = dot(GH[rows(0, m), :], W[h], NN)

        def tile(i):
            r = i * TILE
            at = rows(0, m, r, TILE)
            mean, inverse = MU[at, :], IV1[at, :]
            ys, normeds = [], []
            for h in range(2):
                ys.append(TG[pl.ds(h * LEN + r, TILE), :] * S1[h, at, :].astype(f32))
                normeds.append((POOL[rows(E_AT + h * ROWS, m, r, TILE), :].astype(f32) - mean) * inverse)
            grads = norm_back(ys, normeds, inverse, [V1280[h, 1:2, :] for h in range(2)], 2 * H)
            for h in range(2):
                S1[h, at, :] = (U[h, at, :].astype(f32) + grads[h]).astype(bf16)
                AC[8 + h] += eights(ys[h] * normeds[h])
                AC[10 + h] += eights(ys[h])

        loop(LEN // TILE, tile)
        for h in range(2):
            out_ig(m, h).start()

    AC[...] = jnp.zeros_like(AC)
    for ref in (A2, GM):

        @pl.when(seq == 0)
        def _():
            for m in range(MICRO):
                ref[m, 0:LEN, :] = jnp.zeros((LEN, H), bf16)

        @pl.when(seq == 3)
        def _():
            for m in range(MICRO):
                ref[m, 2 * LEN : 3 * LEN, :] = jnp.zeros((LEN, H), bf16)

    for m in range(MICRO):
        MK[m] = jnp.transpose(jnp.broadcast_to(mask[m : m + 1, :].astype(f32), (128, LEN)))
    for m in range(MICRO):
        for h in range(2):
            load_in(m, h, xin, POOL.at[pl.ds(E_AT + h * ROWS + m * LEN, LEN), :]).wait()
            load_in(m, h, cot, U.at[h, pl.ds(m * LEN, LEN), :]).wait()

    def masked(i):
        keep = MK[i // (LEN // TILE), pl.ds(pl.multiple_of(lax.rem(i, LEN // TILE) * TILE, TILE), TILE), :][:, 0:1]
        at = pl.ds(pl.multiple_of(i * TILE, TILE), TILE)
        for h in range(2):
            U[h, at, :] = (U[h, at, :].astype(f32) * keep).astype(bf16)

    loop(ROWS // TILE, masked)
    own_w.wait()
    if fused:
        gather()
        vectors()
    else:
        own_v.wait()
        for src, dst in ((v640_in, V640), (v1280_in, V1280), (vx_in, VX)):
            dst[...] = src[...]

    @pl.when(first)
    def _():
        span = DILATION_BASE

        def forward(k):
            @pl.when(k < MICRO)
            def _():
                stage_a(k, 2 * span)

            @pl.when(k > 0)
            def _():
                stage_b(k - 1, span, True)

        loop(MICRO + 1, forward)
        if fused:
            gxc(1 - core).wait_recv()
        loop(MICRO, stage_n)

        def backward(m):
            stage_q(m)
            stage_p1(m, 2 * span)
            stage_p2(m, span, False)
            stage_p3(m)

        loop(MICRO, backward)
        loop(MICRO, lambda m: x_send(m, A3).wait_send())

    @pl.when(jnp.logical_not(first))
    def _():
        span = 2 * DILATION_BASE
        if fused:
            gxc(1 - core).wait_recv()

        def both(k):
            @pl.when(k >= 2)
            def _():
                stage_p2(k - 2, span, True)
                stage_p3(k - 2)

            @pl.when(k < MICRO)
            def _():
                stage_x(k)
                stage_a(k, 2 * span)

            @pl.when(jnp.logical_and(k >= 1, k <= MICRO))
            def _():
                stage_b(k - 1, span, False)
                stage_p1(k - 1, 2 * span)

        loop(MICRO + 2, both)
        loop(MICRO, lambda m: x_send(m, GH).wait_send())

    def out_wait(m):
        for h in range(2):
            out_bo(m, h).wait()
            out_ig(m, h).wait()

    loop(MICRO, out_wait)
    for i in range(12):
        VS[0, i : i + 1, :] = jnp.sum(AC[i], axis=0, keepdims=True)
    VS[0, 12:16, :] = jnp.zeros((4, H), f32)

    def gradient(b, span):
        if b < 2:
            TG[...] = dot(GH[...], A1[b], TN)
        elif b < 4:
            TG[...] = dot(A3[...], U[b - 2], TN)
        else:
            at = pl.ds(pl.multiple_of(LEN + (b - 6) * span, 64), LEN)
            for m in range(MICRO):
                term = dot(GM[m, LEN : 2 * LEN, :], A2[m, at, :], TN)
                if m == 0:
                    TG[...] = term
                else:
                    TG[...] += term

    span = DILATION_BASE * (1 + sec)

    if not fused:
        for b in range(BLOCKS):
            gradient(b, span)
            out = pltpu.make_async_copy(TG, gout.at[b], o_g.at[b])
            out.start()
            out.wait()
        vout[...] = VS[0]
        return

    def keep_at(p, s):
        return pl.ds(pl.multiple_of(KEEP_AT + (p * SHARDS + s) * HALF, 16), HALF)

    def give_at(p):
        return pl.ds(GIVE_AT + p * SHARDS * HALF, SHARDS * HALF)

    kind = lambda p: p % 3
    slot = lambda p: p // 3
    zslot = lambda p: slot(p) + (3 if kind(p) == 2 else 0)
    owner = lambda p: y == kind(p) if kind(p) < 2 else y >= 0

    def rc(p):
        return remote(POOL.at[give_at(p), :], CR.at[p], rc_s.at[p], rc_r.at[p], at_core)

    def ry(p, s):
        return remote(POOL.at[keep_at(p, s), :], YR.at[slot(p), s], ry_s.at[slot(p), s], ry_r.at[slot(p), s], at_y)

    def rz(p, s, upward):
        way, idx = (0, s - 1) if upward else (1, s)
        place = (zslot(p), way, idx)
        return remote(POOL.at[keep_at(p, s), :], ZR.at[place], rz_s.at[place], rz_r.at[place], up if upward else down)

    def half_of(half):
        return pl.ds(pl.multiple_of(half * HALF, 16), HALF)

    def fy(p):
        if kind(p) == 2:
            return remote(POOL.at[keep_at(p, ten), :], YX.at[slot(p)], fy_s.at[p], fy_r.at[p], at_y)
        spot = F.at[p, half_of(core), :]
        return remote(spot, spot, fy_s.at[p], fy_r.at[p], at_y)

    def fc(p, half):
        spot = F.at[p, half_of(half), :]
        return remote(spot, spot, fc_s.at[p], fc_r.at[p], at_core)

    def out_g(p):
        return pltpu.make_async_copy(F.at[p], gout.at[ORDER[p]], o_g.at[p])

    def add(at, *others_):
        total = POOL[at, :].astype(f32)
        for other in others_:
            total = total + other.astype(f32)
        return total

    def compute(p):
        gradient(ORDER[p], span)
        for s in range(SHARDS):
            theirs = TG[pl.ds(pl.multiple_of(s * PART + (1 - core) * HALF, 16), HALF), :]
            POOL[pl.ds(GIVE_AT + (p * SHARDS + s) * HALF, HALF), :] = theirs.astype(bf16)
        rc(p).start()
        for s in range(SHARDS):
            POOL[keep_at(p, s), :] = TG[pl.ds(pl.multiple_of(s * PART + core * HALF, 16), HALF), :].astype(bf16)

    def over_core(p):
        rc(p).wait_recv()
        for s in (0, 3, 1, 2):
            POOL[keep_at(p, s), :] = add(keep_at(p, s), CR[p, s * HALF : (s + 1) * HALF, :]).astype(bf16)
            if kind(p) < 2:

                @pl.when(jnp.logical_not(owner(p)))
                def _():
                    ry(p, s).start()

    def over_y(p):
        @pl.when(owner(p))
        def _():
            for s in (0, 3, 1, 2):
                ry(p, s).wait_recv()
                POOL[keep_at(p, s), :] = add(keep_at(p, s), YR[slot(p), s]).astype(bf16)

    def through(p, z, s, upward):
        @pl.when(jnp.logical_and(owner(p), ten == z))
        def _():
            if 0 < z < SHARDS - 1:
                rz(p, s, upward).wait_recv()
                came = ZR[zslot(p), 0, s - 1] if upward else ZR[zslot(p), 1, s]
                POOL[keep_at(p, s), :] = add(keep_at(p, s), came).astype(bf16)
            rz(p, s, upward).start()

    def chain_one(p):
        for s in (3, 2, 1):
            through(p, 0, s, True)
        for s in (0, 1, 2):
            through(p, 3, s, False)

    def chain_two(p):
        for s in (3, 2):
            through(p, 1, s, True)
        for s in (0, 1):
            through(p, 2, s, False)

    def chain_three(p):
        through(p, 2, 3, True)
        through(p, 1, 0, False)

    def chain_end(p):
        for z in range(SHARDS):

            @pl.when(jnp.logical_and(owner(p), ten == z))
            def _():
                came = []
                if z > 0:
                    rz(p, z, True).wait_recv()
                    came.append(ZR[zslot(p), 0, z - 1])
                if z < SHARDS - 1:
                    rz(p, z, False).wait_recv()
                    came.append(ZR[zslot(p), 1, z])
                total = add(keep_at(p, z), *came).astype(bf16)
                if kind(p) == 2:
                    POOL[keep_at(p, z), :] = total
                else:
                    F[p, half_of(core), :] = total

        if kind(p) == 2:
            fy(p).start()
        else:

            @pl.when(owner(p))
            def _():
                fy(p).start()
                fc(p, core).start()

    def settle(p):
        if kind(p) == 2:
            fy(p).wait_recv()
            F[p, half_of(core), :] = add(keep_at(p, ten), YX[slot(p)]).astype(bf16)
            fc(p, core).start()
        else:

            @pl.when(jnp.logical_not(owner(p)))
            def _():
                fy(p).wait_recv()
                fc(p, core).start()

    def finish(p):
        fc(p, 1 - core).wait_recv()
        out_g(p).start()

    def vector_round(i):
        where = [at_core, at_y, (sec, seq, ten + 1 - 2 * lax.rem(ten, 2)), (sec, seq, lax.rem(ten + 2, SHARDS))][i]
        return remote(VS.at[i], VR.at[i], vr_s.at[i], vr_r.at[i], where)

    stages = [(compute, 0, 0), (over_core, 1, 1), (over_y, 3, 9), (chain_one, 3, 2), (chain_two, 4, 3), (chain_three, 5, 4), (chain_end, 6, 5), (settle, 8, 7), (finish, 9, 8)]
    for t in range(BLOCKS + 10):
        if t % 2 == 1 and t < 11:
            i = t // 2
            if i > 0:
                vector_round(i - 1).wait()
                VS[i] = VS[i - 1] + VR[i - 1]
            if i < 4:
                vector_round(i).start()
        for stage, lag_y, lag_z in stages:
            for p in range(BLOCKS):
                if stage is over_y and kind(p) == 2:
                    continue
                if t - p == (lag_z if kind(p) == 2 else lag_y):
                    stage(p)

    vout[...] = VS[4]

    for i in range(BLOCKS):
        out_g(i).wait()
        rc(i).wait_send()
        fc(i, core).wait_send()
        if kind(i) == 2:
            fy(i).wait_send()
        else:

            @pl.when(owner(i))
            def _():
                fy(i).wait_send()

            @pl.when(jnp.logical_not(owner(i)))
            def _():
                for s in range(SHARDS):
                    ry(i, s).wait_send()

        for s in range(SHARDS):

            @pl.when(jnp.logical_and(owner(i), s > ten))
            def _():
                rz(i, s, True).wait_send()

            @pl.when(jnp.logical_and(owner(i), s < ten))
            def _():
                rz(i, s, False).wait_send()

    gx().wait_send()
    gxc(core).wait_send()


def relay(block_input, cotangent, mask, weights, vectors, fused):
    hbm = pl.BlockSpec(memory_space=pl.ANY)
    vmem = pl.BlockSpec(memory_space=pltpu.VMEM)
    dma = lambda *shape: pltpu.SemaphoreType.DMA(shape)
    low = lambda *shape: pltpu.VMEM(shape, bf16)
    full = lambda *shape: pltpu.VMEM(shape, f32)
    scratch = [
        low(BLOCKS, H, H),
        low(2, H, H),
        low(POOL_ROWS, H),
        low(2, ROWS, H),
        low(2, ROWS, H),
        low(MICRO, 3 * LEN, H),
        low(ROWS, H),
        low(ROWS, H),
        low(ROWS, H),
        low(ROWS, H),
        low(ROWS, H),
        low(2, ROWS, H),
        low(MICRO, 3 * LEN, H),
        low(ROWS, H),
        low(ROWS, H),
        full(ROWS, 1),
        full(ROWS, 1),
        full(ROWS, 1),
        full(ROWS, 1),
        full(ROWS, 1),
        full(ROWS, 1),
        full(MICRO, LEN, 128),
        full(H, H),
        full(16, H),
        full(2, 8, H),
        full(2, 8, H),
        full(12, 8, H),
        full(5, 16, H),
        dma(MICRO, 2, 2),
        dma(2),
        dma(MICRO, 2),
        dma(MICRO, 2),
        dma(MICRO),
        dma(MICRO),
        dma(MICRO, 2),
        dma(MICRO, 2),
        dma(MICRO, 2),
        dma(MICRO, 2),
    ]
    if fused:
        scratch += [
            low(2, SHARDS, 16, 256),
            low(BLOCKS, SHARDS * HALF, H),
            low(3, SHARDS, HALF, H),
            low(6, 2, 3, HALF, H),
            low(3, HALF, H),
            low(BLOCKS, PART, H),
            full(4, 16, H),
            dma(7),
            dma(7),
            dma(BLOCKS, SHARDS, 2),
            dma(BLOCKS, SHARDS),
            dma(BLOCKS, SHARDS),
            dma(BLOCKS, SHARDS),
            dma(BLOCKS, SHARDS),
            dma(BLOCKS, SHARDS),
            dma(1),
            dma(1),
            dma(1),
            dma(1),
            dma(BLOCKS),
            dma(BLOCKS),
            dma(3, SHARDS),
            dma(3, SHARDS),
            dma(6, 2, 3),
            dma(6, 2, 3),
            dma(BLOCKS),
            dma(BLOCKS),
            dma(BLOCKS),
            dma(BLOCKS),
            dma(4),
            dma(4),
        ]
    scratch += [dma(BLOCKS)]
    outs = (
        jax.ShapeDtypeStruct((MICRO, LEN, 2 * H), bf16),
        jax.ShapeDtypeStruct((MICRO, LEN, 2 * H), bf16),
        jax.ShapeDtypeStruct((BLOCKS, PART, H), bf16) if fused else jax.ShapeDtypeStruct((BLOCKS, H, H), f32),
        jax.ShapeDtypeStruct((16, H), f32),
    )
    in_specs = [hbm, hbm, vmem] + [hbm] * len(weights) + ([hbm] if fused else [vmem] * 3)
    return pl.pallas_call(
        functools.partial(relay_kernel, fused),
        out_shape=outs,
        in_specs=in_specs,
        out_specs=(hbm, hbm, hbm, vmem),
        scratch_shapes=scratch,
        compiler_params=pltpu.CompilerParams(collective_id=0, has_side_effects=True, vmem_limit_bytes=60 * 2**20),
        cost_estimate=pl.CostEstimate(flops=25_000_000_000, bytes_accessed=20_000_000, transcendentals=4_000_000),
        name="relay",
    )(block_input, cotangent, mask, *weights, *vectors)


def packed_weights(conv_in, conv_mid, conv_out):
    channels = conv_out.shape[0]
    halves = lambda m: m.reshape(channels, 2, H).transpose(1, 0, 2)
    return jnp.concatenate([halves(conv_in.T), halves(conv_out), conv_mid.transpose(0, 2, 1)])


def local(*args):
    block_input, cotangent, mask = args[:3]
    (conv_in, bias_in, conv_mid, bias_mid, conv_out, bias_out, gain_first, shift_first, gain_second, shift_second, gain_third, shift_third) = (a[0] for a in args[3:])
    ten, sec = lax.axis_index("tensor"), lax.axis_index("section")
    shards = lax.axis_size("tensor")
    fused = shards == SHARDS
    channels = conv_out.shape[0]
    xin = block_input.reshape(MICRO, LEN, 2 * H)
    cot = cotangent.reshape(MICRO, LEN, 2 * H)
    mask = mask.reshape(MICRO, LEN)
    mine = packed_weights(conv_in, conv_mid, conv_out)
    narrow = (bias_in, bias_mid, gain_second, shift_second, gain_third, shift_third)
    wide = (bias_out, gain_first, shift_first)
    if fused:
        lines = jnp.stack(list(narrow) + [w[:PART] for w in wide] + [w[PART:] for w in wide])
        vsh = jnp.pad(lines, ((0, 4), (0, 256 - PART)))
        block_out, input_grad, grads, small = relay(xin, cot, mask, (mine,), (vsh,), True)
        grads = grads.astype(f32)
    else:
        whole = lax.all_gather(mine, "tensor", axis=1, tiled=True)
        swap = [(0, 1), (1, 0)]
        give = jnp.where(sec == 0, whole[2:4], whole[0:2])
        other = lax.ppermute(give, "section", swap)
        v_narrow = lax.all_gather(jnp.stack(narrow), "tensor", axis=1, tiled=True)
        v_wide = lax.all_gather(jnp.stack(wide), "tensor", axis=1, tiled=True)
        v640 = jnp.pad(v_narrow.astype(f32), ((0, 10), (0, 0)))
        v1280 = jnp.pad(v_wide.astype(f32).reshape(3, 2, H).transpose(1, 0, 2), ((0, 0), (0, 5), (0, 0)))
        vx = lax.ppermute(v1280, "section", swap)
        block_out, input_grad, grads, small = relay(xin, cot, mask, (whole, other), (v640, v1280, vx), False)
        grads = lax.psum(lax.psum_scatter(grads, "tensor", scatter_dimension=1, tiled=True), "seq")
        small = lax.psum(small, ("seq", "tensor"))
    grad_in = grads[0:2].transpose(0, 2, 1).reshape(2 * H, channels)
    grad_out = grads[2:4].transpose(1, 0, 2).reshape(channels, 2 * H)
    grad_mid = grads[4:9].transpose(0, 2, 1)
    thin = lax.dynamic_slice_in_dim(small[0:6], ten * channels, channels, 1)
    thick = lax.dynamic_slice_in_dim(small[6:12].reshape(3, 2 * H), ten * 2 * channels, 2 * channels, 1)
    shape = (1, MICRO, 1, LEN, 2 * H)
    return (
        block_out.reshape(shape),
        input_grad.reshape(shape),
        grad_in[None],
        thin[0:1],
        grad_mid[None],
        thin[1:2],
        grad_out[None],
        thick[0:1],
        thick[1:2],
        thick[2:3],
        thin[2:3],
        thin[3:4],
        thin[4:5],
        thin[5:6],
    )


def solution(mesh):
    in_specs = (
        P(None, "tensor", "seq", None),
        P(None, "tensor", "seq", None),
        P(None, "tensor", "seq"),
        P("section", None, "tensor"),
        P("section", "tensor"),
        P("section", None, None, "tensor"),
        P("section", "tensor"),
        P("section", "tensor", None),
        P("section", "tensor"),
        P("section", "tensor"),
        P("section", "tensor"),
        P("section", "tensor"),
        P("section", "tensor"),
        P("section", "tensor"),
        P("section", "tensor"),
    )
    out_specs = (
        P("section", None, "tensor", "seq", None),
        P("section", None, "tensor", "seq", None),
        P("section", None, "tensor"),
        P("section", "tensor"),
        P("section", None, None, "tensor"),
        P("section", "tensor"),
        P("section", "tensor", None),
        P("section", "tensor"),
        P("section", "tensor"),
        P("section", "tensor"),
        P("section", "tensor"),
        P("section", "tensor"),
        P("section", "tensor"),
        P("section", "tensor"),
    )
    return jax.shard_map(local, mesh=mesh, in_specs=in_specs, out_specs=out_specs, check_vma=False)
```

```python
import functools

import jax
import jax.numpy as jnp
from jax import lax
from jax.experimental import pallas as pl
from jax.experimental.pallas import tpu as pltpu
from jax.sharding import PartitionSpec as P

DILATION_BASE = 64
EPS = 1e-05
ROOT_HALF = 0.7071067811865476
INVERSE_ROOT_TWO_PI = 0.3989422804014327
MESH = pl.DeviceIdType.MESH
f32 = jnp.float32
bf16 = jnp.bfloat16

MICRO = 4
LEN = 256
H = 640
ROWS = MICRO * LEN
SHARDS = 4
PART = H // SHARDS
HALF = PART // 2
BLOCKS = 9
TILE = 256
WIDE = 128
X_STEP = 10
A_STEP = 8
LEAD = 3
NN = (((1,), (0,)), ((), ()))
NT = (((1,), (1,)), ((), ()))
TN = (((0,), (0,)), ((), ()))

E_AT, SX_AT, LV_AT, POOL_ROWS = 0, 2 * ROWS, 4 * ROWS, 6 * ROWS
KEEP_SLOTS, GIVE_SLOTS = 3, 3
SCHEDULE = (
    ("compute", 0, None),
    ("core", 1, None),
    ("y", 3, False),
    ("one", 3, False),
    ("one", 1, True),
    ("two", 5, False),
    ("two", 3, True),
    ("end", 8, False),
    ("end", 5, True),
    ("settle", 11, False),
    ("settle", 8, True),
    ("finish", 13, None),
)
LAST_LAG = 13


def dot(a, b, dims):
    return lax.dot_general(a, b, dims, preferred_element_type=f32)


def loop(count, body):
    def step(i, carry):
        body(i)
        return carry

    lax.fori_loop(0, count, step, 0)


def unroll(count, body):
    for i in range(count):
        body(i)


def row_stats(parts, width):
    mean = sum(jnp.sum(x, axis=-1, keepdims=True) for x in parts) / width
    spread = sum(jnp.sum(x * x, axis=-1, keepdims=True) for x in parts) / width - mean * mean
    return mean, lax.rsqrt(spread + EPS)


def gelu_slope(v):
    phi = 0.5 * (1.0 + lax.erf(v * ROOT_HALF))
    return phi, phi + v * (jnp.exp(-0.5 * v * v) * INVERSE_ROOT_TWO_PI)


def norm_back(ys, normeds, inverse, gains, width):
    scaled = [y * g for y, g in zip(ys, gains)]
    total = sum(jnp.sum(s, axis=-1, keepdims=True) for s in scaled) / width
    along = sum(jnp.sum(s * n, axis=-1, keepdims=True) for s, n in zip(scaled, normeds)) / width
    return [inverse * (s - total - n * along) for s, n in zip(scaled, normeds)]


def eights(x):
    return jnp.sum(x.reshape(x.shape[0] // 8, 8, x.shape[1]), axis=0)


def relay_kernel(fused, *refs):
    if fused:
        (xin, cot, mask, wsh, vsh, bo, ig, gout, vout) = refs[:9]
        rest = refs[9:]
    else:
        (xin, cot, mask, wfull, wother, v640_in, v1280_in, vx_in, bo, ig, gout, vout) = refs[:12]
        rest = refs[12:]
    (W, WX, POOL, A1, S1, A2, S2, N2, A3, S3, N3, U, GM, GH, XR, ST, TG, V640, V1280, VX, AC, VS) = rest[:22]
    (l_in, l_w, o_bo, o_ig, x_s, x_r, ha_s, ha_r, hg_s, hg_r) = rest[22:32]
    if fused:
        (VG, CR, KEEP, GIVE, YR, ZR, YX, VR, vg_s, vg_r, gz_s, gz_r, gy_s, gy_r, gc_s, gc_r, wx_s, wx_r, wc_s, wc_r, rc_s, rc_r, ry_s, ry_r, rz_s, rz_r, fy_s, fy_r, fc_s, fc_r, vr_s, vr_r, o_g) = rest[32:]
    else:
        (o_g,) = rest[32:]

    sec = lax.axis_index("section")
    seq = lax.axis_index("seq")
    ten = lax.axis_index("tensor")
    y = seq // 2
    core = lax.rem(seq, 2)
    at_core = (sec, y * 2 + (1 - core), ten)
    at_y = (sec, (1 - y) * 2 + core, ten)
    at_diag = (sec, (1 - y) * 2 + (1 - core), ten)
    at_x = (1 - sec, seq, ten)
    up, down = (sec, seq, ten + 1), (sec, seq, ten - 1)
    behind, ahead = (sec, seq - 1, ten), (sec, seq + 1, ten)
    first = sec == 0

    def remote(src, dst, send, recv, where):
        return pltpu.make_async_remote_copy(src_ref=src, dst_ref=dst, send_sem=send, recv_sem=recv, device_id=where, device_id_type=MESH)

    def rows(base, m, r=0, n=LEN):
        return pl.ds(pl.multiple_of(base + m * LEN + r, 16), n)

    def load_in(m, h, ref, into):
        return pltpu.make_async_copy(ref.at[m, :, pl.ds(h * H, H)], into, l_in.at[m, h, 0 if ref is xin else 1])

    for m in range(MICRO):
        for h in range(2):
            load_in(m, h, xin, POOL.at[pl.ds(E_AT + h * ROWS + m * LEN, LEN), :]).start()
            load_in(m, h, cot, U.at[h, pl.ds(m * LEN, LEN), :]).start()
    if fused:
        own_w = pltpu.make_async_copy(wsh, W.at[:, pl.ds(pl.multiple_of(ten * PART, 16), PART), :], l_w.at[0])
        own_v = pltpu.make_async_copy(vsh, VG.at[sec, ten], l_w.at[1])
        own_w.start()
        own_v.start()
        partners = [at_core, at_y, at_diag]
        others = [(s, d) for s in range(2) for d in range(SHARDS) if s or d]
        partners += [(lax.rem(sec + s, 2), seq, lax.rem(ten + d, SHARDS)) for s, d in others]
    else:
        own_w = pltpu.make_async_copy(wfull, W, l_w.at[0])
        own_v = pltpu.make_async_copy(wother, WX, l_w.at[1])
        own_w.start()
        own_v.start()
        partners = [at_core, at_diag, at_x]

    barrier = pltpu.get_barrier_semaphore()
    for partner in partners:
        pl.semaphore_signal(barrier, inc=1, device_id=partner, device_id_type=MESH)
    pl.semaphore_wait(barrier, len(partners))

    def piece(ref, b, s, half):
        return ref.at[b, pl.ds(pl.multiple_of(s * PART + half * HALF, 16), HALF), :]

    def gz(b, s, to_up, src=None):
        spot = piece(W, b, s, core)
        return remote(spot if src is None else src, spot, gz_s.at[b, s, 0 if to_up else 1], gz_r.at[b, s], up if to_up else down)

    def gy(b, s):
        spot = piece(W, b, s, core)
        return remote(spot, spot, gy_s.at[b, s], gy_r.at[b, s], at_y)

    def gc(b, s, half):
        spot = piece(W, b, s, half)
        return remote(spot, spot, gc_s.at[b, s], gc_r.at[b, s], at_core)

    def wanted(b):
        return b // 2 == sec

    def gx(b, s, src=None):
        k = lax.rem(b, 2)
        return remote(piece(W, b, s, core) if src is None else src, piece(WX, k, s, core), wx_s.at[k, s], wx_r.at[k, s], at_x)

    def gxc(k, s, half):
        spot = piece(WX, k, s, half)
        return remote(spot, spot, wc_s.at[k, s], wc_r.at[k, s], at_core)

    mine = lambda b: jnp.logical_or(b == BLOCKS - 1, lax.rem(b, 2) == y)
    def send_own(b):
        src = wsh.at[b, pl.ds(pl.multiple_of(core * HALF, 16), HALF), :]

        @pl.when(jnp.logical_and(mine(b), ten < SHARDS - 1))
        def _():
            gz(b, ten, True, src).start()

        @pl.when(jnp.logical_and(mine(b), ten > 0))
        def _():
            gz(b, ten, False, src).start()

        @pl.when(wanted(b))
        def _():
            gx(b, ten, src).start()

    def gather_begin():
        for i, (s, d) in enumerate(others):
            remote(vsh, VG.at[sec, ten], vg_s.at[i], vg_r.at[i], (lax.rem(sec + s, 2), seq, lax.rem(ten + d, SHARDS))).start()
        for b in range(LEAD):
            send_own(b)

    def gather_step(k):
        @pl.when(k + LEAD < BLOCKS)
        def _():
            send_own(k + LEAD)

        for d in range(1, SHARDS):
            b = k - (d - 1)
            ok = jnp.logical_and(b >= 0, b < BLOCKS)
            for above in (False, True):
                s = ten + d if above else ten - d
                there = jnp.logical_and(ok, s < SHARDS if above else s >= 0)
                onward = (ten > 0) if above else (ten < SHARDS - 1)

                @pl.when(jnp.logical_and(there, mine(b)))
                def _():
                    gz(b, s, True).wait_recv()

                    @pl.when(onward)
                    def _():
                        gz(b, s, not above).start()

                    @pl.when(b < BLOCKS - 1)
                    def _():
                        gy(b, s).start()

                    gc(b, s, core).start()

                    @pl.when(wanted(b))
                    def _():
                        gx(b, s).start()

        for d in range(1, SHARDS):
            b = k - d
            ok = jnp.logical_and(b >= 0, b < BLOCKS)
            for above in (False, True):
                s = ten + d if above else ten - d
                there = jnp.logical_and(ok, s < SHARDS if above else s >= 0)

                @pl.when(jnp.logical_and(there, jnp.logical_not(mine(b))))
                def _():
                    gy(b, s).wait_recv()
                    gc(b, s, core).start()

                    @pl.when(wanted(b))
                    def _():
                        gx(b, s).start()

        b = k - 4
        for s in range(SHARDS):

            @pl.when(jnp.logical_and(jnp.logical_and(b >= 0, b < BLOCKS), s != ten))
            def _():
                gc(b, s, 1 - core).wait_recv()

        @pl.when(jnp.logical_and(k >= X_STEP, k < X_STEP + 2))
        def _():
            for s in range(SHARDS):
                gx(k - X_STEP, s).wait_recv()
                gxc(k - X_STEP, s, core).start()

    def others_blocks():
        for k in range(2):
            for s in range(SHARDS):
                gxc(k, s, 1 - core).wait_recv()

    def gather_drain(b):
        @pl.when(b < 2)
        def _():
            for s in range(SHARDS):
                gx(b, s).wait_send()
                gxc(b, s, core).wait_send()

        for s in range(SHARDS):
            fromabove = s > ten

            @pl.when(jnp.logical_and(mine(b), jnp.logical_and(s <= ten, ten < SHARDS - 1)))
            def _():
                gz(b, s, True).wait_send()

            @pl.when(jnp.logical_and(mine(b), jnp.logical_and(s >= ten, ten > 0)))
            def _():
                gz(b, s, False).wait_send()

            @pl.when(s != ten)
            def _():
                gc(b, s, core).wait_send()

                @pl.when(jnp.logical_and(mine(b), b < BLOCKS - 1))
                def _():
                    gy(b, s).wait_send()

    def vectors():
        own_v.wait()
        for i, (s, d) in enumerate(others):
            remote(vsh, VG.at[sec, ten], vg_s.at[i], vg_r.at[i], at_x).wait()
        line = lax.broadcasted_iota(jnp.int32, (2 * 128, H), 0)
        col = lax.broadcasted_iota(jnp.int32, (2 * 128, H), 1)

        def pick(offset):
            return jnp.where(col == line + offset, 1.0, 0.0).astype(bf16)

        narrow = jnp.zeros((16, H), f32)
        wide = [[jnp.zeros((16, H), f32) for _ in range(4)] for _ in range(2)]
        for s in range(SHARDS):
            inner = pick(s * PART)
            narrow = narrow + dot(VG[sec, s], inner, NN)
            for who in range(2):
                held = VG[sec if who == 0 else 1 - sec, s]
                for h in range(2):
                    for k in range(2):
                        put = pick(s * 2 * PART + k * PART - h * H)
                        wide[who][h * 2 + k] = wide[who][h * 2 + k] + dot(held, put, NN)
        V640[...] = narrow
        for who, into in ((0, V1280), (1, VX)):
            for h in range(2):
                into[h, 0:3, :] = wide[who][h * 2][6:9] + wide[who][h * 2 + 1][9:12]

    def halo(ref, sends, recvs, m, reach, start):
        fwd = remote(ref.at[m, pl.ds(2 * LEN - reach, reach), :], ref.at[m, pl.ds(LEN - reach, reach), :], sends.at[m, 0], recvs.at[m, 0], ahead)
        bwd = remote(ref.at[m, pl.ds(LEN, reach), :], ref.at[m, pl.ds(2 * LEN, reach), :], sends.at[m, 1], recvs.at[m, 1], behind)

        @pl.when(seq < 3)
        def _():
            fwd.start() if start else fwd.wait_send()

        @pl.when(seq > 0)
        def _():
            bwd.start() if start else bwd.wait_send()

        if not start:

            @pl.when(seq > 0)
            def _():
                fwd.wait_recv()

            @pl.when(seq < 3)
            def _():
                bwd.wait_recv()

    def x_send(m, src):
        return remote(src.at[rows(0, m), :], XR.at[rows(0, m), :], x_s.at[m], x_r.at[m], at_x)

    def stage_first(m):
        def tile(i):
            r = i * WIDE
            at = rows(0, m, r, WIDE)
            x = [POOL[rows(E_AT + h * ROWS, m, r, WIDE), :].astype(f32) for h in range(2)]
            mean, inverse = row_stats(x, 2 * H)
            ST[at, 0:1] = mean
            ST[at, 1:2] = inverse
            for h in range(2):
                v = (x[h] - mean) * inverse * V1280[h, 1:2, :] + V1280[h, 2:3, :]
                phi, slope = gelu_slope(v)
                A1[h, at, :] = (v * phi).astype(bf16)
                S1[h, at, :] = slope.astype(bf16)

        unroll(LEN // WIDE, tile)

    def stage_a(m, reach):
        here = rows(0, m)
        TG[0:LEN, :] = dot(A1[0, here, :], W[2], NT) + dot(A1[1, here, :], W[3], NT)

        def tile2(i):
            r = i * TILE
            at = rows(0, m, r, TILE)
            x = TG[pl.ds(r, TILE), :] + V640[0:1, :]
            mean, inverse = row_stats([x], H)
            normed = (x - mean) * inverse
            v = normed * V640[2:3, :] + V640[3:4, :]
            phi, slope = gelu_slope(v)
            A2[m, pl.ds(pl.multiple_of(LEN + r, 16), TILE), :] = (v * phi).astype(bf16)
            S2[at, :] = slope.astype(bf16)
            N2[at, :] = normed.astype(bf16)
            ST[at, 2:3] = inverse

        unroll(LEN // TILE, tile2)
        halo(A2, ha_s, ha_r, m, reach, True)

    def stage_b(m, span, relay):
        halo(A2, ha_s, ha_r, m, 2 * span, False)
        TG[0:LEN, :] = sum(dot(A2[m, pl.ds(LEN + (t - 2) * span, LEN), :], W[4 + t], NT) for t in (2, 0, 1, 3, 4))

        def tile(i):
            r = i * TILE
            at = rows(0, m, r, TILE)
            x = TG[pl.ds(r, TILE), :] + V640[1:2, :]
            mean, inverse = row_stats([x], H)
            normed = (x - mean) * inverse
            v = normed * V640[4:5, :] + V640[5:6, :]
            phi, slope = gelu_slope(v)
            A3[at, :] = (v * phi).astype(bf16)
            S3[at, :] = slope.astype(bf16)
            N3[at, :] = normed.astype(bf16)
            ST[at, 3:4] = inverse

        unroll(LEN // TILE, tile)
        if relay:
            x_send(m, A3).start()
        here = rows(0, m)
        for h in range(2):
            mixed = dot(A3[here, :], W[h], NN) + V1280[h, 0:1, :]
            POOL[rows(LV_AT + h * ROWS, m), :] = (POOL[rows(E_AT + h * ROWS, m), :].astype(f32) + mixed).astype(bf16)
            out_bo(m, h).start()

    def out_bo(m, h):
        return pltpu.make_async_copy(POOL.at[rows(LV_AT + h * ROWS, m), :], bo.at[m, :, pl.ds(h * H, H)], o_bo.at[m, h])

    def out_ig(m, h):
        return pltpu.make_async_copy(S1.at[h, rows(0, m), :], ig.at[m, :, pl.ds(h * H, H)], o_ig.at[m, h])

    def stage_x(m):
        x_send(m, A3).wait_recv()
        for h in range(2):
            at = rows(E_AT + h * ROWS, m)
            mixed = dot(XR[rows(0, m), :], WX[h], NN) + VX[h, 0:1, :]
            POOL[at, :] = (POOL[at, :].astype(f32) + mixed).astype(bf16)

    def stage_n(m):
        def tile(i):
            r = i * WIDE
            at = rows(0, m, r, WIDE)
            x = [POOL[rows(LV_AT + h * ROWS, m, r, WIDE), :].astype(f32) for h in range(2)]
            mean, inverse = row_stats(x, 2 * H)
            ST[at, 4:5] = mean
            ST[at, 5:6] = inverse
            for h in range(2):
                v = (x[h] - mean) * inverse * VX[h, 1:2, :] + VX[h, 2:3, :]
                POOL[rows(SX_AT + h * ROWS, m, r, WIDE), :] = gelu_slope(v)[1].astype(bf16)

        unroll(LEN // WIDE, tile)

    def stage_q(m):
        x_send(m, GH).wait_recv()
        for h in range(2):
            TG[h * LEN : (h + 1) * LEN, :] = dot(XR[rows(0, m), :], WX[h], NN)

        def tile(i):
            r = i * WIDE
            at = rows(0, m, r, WIDE)
            mean, inverse = ST[at, 4:5], ST[at, 5:6]
            ys, normeds = [], []
            for h in range(2):
                slope = POOL[rows(SX_AT + h * ROWS, m, r, WIDE), :].astype(f32)
                ys.append(TG[pl.ds(h * LEN + r, WIDE), :] * slope)
                normeds.append((POOL[rows(LV_AT + h * ROWS, m, r, WIDE), :].astype(f32) - mean) * inverse)
            grads = norm_back(ys, normeds, inverse, [VX[h, 1:2, :] for h in range(2)], 2 * H)
            for h in range(2):
                U[h, at, :] = (U[h, at, :].astype(f32) + grads[h]).astype(bf16)

        unroll(LEN // WIDE, tile)

    def back_three(m):
        here = rows(0, m)
        TG[LEN : 2 * LEN, :] = dot(U[0, here, :], W[0], NT) + dot(U[1, here, :], W[1], NT)

    def stage_p1(m, reach):
        back_three(m)

        def tile(i):
            r = i * TILE
            at = rows(0, m, r, TILE)
            y_ = TG[pl.ds(LEN + r, TILE), :] * S3[at, :].astype(f32)
            normed = N3[at, :].astype(f32)
            (grad,) = norm_back([y_], [normed], ST[at, 3:4], [V640[4:5, :]], H)
            low = grad.astype(bf16)
            GM[m, pl.ds(pl.multiple_of(LEN + r, 16), TILE), :] = low
            AC[4] += eights(y_ * normed)
            AC[5] += eights(y_)
            AC[1] += eights(low.astype(f32))
            for h in range(2):
                AC[6 + h] += eights(U[h, at, :].astype(f32))

        unroll(LEN // TILE, tile)
        halo(GM, hg_s, hg_r, m, reach, True)

    def stage_p2(m, span, relay):
        halo(GM, hg_s, hg_r, m, 2 * span, False)
        TG[0:LEN, :] = sum(dot(GM[m, pl.ds(LEN - (t - 2) * span, LEN), :], W[4 + t], NN) for t in (2, 0, 1, 3, 4))

        def tile(i):
            r = i * TILE
            at = rows(0, m, r, TILE)
            y_ = TG[pl.ds(r, TILE), :] * S2[at, :].astype(f32)
            normed = N2[at, :].astype(f32)
            (grad,) = norm_back([y_], [normed], ST[at, 2:3], [V640[2:3, :]], H)
            low = grad.astype(bf16)
            GH[at, :] = low
            AC[2] += eights(y_ * normed)
            AC[3] += eights(y_)
            AC[0] += eights(low.astype(f32))

        unroll(LEN // TILE, tile)
        if relay:
            x_send(m, GH).start()

    def stage_p3(m):
        for h in range(2):
            TG[h * LEN : (h + 1) * LEN, :] = dot(GH[rows(0, m), :], W[2 + h], NN)

        def tile(i):
            r = i * WIDE
            at = rows(0, m, r, WIDE)
            mean, inverse = ST[at, 0:1], ST[at, 1:2]
            ys, normeds = [], []
            for h in range(2):
                ys.append(TG[pl.ds(h * LEN + r, WIDE), :] * S1[h, at, :].astype(f32))
                normeds.append((POOL[rows(E_AT + h * ROWS, m, r, WIDE), :].astype(f32) - mean) * inverse)
            grads = norm_back(ys, normeds, inverse, [V1280[h, 1:2, :] for h in range(2)], 2 * H)
            for h in range(2):
                S1[h, at, :] = (U[h, at, :].astype(f32) + grads[h]).astype(bf16)
                AC[8 + h] += eights(ys[h] * normeds[h])
                AC[10 + h] += eights(ys[h])

        unroll(LEN // WIDE, tile)
        for h in range(2):
            out_ig(m, h).start()

    def prepare():
        AC[...] = jnp.zeros_like(AC)
        for ref in (A2, GM):

            @pl.when(seq == 0)
            def _():
                for m in range(MICRO):
                    ref[m, 0:LEN, :] = jnp.zeros((LEN, H), bf16)

            @pl.when(seq == 3)
            def _():
                for m in range(MICRO):
                    ref[m, 2 * LEN : 3 * LEN, :] = jnp.zeros((LEN, H), bf16)

        for m in range(MICRO):
            ST[m * LEN : (m + 1) * LEN, 6:7] = jnp.transpose(jnp.broadcast_to(mask[m : m + 1, :].astype(f32), (128, LEN)))[:, 0:1]
        for m in range(MICRO):
            for h in range(2):
                load_in(m, h, xin, POOL.at[pl.ds(E_AT + h * ROWS + m * LEN, LEN), :]).wait()
                load_in(m, h, cot, U.at[h, pl.ds(m * LEN, LEN), :]).wait()

        def masked(m):
            at = rows(0, m)
            keep = ST[at, 6:7]
            for h in range(2):
                U[h, at, :] = (U[h, at, :].astype(f32) * keep).astype(bf16)

        loop(MICRO, masked)

    SPAN_0, SPAN_1 = DILATION_BASE, 2 * DILATION_BASE
    span = DILATION_BASE * (1 + sec)
    early = 0
    if fused:
        gather_begin()
        prepare()
        own_w.wait()
        vectors()
        early = MICRO

        def step(k):
            gather_step(k)

            @pl.when(jnp.logical_and(first, jnp.logical_and(k >= 1, k < 1 + MICRO)))
            def _():
                stage_first(k - 1)

            @pl.when(jnp.logical_and(first, jnp.logical_and(k >= A_STEP, k < A_STEP + MICRO)))
            def _():
                stage_a(k - A_STEP, 2 * SPAN_0)

        loop(BLOCKS + 4, step)
    else:
        own_w.wait()
        own_v.wait()
        for src, dst in ((v640_in, V640), (v1280_in, V1280), (vx_in, VX)):
            dst[...] = src[...]
        prepare()

    @pl.when(first)
    def _():
        def firsts(m):
            stage_first(m)
            stage_a(m, 2 * SPAN_0)

        if early == 0:
            loop(MICRO, firsts)
        loop(MICRO, lambda m: stage_b(m, SPAN_0, True))
        if fused:
            others_blocks()
        loop(MICRO, stage_n)

        def backward(m):
            stage_q(m)
            stage_p1(m, 2 * SPAN_0)

            @pl.when(m > 0)
            def _():
                stage_p3(m - 1)

            @pl.when(m < MICRO - 1)
            def _():
                stage_p2(m, SPAN_0, False)

        loop(MICRO, backward)

    @pl.when(jnp.logical_not(first))
    def _():
        if fused:
            others_blocks()

        def both(k):
            @pl.when(k == MICRO + 1)
            def _():
                loop(MICRO - 1, stage_p3)

            @pl.when(k < MICRO)
            def _():
                stage_x(k)
                stage_first(k)
                stage_a(k, 2 * SPAN_1)

            inner = jnp.logical_and(k >= 1, k <= MICRO)

            @pl.when(inner)
            def _():
                stage_b(k - 1, SPAN_1, False)

            @pl.when(k >= 2)
            def _():
                stage_p2(k - 2, SPAN_1, True)

            @pl.when(inner)
            def _():
                stage_p1(k - 1, 2 * SPAN_1)

        loop(MICRO + 2, both)

    def last_grad_hidden():
        @pl.when(first)
        def _():
            stage_p2(MICRO - 1, SPAN_0, False)

    def last_input_grad():
        stage_p3(MICRO - 1)
        for i in range(12):
            VS[0, i : i + 1, :] = jnp.sum(AC[i], axis=0, keepdims=True)
        VS[0, 12:16, :] = jnp.zeros((4, H), f32)

    def relay_drain():
        loop(MICRO, lambda m: x_send(m, A3).wait_send())

        def out_wait(m):
            for h in range(2):
                out_bo(m, h).wait()
                out_ig(m, h).wait()

        loop(MICRO, out_wait)

    def gradient(b):
        @pl.when(b < 2)
        def _():
            TG[...] = dot(A3[...], U[b], TN)

        @pl.when(jnp.logical_and(b >= 2, b < 4))
        def _():
            TG[...] = dot(GH[...], A1[b - 2], TN)

        @pl.when(b >= 4)
        def _():
            at = pl.ds(pl.multiple_of(LEN + (b - 6) * span, 64), LEN)
            TG[...] = sum(dot(GM[m, LEN : 2 * LEN, :], A2[m, at, :], TN) for m in range(MICRO))

    if not fused:
        last_grad_hidden()
        last_input_grad()
        relay_drain()

        def whole(b):
            gradient(b)
            out = pltpu.make_async_copy(TG, gout.at[b], o_g.at[b])
            out.start()
            out.wait()

        loop(BLOCKS, whole)
        vout[...] = VS[0]
        return

    kind = lambda p: lax.rem(p + 2, 3)
    slot = lambda p: p // 3
    over_tensor_first = lambda p: kind(p) == 2
    zslot = lambda p: slot(p) + jnp.where(over_tensor_first(p), 3, 0)
    owned = lambda p: jnp.logical_or(over_tensor_first(p), kind(p) == y)
    block = lambda p: jnp.where(p < 2, p, jnp.where(p < 7, p + 2, p - 5))
    outer = jnp.logical_or(ten == 0, ten == SHARDS - 1)
    low_side = ten < SHARDS // 2
    FAR, NEAR = jnp.where(low_side, 3, 0), jnp.where(low_side, 2, 1)

    def half_of(half):
        return pl.ds(pl.multiple_of(half * HALF, 16), HALF)

    def part(p, s):
        return CR.at[p, pl.ds(pl.multiple_of(s * HALF, 16), HALF), :]

    def kept(p, s):
        return KEEP.at[lax.rem(p, KEEP_SLOTS), s * HALF : (s + 1) * HALF, :]

    def final(p, half):
        return gout.at[block(p), half_of(half), :]

    def rc(p):
        return remote(GIVE.at[lax.rem(p, GIVE_SLOTS)], CR.at[p], rc_s.at[p], rc_r.at[p], at_core)

    def ry(p, s):
        return remote(part(p, s), YR.at[slot(p), s], ry_s.at[slot(p), s], ry_r.at[slot(p), s], at_y)

    def rz(p, s, idx_send, idx, to):
        return remote(part(p, s), ZR.at[zslot(p), idx], rz_s.at[zslot(p), idx_send], rz_r.at[zslot(p), idx], (sec, seq, to))

    def fy(p, into):
        return remote(part(p, ten), into, fy_s.at[p], fy_r.at[p], at_y)

    def fc(p, src, half):
        return remote(src, final(p, half), fc_s.at[p], fc_r.at[p], at_core)

    def out_g(p):
        return pltpu.make_async_copy(part(p, ten), final(p, core), o_g.at[p])

    def add(ref, *others_):
        total = ref[...].astype(f32)
        for other in others_:
            total = total + other[...].astype(f32)
        ref[...] = total.astype(bf16)

    def compute(p):
        @pl.when(p >= GIVE_SLOTS)
        def _():
            rc(p - GIVE_SLOTS).wait_send()

        gradient(block(p))
        for s in range(SHARDS):
            theirs = TG[pl.ds(pl.multiple_of(s * PART + (1 - core) * HALF, 16), HALF), :]
            GIVE[lax.rem(p, GIVE_SLOTS), s * HALF : (s + 1) * HALF, :] = theirs.astype(bf16)
        rc(p).start()
        for s in range(SHARDS):
            kept(p, s)[...] = TG[pl.ds(pl.multiple_of(s * PART + core * HALF, 16), HALF), :].astype(bf16)

    def over_core(p):
        rc(p).wait_recv()
        for s in (0, 3, 1, 2):
            add(part(p, s), kept(p, s))

            @pl.when(jnp.logical_not(owned(p)))
            def _():
                ry(p, s).start()

    def over_y(p):
        @pl.when(owned(p))
        def _():
            for s in (0, 3, 1, 2):
                ry(p, s).wait_recv()
                add(part(p, s), YR.at[slot(p), s])

    def chain_one(p):
        @pl.when(jnp.logical_and(owned(p), outer))
        def _():
            for k in range(3):
                s = jnp.where(low_side, 3 - k, k)
                idx = jnp.where(low_side, s - 1, s)
                rz(p, s, idx, idx, jnp.where(low_side, 1, 2)).start()

        @pl.when(jnp.logical_and(owned(p), jnp.logical_not(outer)))
        def _():
            s = jnp.where(low_side, 0, 3)
            rz(p, s, 0, 0, s).start()

    def chain_two(p):
        @pl.when(jnp.logical_and(owned(p), jnp.logical_not(outer)))
        def _():
            for s, idx, idx_send in ((FAR, jnp.where(low_side, 2, 0), 1), (NEAR, 1, 2)):
                rz(p, s, idx_send, idx, s).wait_recv()
                add(part(p, s), ZR.at[zslot(p), idx])
                rz(p, s, idx_send, 3, s).start()

    def chain_end(p):
        @pl.when(owned(p))
        def _():
            idx = jnp.where(ten == 2, 2, 0)
            rz(p, ten, 0, idx, ten).wait_recv()
            rz(p, ten, 0, 3, ten).wait_recv()
            add(part(p, ten), ZR.at[zslot(p), idx], ZR.at[zslot(p), 3])

            @pl.when(over_tensor_first(p))
            def _():
                fy(p, YX.at[slot(p)]).start()

            @pl.when(jnp.logical_not(over_tensor_first(p)))
            def _():
                fy(p, final(p, core)).start()
                fc(p, part(p, ten), core).start()
                out_g(p).start()

    def settle(p):
        @pl.when(over_tensor_first(p))
        def _():
            fy(p, YX.at[slot(p)]).wait()
            add(part(p, ten), YX.at[slot(p)])
            fc(p, part(p, ten), core).start()
            out_g(p).start()

        @pl.when(jnp.logical_not(owned(p)))
        def _():
            fy(p, final(p, core)).wait_recv()
            fc(p, final(p, core), core).start()

    def finish(p):
        fc(p, part(p, ten), 1 - core).wait_recv()

    def vector_round(i):
        pair, far = ten + 1 - 2 * lax.rem(ten, 2), lax.rem(ten + 2, SHARDS)
        where_seq = jnp.where(i == 0, y * 2 + 1 - core, jnp.where(i == 1, (1 - y) * 2 + core, seq))
        where_ten = jnp.where(i == 2, pair, jnp.where(i == 3, far, ten))
        return remote(VS.at[i], VR.at[i], vr_s.at[i], vr_r.at[i], (sec, where_seq, where_ten))

    def sums(t):
        for stage, lag, first_kind in SCHEDULE:
            p = t - lag
            fits = jnp.logical_and(p >= 0, p < BLOCKS)
            if first_kind is not None:
                fits = jnp.logical_and(fits, over_tensor_first(p) if first_kind else jnp.logical_not(over_tensor_first(p)))
            if stage == "compute":

                @pl.when(p == BLOCKS - 2)
                def _():
                    last_grad_hidden()

            @pl.when(fits)
            def _():
                dict(compute=compute, core=over_core, y=over_y, one=chain_one, two=chain_two, end=chain_end, settle=settle, finish=finish)[stage](p)

        @pl.when(t == BLOCKS)
        def _():
            last_input_grad()

        i = t - BLOCKS - 1

        @pl.when(jnp.logical_and(i > 0, i <= 4))
        def _():
            vector_round(i - 1).wait()
            VS[i] = VS[i - 1] + VR[i - 1]

        @pl.when(jnp.logical_and(i >= 0, i < 4))
        def _():
            vector_round(i).start()

    loop(BLOCKS + LAST_LAG, sums)
    vout[...] = VS[4]

    relay_drain()
    loop(BLOCKS, gather_drain)

    def drain(p):
        @pl.when(p >= BLOCKS - GIVE_SLOTS)
        def _():
            rc(p).wait_send()

        fc(p, part(p, ten), core).wait_send()

        @pl.when(owned(p))
        def _():
            out_g(p).wait()

            @pl.when(jnp.logical_not(over_tensor_first(p)))
            def _():
                fy(p, final(p, core)).wait_send()

            for k in range(3):
                rz(p, ten, k, 0, ten).wait_send()

        @pl.when(jnp.logical_not(owned(p)))
        def _():
            for s in range(SHARDS):
                ry(p, s).wait_send()

    loop(BLOCKS, drain)


def relay(block_input, cotangent, mask, weights, vectors, fused):
    hbm = pl.BlockSpec(memory_space=pl.ANY)
    vmem = pl.BlockSpec(memory_space=pltpu.VMEM)
    dma = lambda *shape: pltpu.SemaphoreType.DMA(shape)
    low = lambda *shape: pltpu.VMEM(shape, bf16)
    full = lambda *shape: pltpu.VMEM(shape, f32)
    scratch = [
        low(BLOCKS, H, H),
        low(2, H, H),
        low(POOL_ROWS, H),
        low(2, ROWS, H),
        low(2, ROWS, H),
        low(MICRO, 3 * LEN, H),
        low(ROWS, H),
        low(ROWS, H),
        low(ROWS, H),
        low(ROWS, H),
        low(ROWS, H),
        low(2, ROWS, H),
        low(MICRO, 3 * LEN, H),
        low(ROWS, H),
        low(ROWS, H),
        full(ROWS, 8),
        full(H, H),
        full(16, H),
        full(2, 8, H),
        full(2, 8, H),
        full(12, 8, H),
        full(5, 16, H),
        dma(MICRO, 2, 2),
        dma(2),
        dma(MICRO, 2),
        dma(MICRO, 2),
        dma(MICRO),
        dma(MICRO),
        dma(MICRO, 2),
        dma(MICRO, 2),
        dma(MICRO, 2),
        dma(MICRO, 2),
    ]
    if fused:
        scratch += [
            low(2, SHARDS, 16, 256),
            low(BLOCKS, SHARDS * HALF, H),
            low(KEEP_SLOTS, SHARDS * HALF, H),
            low(GIVE_SLOTS, SHARDS * HALF, H),
            low(3, SHARDS, HALF, H),
            low(6, 4, HALF, H),
            low(3, HALF, H),
            full(4, 16, H),
            dma(7),
            dma(7),
            dma(BLOCKS, SHARDS, 2),
            dma(BLOCKS, SHARDS),
            dma(BLOCKS, SHARDS),
            dma(BLOCKS, SHARDS),
            dma(BLOCKS, SHARDS),
            dma(BLOCKS, SHARDS),
            dma(2, SHARDS),
            dma(2, SHARDS),
            dma(2, SHARDS),
            dma(2, SHARDS),
            dma(BLOCKS),
            dma(BLOCKS),
            dma(3, SHARDS),
            dma(3, SHARDS),
            dma(6, 3),
            dma(6, 4),
            dma(BLOCKS),
            dma(BLOCKS),
            dma(BLOCKS),
            dma(BLOCKS),
            dma(4),
            dma(4),
        ]
    scratch += [dma(BLOCKS)]
    outs = (
        jax.ShapeDtypeStruct((MICRO, LEN, 2 * H), bf16),
        jax.ShapeDtypeStruct((MICRO, LEN, 2 * H), bf16),
        jax.ShapeDtypeStruct((BLOCKS, PART, H), bf16) if fused else jax.ShapeDtypeStruct((BLOCKS, H, H), f32),
        jax.ShapeDtypeStruct((16, H), f32),
    )
    in_specs = [hbm, hbm, vmem] + [hbm] * len(weights) + ([hbm] if fused else [vmem] * 3)
    return pl.pallas_call(
        functools.partial(relay_kernel, fused),
        out_shape=outs,
        in_specs=in_specs,
        out_specs=(hbm, hbm, hbm, vmem),
        scratch_shapes=scratch,
        compiler_params=pltpu.CompilerParams(collective_id=0, has_side_effects=True, vmem_limit_bytes=62 * 2**20),
        cost_estimate=pl.CostEstimate(flops=25_000_000_000, bytes_accessed=20_000_000, transcendentals=4_000_000),
        name="relay",
    )(block_input, cotangent, mask, *weights, *vectors)


def packed_weights(conv_in, conv_mid, conv_out):
    channels = conv_out.shape[0]
    halves = lambda m: m.reshape(channels, 2, H).transpose(1, 0, 2)
    return jnp.concatenate([halves(conv_out), halves(conv_in.T), conv_mid.transpose(0, 2, 1)])


def local(*args):
    block_input, cotangent, mask = args[:3]
    (conv_in, bias_in, conv_mid, bias_mid, conv_out, bias_out, gain_first, shift_first, gain_second, shift_second, gain_third, shift_third) = (a[0] for a in args[3:])
    ten, sec = lax.axis_index("tensor"), lax.axis_index("section")
    shards = lax.axis_size("tensor")
    fused = shards == SHARDS
    channels = conv_out.shape[0]
    xin = block_input.reshape(MICRO, LEN, 2 * H)
    cot = cotangent.reshape(MICRO, LEN, 2 * H)
    mask = mask.reshape(MICRO, LEN)
    mine = packed_weights(conv_in, conv_mid, conv_out)
    narrow = (bias_in, bias_mid, gain_second, shift_second, gain_third, shift_third)
    wide = (bias_out, gain_first, shift_first)
    if fused:
        lines = jnp.stack(list(narrow) + [w[:PART] for w in wide] + [w[PART:] for w in wide])
        vsh = jnp.pad(lines, ((0, 4), (0, 256 - PART)))
        block_out, input_grad, grads, small = relay(xin, cot, mask, (mine,), (vsh,), True)
        grads = grads.astype(f32)
    else:
        whole = lax.all_gather(mine, "tensor", axis=1, tiled=True)
        swap = [(0, 1), (1, 0)]
        give = jnp.where(sec == 0, whole[0:2], whole[2:4])
        other = lax.ppermute(give, "section", swap)
        v_narrow = lax.all_gather(jnp.stack(narrow), "tensor", axis=1, tiled=True)
        v_wide = lax.all_gather(jnp.stack(wide), "tensor", axis=1, tiled=True)
        v640 = jnp.pad(v_narrow.astype(f32), ((0, 10), (0, 0)))
        v1280 = jnp.pad(v_wide.astype(f32).reshape(3, 2, H).transpose(1, 0, 2), ((0, 0), (0, 5), (0, 0)))
        vx = lax.ppermute(v1280, "section", swap)
        block_out, input_grad, grads, small = relay(xin, cot, mask, (whole, other), (v640, v1280, vx), False)
        grads = lax.psum(lax.psum_scatter(grads, "tensor", scatter_dimension=1, tiled=True), "seq")
        small = lax.psum(small, ("seq", "tensor"))
    grad_in = grads[2:4].transpose(0, 2, 1).reshape(2 * H, channels)
    grad_out = grads[0:2].transpose(1, 0, 2).reshape(channels, 2 * H)
    grad_mid = grads[4:9].transpose(0, 2, 1)
    thin = lax.dynamic_slice_in_dim(small[0:6], ten * channels, channels, 1)
    thick = lax.dynamic_slice_in_dim(small[6:12].reshape(3, 2 * H), ten * 2 * channels, 2 * channels, 1)
    shape = (1, MICRO, 1, LEN, 2 * H)
    return (
        block_out.reshape(shape),
        input_grad.reshape(shape),
        grad_in[None],
        thin[0:1],
        grad_mid[None],
        thin[1:2],
        grad_out[None],
        thick[0:1],
        thick[1:2],
        thick[2:3],
        thin[2:3],
        thin[3:4],
        thin[4:5],
        thin[5:6],
    )


def solution(mesh):
    in_specs = (
        P(None, "tensor", "seq", None),
        P(None, "tensor", "seq", None),
        P(None, "tensor", "seq"),
        P("section", None, "tensor"),
        P("section", "tensor"),
        P("section", None, None, "tensor"),
        P("section", "tensor"),
        P("section", "tensor", None),
        P("section", "tensor"),
        P("section", "tensor"),
        P("section", "tensor"),
        P("section", "tensor"),
        P("section", "tensor"),
        P("section", "tensor"),
        P("section", "tensor"),
    )
    out_specs = (
        P("section", None, "tensor", "seq", None),
        P("section", None, "tensor", "seq", None),
        P("section", None, "tensor"),
        P("section", "tensor"),
        P("section", None, None, "tensor"),
        P("section", "tensor"),
        P("section", "tensor", None),
        P("section", "tensor"),
        P("section", "tensor"),
        P("section", "tensor"),
        P("section", "tensor"),
        P("section", "tensor"),
        P("section", "tensor"),
        P("section", "tensor"),
    )
    return jax.shard_map(local, mesh=mesh, in_specs=in_specs, out_specs=out_specs, check_vma=False)
```

```python
import functools

import jax
import jax.numpy as jnp
from jax import lax
from jax.experimental import pallas as pl
from jax.experimental.pallas import tpu as pltpu
from jax.sharding import PartitionSpec as P

DILATION_BASE = 64
EPS = 1e-05
ROOT_HALF = 0.7071067811865476
INVERSE_ROOT_TWO_PI = 0.3989422804014327
MESH = pl.DeviceIdType.MESH
f32 = jnp.float32
bf16 = jnp.bfloat16

MICRO = 4
LEN = 256
H = 640
ROWS = MICRO * LEN
SHARDS = 4
PART = H // SHARDS
HALF = PART // 2
BLOCKS = 9
TILE = 256
WIDE = 128
Y_LAG, C_LAG = 1, 6
X_STEP = 9
F_STEP = 2
A_STEP = C_LAG + 1
LEAD = 3
NN = (((1,), (0,)), ((), ()))
NT = (((1,), (1,)), ((), ()))
TN = (((0,), (0,)), ((), ()))

E_AT, SX_AT, LV_AT, POOL_ROWS = 0, 2 * ROWS, 4 * ROWS, 6 * ROWS
KEEP_SLOTS, GIVE_SLOTS = 3, 3
SCHEDULE = (
    ("two", 6, False),
    ("compute", 0, None),
    ("settle", 12, True),
    ("core", 1, None),
    ("end", 8, True),
    ("settle", 12, False),
    ("two", 3, True),
    ("one", 1, True),
    ("end", 8, False),
    ("y", 4, False),
    ("one", 4, False),
)
LAST_LAG = 12
LATE = 2


def dot(a, b, dims):
    return lax.dot_general(a, b, dims, preferred_element_type=f32)


def loop(count, body):
    def step(i, carry):
        body(i)
        return carry

    lax.fori_loop(0, count, step, 0)


def unroll(count, body):
    for i in range(count):
        body(i)


def row_stats(parts, width):
    mean = sum(jnp.sum(x, axis=-1, keepdims=True) for x in parts) / width
    spread = sum(jnp.sum(x * x, axis=-1, keepdims=True) for x in parts) / width - mean * mean
    return mean, lax.rsqrt(spread + EPS)


def gelu_slope(v):
    phi = 0.5 * (1.0 + lax.erf(v * ROOT_HALF))
    return phi, phi + v * (jnp.exp(-0.5 * v * v) * INVERSE_ROOT_TWO_PI)


def norm_back(ys, normeds, inverse, gains, width):
    scaled = [y * g for y, g in zip(ys, gains)]
    total = sum(jnp.sum(s, axis=-1, keepdims=True) for s in scaled) / width
    along = sum(jnp.sum(s * n, axis=-1, keepdims=True) for s, n in zip(scaled, normeds)) / width
    return [inverse * (s - total - n * along) for s, n in zip(scaled, normeds)]


def eights(x):
    return jnp.sum(x.reshape(x.shape[0] // 8, 8, x.shape[1]), axis=0)


def relay_kernel(fused, *refs):
    if fused:
        (xin, cot, mask, w_in, w_mid, w_out) = refs[:6]
        narrow_in, wide_in = refs[6:12], refs[12:15]
        (bo, ig, gout, vout) = refs[15:19]
        rest = refs[19:]
    else:
        (xin, cot, mask, wfull, wother, v640_in, v1280_in, vx_in, bo, ig, gout, vout) = refs[:12]
        rest = refs[12:]
    (W, WX, POOL, A1, S1, A2, S2, N2, A3, S3, N3, U, GM, GH, XR, ST, TG, V640, V1280, VX, AC, VS) = rest[:22]
    (l_in, l_w, o_s, x_s, x_r, ha_s, ha_r, hg_s, hg_r) = rest[22:31]
    if fused:
        (VF, VG, CR, KEEP, GIVE, YR, ZR, YX, VR, g_s, vg_r, ga_r, gc_r, wx_r, wc_r, r_s, rc_s, rc_r, ry_r, rz_r, yx_s, fy_r, fc_r, vr_s, vr_r) = rest[31:]

    sec = lax.axis_index("section")
    seq = lax.axis_index("seq")
    ten = lax.axis_index("tensor")
    y = seq // 2
    core = lax.rem(seq, 2)
    at_core = (sec, y * 2 + (1 - core), ten)
    at_y = (sec, (1 - y) * 2 + core, ten)
    at_diag = (sec, (1 - y) * 2 + (1 - core), ten)
    at_x = (1 - sec, seq, ten)
    up, down = (sec, seq, ten + 1), (sec, seq, ten - 1)
    behind, ahead = (sec, seq - 1, ten), (sec, seq + 1, ten)
    first = sec == 0

    def remote(src, dst, send, recv, where):
        return pltpu.make_async_remote_copy(src_ref=src, dst_ref=dst, send_sem=send, recv_sem=recv, device_id=where, device_id_type=MESH)

    def left(send, count, width=None):
        lines = VG.at[pl.ds(0, count)] if width else POOL.at[pl.ds(0, count), :]
        remote(lines, lines, send, x_r.at[0], at_x).wait_send()

    def rows(base, m, r=0, n=LEN):
        return pl.ds(pl.multiple_of(base + m * LEN + r, 16), n)

    def load_in(m, h, ref, into, sem):
        pltpu.make_async_copy(ref.at[m, 0, :, pl.ds(h * H, H)], into, sem).start()

    def loaded(into, sem):
        pltpu.make_async_copy(into, into, sem).wait()

    if fused:
        own_rows = pl.ds(pl.multiple_of(ten * PART, 16), PART)
        own = [pltpu.make_async_copy(w_in.at[:, pl.ds(h * H, H)], W.at[h, own_rows, :], l_w.at[h]) for h in range(2)]
        own += [pltpu.make_async_copy(w_out.at[:, pl.ds(h * H, H)], W.at[2 + h, own_rows, :], l_w.at[2 + h]) for h in range(2)]
        own += [pltpu.make_async_copy(w_mid, W.at[pl.ds(4, 5), own_rows, :], l_w.at[4])]
        partners = [at_core, at_y, at_diag]
        others = [(s, d) for s in range(2) for d in range(SHARDS) if s or d]
        partners += [(lax.rem(sec + s, 2), seq, lax.rem(ten + d, SHARDS)) for s, d in others]
    else:
        own = [pltpu.make_async_copy(wfull, W, l_w.at[0]), pltpu.make_async_copy(wother, WX, l_w.at[1])]
        partners = [at_core, at_diag, at_x]
    for copy in own:
        copy.start()
    for m in range(MICRO):
        for h in range(2):
            load_in(m, h, xin, POOL.at[pl.ds(E_AT + h * ROWS + m * LEN, LEN), :], l_in.at[0])
            load_in(m, h, cot, U.at[h, pl.ds(m * LEN, LEN), :], l_in.at[1])

    if fused:
        VF[...] = jnp.zeros_like(VF)
        for i, ref in enumerate(narrow_in):
            VF[i : i + 1, 0:PART] = ref[...].astype(f32)
        for i, ref in enumerate(wide_in):
            for half in range(2):
                VF[6 + 3 * half + i : 7 + 3 * half + i, 0:PART] = ref[:, half * PART : (half + 1) * PART].astype(f32)
        VG[sec * SHARDS + ten] = VF[...].astype(bf16)

    barrier = pltpu.get_barrier_semaphore()
    for partner in partners:
        pl.semaphore_signal(barrier, inc=1, device_id=partner, device_id_type=MESH)
    pl.semaphore_wait(barrier, len(partners))

    def piece(ref, b, s, half):
        return ref.at[b, pl.ds(pl.multiple_of(s * PART + half * HALF, 16), HALF), :]

    UP, DOWN, Y_, CORE_, X_, XC_, V_ = range(7)

    def gz(b, s, to_up):
        spot = piece(W, b, s, core)
        return remote(spot, spot, g_s.at[UP if to_up else DOWN], ga_r.at[b, s], up if to_up else down)

    def gy(b, s):
        spot = piece(W, b, s, core)
        return remote(spot, spot, g_s.at[Y_], ga_r.at[b, s], at_y)

    def gc(b, s):
        spot = piece(W, b, s, core)
        return remote(spot, spot, g_s.at[CORE_], gc_r.at[b], at_core)

    def gc_here(b):
        lines = W.at[b, pl.ds(0, (SHARDS - 1) * HALF), :]
        remote(lines, lines, g_s.at[CORE_], gc_r.at[b], at_core).wait_recv()

    def wanted(b):
        return b // 2 == 1 - sec

    def gx(b, s):
        k = lax.rem(b, 2)
        return remote(piece(W, b, s, core), piece(WX, k, s, core), g_s.at[X_], wx_r.at[k], at_x)

    def gx_here(k):
        lines = WX.at[k, pl.ds(0, SHARDS * HALF), :]
        remote(lines, lines, g_s.at[X_], wx_r.at[k], at_x).wait_recv()

    def gxc(k, s):
        spot = piece(WX, k, s, core)
        return remote(spot, spot, g_s.at[XC_], wc_r.at[0], at_core)

    def gv(i):
        s, d = others[i]
        return remote(VG.at[sec * SHARDS + ten], VG.at[sec * SHARDS + ten], g_s.at[V_], vg_r.at[0], (lax.rem(sec + s, 2), seq, lax.rem(ten + d, SHARDS)))

    mine = lambda b: jnp.logical_or(b == BLOCKS - 1, lax.rem(b, 2) == y)
    def send_own(b):
        @pl.when(jnp.logical_and(mine(b), ten < SHARDS - 1))
        def _():
            gz(b, ten, True).start()

        @pl.when(jnp.logical_and(mine(b), ten > 0))
        def _():
            gz(b, ten, False).start()

        @pl.when(wanted(b))
        def _():
            gx(b, ten).start()

    def gather_begin():
        for b in range(LEAD):
            own[b].wait()
            send_own(b)
        for i in range(len(others)):
            gv(i).start()
        for copy in own[LEAD:]:
            copy.wait()

    def gather_step(k):
        @pl.when(k + LEAD < BLOCKS)
        def _():
            send_own(k + LEAD)

        for d in range(1, SHARDS):
            b = k - (d - 1)
            ok = jnp.logical_and(b >= 0, b < BLOCKS)
            for above in (False, True):
                s = ten + d if above else ten - d
                there = jnp.logical_and(ok, s < SHARDS if above else s >= 0)
                onward = (ten > 0) if above else (ten < SHARDS - 1)

                @pl.when(jnp.logical_and(there, mine(b)))
                def _():
                    gz(b, s, True).wait_recv()

                    @pl.when(onward)
                    def _():
                        gz(b, s, not above).start()

                    @pl.when(b < BLOCKS - 1)
                    def _():
                        gy(b, s).start()

                    gc(b, s).start()

                    @pl.when(wanted(b))
                    def _():
                        gx(b, s).start()

        for d in range(1, SHARDS):
            b = k - d - Y_LAG
            ok = jnp.logical_and(b >= 0, b < BLOCKS)
            for above in (False, True):
                s = ten + d if above else ten - d
                there = jnp.logical_and(ok, s < SHARDS if above else s >= 0)

                @pl.when(jnp.logical_and(there, jnp.logical_not(mine(b))))
                def _():
                    gy(b, s).wait_recv()
                    gc(b, s).start()

                    @pl.when(wanted(b))
                    def _():
                        gx(b, s).start()

        b = k - C_LAG

        @pl.when(jnp.logical_and(b >= 0, b < BLOCKS))
        def _():
            gc_here(b)

        @pl.when(jnp.logical_and(k >= X_STEP, k < X_STEP + 2))
        def _():
            gx_here(k - X_STEP)
            for s in range(SHARDS):
                gxc(k - X_STEP, s).start()

    def others_blocks():
        lines = POOL.at[pl.ds(0, 2 * SHARDS * HALF), :]
        remote(lines, lines, g_s.at[XC_], wc_r.at[0], at_core).wait_recv()

    def gather_drain():
        left(g_s.at[V_], len(others), True)
        left(g_s.at[Y_], 4 * (SHARDS - 1) * HALF)
        left(g_s.at[CORE_], BLOCKS * (SHARDS - 1) * HALF)
        left(g_s.at[X_], 2 * SHARDS * HALF)
        left(g_s.at[XC_], 2 * SHARDS * HALF)
        for z in range(SHARDS):

            @pl.when(ten == z)
            def _():
                if z < SHARDS - 1:
                    left(g_s.at[UP], 5 * (z + 1) * HALF)
                if z > 0:
                    left(g_s.at[DOWN], 5 * (SHARDS - z) * HALF)

    def vectors():
        lines = VG.at[pl.ds(0, len(others))]
        remote(lines, lines, g_s.at[V_], vg_r.at[0], at_x).wait_recv()
        line = lax.broadcasted_iota(jnp.int32, (2 * 128, H), 0)
        col = lax.broadcasted_iota(jnp.int32, (2 * 128, H), 1)

        def pick(offset):
            return jnp.where(col == line + offset, 1.0, 0.0).astype(bf16)

        narrow = jnp.zeros((16, H), f32)
        wide = [[jnp.zeros((16, H), f32) for _ in range(4)] for _ in range(2)]
        for s in range(SHARDS):
            inner = pick(s * PART)
            narrow = narrow + dot(VG[sec * SHARDS + s], inner, NN)
            for who in range(2):
                held = VG[(sec if who == 0 else 1 - sec) * SHARDS + s]
                for h in range(2):
                    for k in range(2):
                        put = pick(s * 2 * PART + k * PART - h * H)
                        wide[who][h * 2 + k] = wide[who][h * 2 + k] + dot(held, put, NN)
        V640[...] = narrow
        for who, into in ((0, V1280), (1, VX)):
            for h in range(2):
                into[h, 0:3, :] = wide[who][h * 2][6:9] + wide[who][h * 2 + 1][9:12]

    def halo(ref, sends, recvs, m, reach, start):
        fwd = remote(ref.at[m, pl.ds(2 * LEN - reach, reach), :], ref.at[m, pl.ds(LEN - reach, reach), :], sends.at[0], recvs.at[m, 0], ahead)
        bwd = remote(ref.at[m, pl.ds(LEN, reach), :], ref.at[m, pl.ds(2 * LEN, reach), :], sends.at[1], recvs.at[m, 1], behind)

        @pl.when(seq < 3)
        def _():
            fwd.start() if start else bwd.wait_recv()

        @pl.when(seq > 0)
        def _():
            bwd.start() if start else fwd.wait_recv()

    def halo_drain(sends):
        for s, reach in ((0, 2 * SPAN_0), (1, 2 * SPAN_1)):

            @pl.when(jnp.logical_and(sec == s, seq < 3))
            def _():
                left(sends.at[0], MICRO * reach)

            @pl.when(jnp.logical_and(sec == s, seq > 0))
            def _():
                left(sends.at[1], MICRO * reach)

    def x_send(m, src):
        return remote(src.at[rows(0, m), :], XR.at[rows(0, m), :], x_s.at[0], x_r.at[m], at_x)

    def stage_first(m):
        def tile(i):
            r = i * WIDE
            at = rows(0, m, r, WIDE)
            x = [POOL[rows(E_AT + h * ROWS, m, r, WIDE), :].astype(f32) for h in range(2)]
            mean, inverse = row_stats(x, 2 * H)
            ST[at, 0:1] = mean
            ST[at, 1:2] = inverse
            for h in range(2):
                v = (x[h] - mean) * inverse * V1280[h, 1:2, :] + V1280[h, 2:3, :]
                phi, slope = gelu_slope(v)
                A1[h, at, :] = (v * phi).astype(bf16)
                S1[h, at, :] = slope.astype(bf16)

        unroll(LEN // WIDE, tile)

    def stage_a(m, reach):
        here = rows(0, m)
        TG[0:LEN, :] = dot(A1[0, here, :], W[0], NT) + dot(A1[1, here, :], W[1], NT)

        def tile2(i):
            r = i * TILE
            at = rows(0, m, r, TILE)
            x = TG[pl.ds(r, TILE), :] + V640[0:1, :]
            mean, inverse = row_stats([x], H)
            normed = (x - mean) * inverse
            v = normed * V640[2:3, :] + V640[3:4, :]
            phi, slope = gelu_slope(v)
            A2[m, pl.ds(pl.multiple_of(LEN + r, 16), TILE), :] = (v * phi).astype(bf16)
            S2[at, :] = slope.astype(bf16)
            N2[at, :] = normed.astype(bf16)
            ST[at, 2:3] = inverse

        unroll(LEN // TILE, tile2)
        halo(A2, ha_s, ha_r, m, reach, True)

    def stage_b(m, span, relay):
        halo(A2, ha_s, ha_r, m, 2 * span, False)
        TG[0:LEN, :] = sum(dot(A2[m, pl.ds(LEN + (t - 2) * span, LEN), :], W[4 + t], NT) for t in (2, 0, 1, 3, 4))

        def tile(i):
            r = i * TILE
            at = rows(0, m, r, TILE)
            x = TG[pl.ds(r, TILE), :] + V640[1:2, :]
            mean, inverse = row_stats([x], H)
            normed = (x - mean) * inverse
            v = normed * V640[4:5, :] + V640[5:6, :]
            phi, slope = gelu_slope(v)
            A3[at, :] = (v * phi).astype(bf16)
            S3[at, :] = slope.astype(bf16)
            N3[at, :] = normed.astype(bf16)
            ST[at, 3:4] = inverse

        unroll(LEN // TILE, tile)
        if relay:
            x_send(m, A3).start()
        here = rows(0, m)
        for h in range(2):
            mixed = dot(A3[here, :], W[2 + h], NN) + V1280[h, 0:1, :]
            POOL[rows(LV_AT + h * ROWS, m), :] = (POOL[rows(E_AT + h * ROWS, m), :].astype(f32) + mixed).astype(bf16)
            out_bo(m, h).start()

    def out_bo(m, h):
        return pltpu.make_async_copy(POOL.at[rows(LV_AT + h * ROWS, m), :], bo.at[m, :, pl.ds(h * H, H)], o_s.at[0])

    def out_ig(m, h):
        return pltpu.make_async_copy(S1.at[h, rows(0, m), :], ig.at[m, :, pl.ds(h * H, H)], o_s.at[1])

    def stage_x(m):
        x_send(m, A3).wait_recv()
        for h in range(2):
            at = rows(E_AT + h * ROWS, m)
            mixed = dot(XR[rows(0, m), :], WX[h], NN) + VX[h, 0:1, :]
            POOL[at, :] = (POOL[at, :].astype(f32) + mixed).astype(bf16)

    def stage_n(m):
        def tile(i):
            r = i * WIDE
            at = rows(0, m, r, WIDE)
            x = [POOL[rows(LV_AT + h * ROWS, m, r, WIDE), :].astype(f32) for h in range(2)]
            mean, inverse = row_stats(x, 2 * H)
            ST[at, 4:5] = mean
            ST[at, 5:6] = inverse
            for h in range(2):
                v = (x[h] - mean) * inverse * VX[h, 1:2, :] + VX[h, 2:3, :]
                POOL[rows(SX_AT + h * ROWS, m, r, WIDE), :] = gelu_slope(v)[1].astype(bf16)

        unroll(LEN // WIDE, tile)

    def stage_q(m):
        x_send(m, GH).wait_recv()
        for h in range(2):
            TG[h * LEN : (h + 1) * LEN, :] = dot(XR[rows(0, m), :], WX[h], NN)

        def tile(i):
            r = i * WIDE
            at = rows(0, m, r, WIDE)
            mean, inverse = ST[at, 4:5], ST[at, 5:6]
            ys, normeds = [], []
            for h in range(2):
                slope = POOL[rows(SX_AT + h * ROWS, m, r, WIDE), :].astype(f32)
                ys.append(TG[pl.ds(h * LEN + r, WIDE), :] * slope)
                normeds.append((POOL[rows(LV_AT + h * ROWS, m, r, WIDE), :].astype(f32) - mean) * inverse)
            grads = norm_back(ys, normeds, inverse, [VX[h, 1:2, :] for h in range(2)], 2 * H)
            for h in range(2):
                U[h, at, :] = (U[h, at, :].astype(f32) + grads[h]).astype(bf16)

        unroll(LEN // WIDE, tile)

    def back_three(m):
        here = rows(0, m)
        TG[LEN : 2 * LEN, :] = dot(U[0, here, :], W[2], NT) + dot(U[1, here, :], W[3], NT)

    def stage_p1(m, reach):
        back_three(m)

        def tile(i):
            r = i * TILE
            at = rows(0, m, r, TILE)
            y_ = TG[pl.ds(LEN + r, TILE), :] * S3[at, :].astype(f32)
            normed = N3[at, :].astype(f32)
            (grad,) = norm_back([y_], [normed], ST[at, 3:4], [V640[4:5, :]], H)
            low = grad.astype(bf16)
            GM[m, pl.ds(pl.multiple_of(LEN + r, 16), TILE), :] = low
            AC[4] += eights(y_ * normed)
            AC[5] += eights(y_)
            AC[1] += eights(low.astype(f32))
            for h in range(2):
                AC[6 + h] += eights(U[h, at, :].astype(f32))

        unroll(LEN // TILE, tile)
        halo(GM, hg_s, hg_r, m, reach, True)

    def stage_p2(m, span, relay):
        halo(GM, hg_s, hg_r, m, 2 * span, False)
        TG[0:LEN, :] = sum(dot(GM[m, pl.ds(LEN - (t - 2) * span, LEN), :], W[4 + t], NN) for t in (2, 0, 1, 3, 4))

        def tile(i):
            r = i * TILE
            at = rows(0, m, r, TILE)
            y_ = TG[pl.ds(r, TILE), :] * S2[at, :].astype(f32)
            normed = N2[at, :].astype(f32)
            (grad,) = norm_back([y_], [normed], ST[at, 2:3], [V640[2:3, :]], H)
            low = grad.astype(bf16)
            GH[at, :] = low
            AC[2] += eights(y_ * normed)
            AC[3] += eights(y_)
            AC[0] += eights(low.astype(f32))

        unroll(LEN // TILE, tile)
        if relay:
            x_send(m, GH).start()

    def stage_p3(m):
        for h in range(2):
            TG[h * LEN : (h + 1) * LEN, :] = dot(GH[rows(0, m), :], W[h], NN)

        def tile(i):
            r = i * WIDE
            at = rows(0, m, r, WIDE)
            mean, inverse = ST[at, 0:1], ST[at, 1:2]
            ys, normeds = [], []
            for h in range(2):
                ys.append(TG[pl.ds(h * LEN + r, WIDE), :] * S1[h, at, :].astype(f32))
                normeds.append((POOL[rows(E_AT + h * ROWS, m, r, WIDE), :].astype(f32) - mean) * inverse)
            grads = norm_back(ys, normeds, inverse, [V1280[h, 1:2, :] for h in range(2)], 2 * H)
            for h in range(2):
                S1[h, at, :] = (U[h, at, :].astype(f32) + grads[h]).astype(bf16)
                AC[8 + h] += eights(ys[h] * normeds[h])
                AC[10 + h] += eights(ys[h])

        unroll(LEN // WIDE, tile)
        for h in range(2):
            out_ig(m, h).start()

    def prepare():
        AC[...] = jnp.zeros_like(AC)
        for ref in (A2, GM):

            @pl.when(seq == 0)
            def _():
                for m in range(MICRO):
                    ref[m, 0:LEN, :] = jnp.zeros((LEN, H), bf16)

            @pl.when(seq == 3)
            def _():
                for m in range(MICRO):
                    ref[m, 2 * LEN : 3 * LEN, :] = jnp.zeros((LEN, H), bf16)

        for m in range(MICRO):
            ST[m * LEN : (m + 1) * LEN, 6:7] = jnp.transpose(jnp.broadcast_to(mask[m].astype(f32), (128, LEN)))[:, 0:1]
        loaded(POOL.at[pl.ds(E_AT, 2 * ROWS), :], l_in.at[0])
        loaded(U, l_in.at[1])

        def masked(m):
            at = rows(0, m)
            keep = ST[at, 6:7]
            for h in range(2):
                U[h, at, :] = (U[h, at, :].astype(f32) * keep).astype(bf16)

        loop(MICRO, masked)

    SPAN_0, SPAN_1 = DILATION_BASE, 2 * DILATION_BASE
    span = DILATION_BASE * (1 + sec)
    early = 0
    if fused:
        gather_begin()
        prepare()
        early = MICRO

        def step(k):
            gather_step(k)

            @pl.when(k == F_STEP)
            def _():
                vectors()

            @pl.when(jnp.logical_and(first, jnp.logical_and(k >= F_STEP, k < F_STEP + MICRO)))
            def _():
                stage_first(k - F_STEP)

            @pl.when(jnp.logical_and(first, jnp.logical_and(k >= A_STEP, k < A_STEP + MICRO)))
            def _():
                stage_a(k - A_STEP, 2 * SPAN_0)

        loop(BLOCKS + C_LAG, step)
    else:
        for copy in own:
            copy.wait()
        for src, dst in ((v640_in, V640), (v1280_in, V1280), (vx_in, VX)):
            dst[...] = src[...]
        prepare()

    @pl.when(first)
    def _():
        def firsts(m):
            stage_first(m)
            stage_a(m, 2 * SPAN_0)

        if early == 0:
            loop(MICRO, firsts)
        loop(MICRO, lambda m: stage_b(m, SPAN_0, True))
        if fused:
            others_blocks()
        loop(MICRO, stage_n)

        def backward(m):
            stage_q(m)
            stage_p1(m, 2 * SPAN_0)

            @pl.when(jnp.logical_and(m > 0, m < MICRO - 1))
            def _():
                stage_p2(m - 1, SPAN_0, False)
                stage_p3(m - 1)

        loop(MICRO, backward)

    @pl.when(jnp.logical_not(first))
    def _():
        if fused:
            others_blocks()

        def both(k):
            @pl.when(k < MICRO)
            def _():
                stage_x(k)
                stage_first(k)
                stage_a(k, 2 * SPAN_1)

            @pl.when(jnp.logical_and(k >= 1, k <= MICRO))
            def _():
                stage_b(k - 1, SPAN_1, False)
                stage_p1(k - 1, 2 * SPAN_1)

            @pl.when(k == MICRO + 1)
            def _():
                loop(MICRO - LATE, stage_p3)

            @pl.when(k >= 2)
            def _():
                stage_p2(k - 2, SPAN_1, True)

        loop(MICRO + 2, both)

    def last_grad_hidden():
        @pl.when(first)
        def _():
            loop(LATE, lambda m: stage_p2(m + MICRO - LATE, SPAN_0, False))

    def small_gradients():
        for i in range(12):
            VS[0, i : i + 1, :] = jnp.sum(AC[i], axis=0, keepdims=True)
        VS[0, 12:16, :] = jnp.zeros((4, H), f32)

    def relay_drain():
        left(x_s.at[0], ROWS)
        halo_drain(ha_s)
        halo_drain(hg_s)
        for i in range(2):
            lines = POOL.at[pl.ds(0, 2 * ROWS), :]
            pltpu.make_async_copy(lines, lines, o_s.at[i]).wait()

    def gradient(b):
        @pl.when(b < 2)
        def _():
            TG[...] = dot(GH[...], A1[b], TN)

        @pl.when(jnp.logical_and(b >= 2, b < 4))
        def _():
            TG[...] = dot(A3[...], U[b - 2], TN)

        @pl.when(b >= 4)
        def _():
            at = pl.ds(pl.multiple_of(LEN + (b - 6) * span, 64), LEN)
            TG[...] = sum(dot(GM[m, LEN : 2 * LEN, :], A2[m, at, :], TN) for m in range(MICRO))

    if not fused:
        last_grad_hidden()
        loop(LATE, lambda m: stage_p3(m + MICRO - LATE))
        small_gradients()
        relay_drain()

        def whole(b):
            gradient(b)
            out = pltpu.make_async_copy(TG, gout.at[b], l_w.at[0])
            out.start()
            out.wait()

        loop(BLOCKS, whole)
        vout[...] = VS[0]
        return

    kind = lambda p: lax.rem(p + 2, 3)
    slot = lambda p: p // 3
    over_tensor_first = lambda p: kind(p) == 2
    zslot = lambda p: slot(p) + jnp.where(over_tensor_first(p), 3, 0)
    owned = lambda p: jnp.logical_or(over_tensor_first(p), kind(p) == y)
    block = lambda p: jnp.where(p < 7, p + 2, p - 7)
    outer = jnp.logical_or(ten == 0, ten == SHARDS - 1)
    low_side = ten < SHARDS // 2
    FAR, NEAR = jnp.where(low_side, 3, 0), jnp.where(low_side, 2, 1)

    def half_of(half):
        return pl.ds(pl.multiple_of(half * HALF, 16), HALF)

    def part(p, s):
        return CR.at[p, pl.ds(pl.multiple_of(s * HALF, 16), HALF), :]

    def kept(p, s):
        return KEEP.at[lax.rem(p, KEEP_SLOTS), s * HALF : (s + 1) * HALF, :]

    def final(p, half):
        return gout.at[block(p), half_of(half), :]

    def rc(p):
        return remote(GIVE.at[lax.rem(p, GIVE_SLOTS)], CR.at[p], rc_s.at[lax.rem(p, GIVE_SLOTS)], rc_r.at[p], at_core)

    R_Y, R_Z, R_FY, R_FC, R_OUT = range(5)

    def ry(p):
        return remote(CR.at[p], YR.at[slot(p)], r_s.at[R_Y], ry_r.at[slot(p)], at_y)

    def rz(p, s, idx, to):
        return remote(part(p, s), ZR.at[zslot(p), idx], r_s.at[R_Z], rz_r.at[zslot(p), idx], (sec, seq, to))

    def yx(p):
        return remote(part(p, ten), YX.at[slot(p)], yx_s.at[slot(p)], fy_r.at[p], at_y)

    def fy(p):
        return remote(part(p, ten), final(p, core), r_s.at[R_FY], fy_r.at[p], at_y)

    def fc(p, src):
        return remote(src, final(p, core), r_s.at[R_FC], fc_r.at[0], at_core)

    def out_g(p):
        return pltpu.make_async_copy(part(p, ten), final(p, core), r_s.at[R_OUT])

    def add(ref, *others_):
        total = ref[...].astype(f32)
        for other in others_:
            total = total + other[...].astype(f32)
        ref[...] = total.astype(bf16)

    def compute(p):
        @pl.when(p >= GIVE_SLOTS)
        def _():
            rc(p - GIVE_SLOTS).wait_send()

        gradient(block(p))
        for s in range(SHARDS):
            theirs = TG[pl.ds(pl.multiple_of(s * PART + (1 - core) * HALF, 16), HALF), :]
            GIVE[lax.rem(p, GIVE_SLOTS), s * HALF : (s + 1) * HALF, :] = theirs.astype(bf16)
        rc(p).start()
        for s in range(SHARDS):
            kept(p, s)[...] = TG[pl.ds(pl.multiple_of(s * PART + core * HALF, 16), HALF), :].astype(bf16)

    def over_core(p):
        rc(p).wait_recv()
        for s in range(SHARDS):
            add(part(p, s), kept(p, s))

        @pl.when(jnp.logical_not(owned(p)))
        def _():
            ry(p).start()

    def over_y(p):
        @pl.when(owned(p))
        def _():
            ry(p).wait_recv()
            for s in range(SHARDS):
                add(part(p, s), YR.at[slot(p), s * HALF : (s + 1) * HALF, :])

    def chain_one(p):
        @pl.when(jnp.logical_and(owned(p), outer))
        def _():
            for k in range(3):
                s = jnp.where(low_side, 3 - k, k)
                idx = jnp.where(low_side, s - 1, s)
                rz(p, s, idx, jnp.where(low_side, 1, 2)).start()

        @pl.when(jnp.logical_and(owned(p), jnp.logical_not(outer)))
        def _():
            s = jnp.where(low_side, 0, 3)
            rz(p, s, 0, s).start()

    def chain_two(p):
        @pl.when(jnp.logical_and(owned(p), jnp.logical_not(outer)))
        def _():
            for s, idx in ((FAR, jnp.where(low_side, 2, 0)), (NEAR, 1)):
                rz(p, s, idx, s).wait_recv()
                add(part(p, s), ZR.at[zslot(p), idx])
                rz(p, s, 3, s).start()

    def chain_end(p):
        @pl.when(owned(p))
        def _():
            idx, at_z = jnp.where(ten == 2, 2, 0), lax.rem(ten + 1, SHARDS)
            rz(p, ten, idx, at_z).wait_recv()
            rz(p, ten, 3, at_z).wait_recv()
            add(part(p, ten), ZR.at[zslot(p), idx], ZR.at[zslot(p), 3])

            @pl.when(over_tensor_first(p))
            def _():
                yx(p).start()

            @pl.when(jnp.logical_not(over_tensor_first(p)))
            def _():
                fy(p).start()
                fc(p, part(p, ten)).start()
                out_g(p).start()

    def settle(p):
        @pl.when(over_tensor_first(p))
        def _():
            yx(p).wait()
            add(part(p, ten), YX.at[slot(p)])
            fc(p, part(p, ten)).start()
            out_g(p).start()

        @pl.when(jnp.logical_not(owned(p)))
        def _():
            fy(p).wait_recv()
            fc(p, final(p, core)).start()

    def vector_round(i):
        pair, far = ten + 1 - 2 * lax.rem(ten, 2), lax.rem(ten + 2, SHARDS)
        where_seq = jnp.where(i == 0, y * 2 + 1 - core, jnp.where(i == 1, (1 - y) * 2 + core, seq))
        where_ten = jnp.where(i == 2, pair, jnp.where(i == 3, far, ten))
        return remote(VS.at[i], VR.at[i], vr_s.at[i], vr_r.at[i], (sec, where_seq, where_ten))

    def sums(t):
        @pl.when(t == BLOCKS - 2)
        def _():
            last_grad_hidden()

        for stage, lag, first_kind in SCHEDULE:
            p = t - lag
            fits = jnp.logical_and(p >= 0, p < BLOCKS)
            if first_kind is not None:
                fits = jnp.logical_and(fits, over_tensor_first(p) if first_kind else jnp.logical_not(over_tensor_first(p)))

            @pl.when(fits)
            def _():
                dict(compute=compute, core=over_core, y=over_y, one=chain_one, two=chain_two, end=chain_end, settle=settle)[stage](p)

        late = t - BLOCKS

        @pl.when(jnp.logical_and(late >= 0, late < LATE))
        def _():
            stage_p3(late + MICRO - LATE)

        i = late - LATE

        @pl.when(i == 0)
        def _():
            small_gradients()

        @pl.when(jnp.logical_and(i > 0, i <= 4))
        def _():
            vector_round(i - 1).wait()
            VS[i] = VS[i - 1] + VR[i - 1]

        @pl.when(jnp.logical_and(i >= 0, i < 4))
        def _():
            vector_round(i).start()

    loop(BLOCKS + LAST_LAG, sums)
    vout[...] = VS[4]

    lines = POOL.at[pl.ds(0, BLOCKS * HALF), :]
    remote(lines, lines, r_s.at[R_FC], fc_r.at[0], at_core).wait()
    relay_drain()
    gather_drain()
    loop(GIVE_SLOTS, lambda i: rc(i).wait_send())
    left(r_s.at[R_Y], 3 * SHARDS * HALF)
    left(r_s.at[R_Z], 6 * 3 * HALF)
    left(r_s.at[R_FY], 3 * HALF)
    lines = POOL.at[pl.ds(0, 6 * HALF), :]
    pltpu.make_async_copy(lines, lines, r_s.at[R_OUT]).wait()


def relay(block_input, cotangent, mask, weights, vectors, fused):
    hbm = pl.BlockSpec(memory_space=pl.ANY)
    vmem = pl.BlockSpec(memory_space=pltpu.VMEM)
    dma = lambda *shape: pltpu.SemaphoreType.DMA(shape)
    low = lambda *shape: pltpu.VMEM(shape, bf16)
    full = lambda *shape: pltpu.VMEM(shape, f32)
    scratch = [
        low(BLOCKS, H, H),
        low(2, H, H),
        low(POOL_ROWS, H),
        low(2, ROWS, H),
        low(2, ROWS, H),
        low(MICRO, 3 * LEN, H),
        low(ROWS, H),
        low(ROWS, H),
        low(ROWS, H),
        low(ROWS, H),
        low(ROWS, H),
        low(2, ROWS, H),
        low(MICRO, 3 * LEN, H),
        low(ROWS, H),
        low(ROWS, H),
        full(ROWS, 8),
        full(H, H),
        full(16, H),
        full(2, 8, H),
        full(2, 8, H),
        full(12, 8, H),
        full(5, 16, H),
        dma(2),
        dma(5),
        dma(2),
        dma(1),
        dma(MICRO),
        dma(2),
        dma(MICRO, 2),
        dma(2),
        dma(MICRO, 2),
    ]
    if fused:
        scratch += [
            full(16, 256),
            low(2 * SHARDS, 16, 256),
            low(BLOCKS, SHARDS * HALF, H),
            low(KEEP_SLOTS, SHARDS * HALF, H),
            low(GIVE_SLOTS, SHARDS * HALF, H),
            low(3, SHARDS * HALF, H),
            low(6, 4, HALF, H),
            low(3, HALF, H),
            full(4, 16, H),
            dma(7),
            dma(1),
            dma(BLOCKS, SHARDS),
            dma(BLOCKS),
            dma(2),
            dma(1),
            dma(5),
            dma(GIVE_SLOTS),
            dma(BLOCKS),
            dma(3),
            dma(6, 4),
            dma(3),
            dma(BLOCKS),
            dma(1),
            dma(4),
            dma(4),
        ]
    outs = (
        jax.ShapeDtypeStruct((MICRO, LEN, 2 * H), bf16),
        jax.ShapeDtypeStruct((MICRO, LEN, 2 * H), bf16),
        jax.ShapeDtypeStruct((BLOCKS, PART, H), bf16) if fused else jax.ShapeDtypeStruct((BLOCKS, H, H), f32),
        jax.ShapeDtypeStruct((16, H), f32),
    )
    in_specs = [hbm, hbm, vmem] + [hbm] * len(weights) + [vmem] * len(vectors)
    return pl.pallas_call(
        functools.partial(relay_kernel, fused),
        out_shape=outs,
        in_specs=in_specs,
        out_specs=(hbm, hbm, hbm, vmem),
        scratch_shapes=scratch,
        compiler_params=pltpu.CompilerParams(collective_id=0, has_side_effects=True, vmem_limit_bytes=62 * 2**20),
        cost_estimate=pl.CostEstimate(flops=25_000_000_000, bytes_accessed=20_000_000, transcendentals=4_000_000),
        name="relay",
    )(block_input, cotangent, mask, *weights, *vectors)


def unpack_kernel(bo, ig, grads, small, bo_out, ig_out, in_out, mid_out, out_out, *rest):
    vectors, (B, G, F, sems) = rest[:9], rest[9:]
    ten = lax.axis_index("tensor")
    load = pltpu.make_async_copy(grads, G, sems.at[2, 0])
    load.start()
    arrays = [(k, m, src, dst) for k, (src, dst) in enumerate(((bo, bo_out), (ig, ig_out))) for m in range(MICRO)]
    arrive = [pltpu.make_async_copy(src.at[m], B.at[k, m], sems.at[k, m]) for k, m, src, dst in arrays]
    leave = [pltpu.make_async_copy(B.at[k, m], dst.at[0, m, 0], sems.at[4 + k, m]) for k, m, src, dst in arrays]
    for copy in arrive:
        copy.start()
    for z in range(SHARDS):

        @pl.when(ten == z)
        def _():
            for row, ref in zip((0, 1, 2, 3, 4, 5), vectors[:6]):
                ref[...] = small[row : row + 1, z * PART : (z + 1) * PART]
            for i, ref in enumerate(vectors[6:]):
                row, at = 6 + 2 * i + z // 2, z % 2 * 2 * PART
                ref[...] = small[row : row + 1, at : at + 2 * PART]

    load.wait()
    F[...] = G[...].astype(f32)
    outs = [pltpu.make_async_copy(F.at[h + 2 * k], ref.at[:, pl.ds(h * H, H)], sems.at[3, 2 * k + h]) for k, ref in enumerate((in_out, out_out)) for h in range(2)]
    outs += [pltpu.make_async_copy(F.at[pl.ds(4, 5)], mid_out, sems.at[2, 1])]
    for out in outs:
        out.start()
    for came, copy in zip(arrive, leave):
        came.wait()
        copy.start()
    for copy in leave + outs:
        copy.wait()


def unpacked(block_out, input_grad, grads, small):
    hbm, vmem = pl.BlockSpec(memory_space=pl.ANY), pl.BlockSpec(memory_space=pltpu.VMEM)
    like = lambda *shape: jax.ShapeDtypeStruct(shape, f32)
    rows_like = jax.ShapeDtypeStruct((1, MICRO, 1, LEN, 2 * H), bf16)
    (block_out, input_grad, grad_in, grad_mid, grad_out, *vectors) = pl.pallas_call(
        unpack_kernel,
        out_shape=[rows_like, rows_like, like(PART, 2 * H), like(5, PART, H), like(PART, 2 * H)] + [like(1, PART)] * 6 + [like(1, 2 * PART)] * 3,
        in_specs=[hbm, hbm, hbm, vmem],
        out_specs=[hbm] * 5 + [vmem] * 9,
        scratch_shapes=[pltpu.VMEM((2, MICRO, LEN, 2 * H), bf16), pltpu.VMEM((BLOCKS, PART, H), bf16), pltpu.VMEM((BLOCKS, PART, H), f32), pltpu.SemaphoreType.DMA((6, MICRO))],
        compiler_params=pltpu.CompilerParams(vmem_limit_bytes=62 * 2**20),
        name="unpack",
    )(block_out, input_grad, grads, small)
    (bias_in, bias_mid, gain_second, shift_second, gain_third, shift_third, bias_out, gain_first, shift_first) = vectors
    return (
        block_out,
        input_grad,
        grad_in.T[None],
        bias_in,
        grad_mid.transpose(0, 2, 1)[None],
        bias_mid,
        grad_out[None],
        bias_out,
        gain_first,
        shift_first,
        gain_second,
        shift_second,
        gain_third,
        shift_third,
    )


def packed_weights(conv_in, conv_mid, conv_out):
    channels = conv_out.shape[0]
    halves = lambda m: m.reshape(channels, 2, H).transpose(1, 0, 2)
    return jnp.concatenate([halves(conv_in.T), halves(conv_out), conv_mid.transpose(0, 2, 1)])


def local(*args):
    block_input, cotangent, mask = args[:3]
    (conv_in, bias_in, conv_mid, bias_mid, conv_out, bias_out, gain_first, shift_first, gain_second, shift_second, gain_third, shift_third) = (a[0] for a in args[3:])
    ten, sec = lax.axis_index("tensor"), lax.axis_index("section")
    shards = lax.axis_size("tensor")
    fused = shards == SHARDS
    channels = conv_out.shape[0]
    narrow = (bias_in, bias_mid, gain_second, shift_second, gain_third, shift_third)
    wide = (bias_out, gain_first, shift_first)
    if fused:
        weights = (conv_in.T, conv_mid.transpose(0, 2, 1), conv_out)
        block_out, input_grad, grads, small = relay(block_input, cotangent, mask, weights, tuple(v[None] for v in narrow + wide), True)
        return unpacked(block_out, input_grad, grads, small)
    else:
        mine = packed_weights(conv_in, conv_mid, conv_out)
        whole = lax.all_gather(mine, "tensor", axis=1, tiled=True)
        swap = [(0, 1), (1, 0)]
        give = jnp.where(sec == 0, whole[2:4], whole[0:2])
        other = lax.ppermute(give, "section", swap)
        v_narrow = lax.all_gather(jnp.stack(narrow), "tensor", axis=1, tiled=True)
        v_wide = lax.all_gather(jnp.stack(wide), "tensor", axis=1, tiled=True)
        v640 = jnp.pad(v_narrow.astype(f32), ((0, 10), (0, 0)))
        v1280 = jnp.pad(v_wide.astype(f32).reshape(3, 2, H).transpose(1, 0, 2), ((0, 0), (0, 5), (0, 0)))
        vx = lax.ppermute(v1280, "section", swap)
        block_out, input_grad, grads, small = relay(block_input, cotangent, mask, (whole, other), (v640, v1280, vx), False)
        grads = lax.psum(lax.psum_scatter(grads, "tensor", scatter_dimension=1, tiled=True), "seq")
        small = lax.psum(small, ("seq", "tensor"))
    grad_in = grads[0:2].transpose(0, 2, 1).reshape(2 * H, channels)
    grad_out = grads[2:4].transpose(1, 0, 2).reshape(channels, 2 * H)
    grad_mid = grads[4:9].transpose(0, 2, 1)
    thin = lax.dynamic_slice_in_dim(small[0:6], ten * channels, channels, 1)
    thick = lax.dynamic_slice_in_dim(small[6:12].reshape(3, 2 * H), ten * 2 * channels, 2 * channels, 1)
    shape = (1, MICRO, 1, LEN, 2 * H)
    return (
        block_out.reshape(shape),
        input_grad.reshape(shape),
        grad_in[None],
        thin[0:1],
        grad_mid[None],
        thin[1:2],
        grad_out[None],
        thick[0:1],
        thick[1:2],
        thick[2:3],
        thin[2:3],
        thin[3:4],
        thin[4:5],
        thin[5:6],
    )


def solution(mesh):
    in_specs = (
        P(None, "tensor", "seq", None),
        P(None, "tensor", "seq", None),
        P(None, "tensor", "seq"),
        P("section", None, "tensor"),
        P("section", "tensor"),
        P("section", None, None, "tensor"),
        P("section", "tensor"),
        P("section", "tensor", None),
        P("section", "tensor"),
        P("section", "tensor"),
        P("section", "tensor"),
        P("section", "tensor"),
        P("section", "tensor"),
        P("section", "tensor"),
        P("section", "tensor"),
    )
    out_specs = (
        P("section", None, "tensor", "seq", None),
        P("section", None, "tensor", "seq", None),
        P("section", None, "tensor"),
        P("section", "tensor"),
        P("section", None, None, "tensor"),
        P("section", "tensor"),
        P("section", "tensor", None),
        P("section", "tensor"),
        P("section", "tensor"),
        P("section", "tensor"),
        P("section", "tensor"),
        P("section", "tensor"),
        P("section", "tensor"),
        P("section", "tensor"),
    )
    return jax.shard_map(local, mesh=mesh, in_specs=in_specs, out_specs=out_specs, check_vma=False)
```

```python
import functools

import jax
import jax.numpy as jnp
from jax import lax
from jax.experimental import pallas as pl
from jax.experimental.pallas import tpu as pltpu
from jax.sharding import PartitionSpec as P

DILATION_BASE = 64
EPS = 1e-05
ROOT_HALF = 0.7071067811865476
INVERSE_ROOT_TWO_PI = 0.3989422804014327
MESH = pl.DeviceIdType.MESH
f32 = jnp.float32
bf16 = jnp.bfloat16

MICRO = 4
LEN = 256
H = 640
ROWS = MICRO * LEN
SHARDS = 4
PART = H // SHARDS
HALF = PART // 2
BLOCKS = 9
LAST = BLOCKS - 1
GUEST, GUEST_TURN = BLOCKS, 3
TILE = 256
WIDE = 128
Y_LAG, C_LAG = 1, 6
X_STEP = 9
F_STEP = 2
A_STEP = C_LAG + 1
LEAD = 3
NN = (((1,), (0,)), ((), ()))
NT = (((1,), (1,)), ((), ()))
TN = (((0,), (0,)), ((), ()))

E_AT, SX_AT, LV_AT, POOL_ROWS = 0, 2 * ROWS, 4 * ROWS, 6 * ROWS
KEEP_SLOTS, GIVE_SLOTS = 3, 3
SCHEDULE = (
    ("two", 6, False),
    ("compute", 0, None),
    ("settle", 12, True),
    ("core", 1, None),
    ("end", 8, True),
    ("settle", 12, False),
    ("two", 3, True),
    ("one", 1, True),
    ("end", 8, False),
    ("y", 4, False),
    ("one", 4, False),
)
LAST_LAG = 12
LATE_P2, LATE_P3 = 2, 3


def dot(a, b, dims):
    return lax.dot_general(a, b, dims, preferred_element_type=f32)


def loop(count, body):
    def step(i, carry):
        body(i)
        return carry

    lax.fori_loop(0, count, step, 0)


def unroll(count, body):
    for i in range(count):
        body(i)


def row_stats(parts, width):
    mean = sum(jnp.sum(x, axis=-1, keepdims=True) for x in parts) / width
    spread = sum(jnp.sum(x * x, axis=-1, keepdims=True) for x in parts) / width - mean * mean
    return mean, lax.rsqrt(spread + EPS)


def gelu_slope(v):
    phi = 0.5 * (1.0 + lax.erf(v * ROOT_HALF))
    return phi, phi + v * (jnp.exp(-0.5 * v * v) * INVERSE_ROOT_TWO_PI)


def norm_back(ys, normeds, inverse, gains, width):
    scaled = [y * g for y, g in zip(ys, gains)]
    total = sum(jnp.sum(s, axis=-1, keepdims=True) for s in scaled) / width
    along = sum(jnp.sum(s * n, axis=-1, keepdims=True) for s, n in zip(scaled, normeds)) / width
    return [inverse * (s - total - n * along) for s, n in zip(scaled, normeds)]


def eights(x):
    return jnp.sum(x.reshape(x.shape[0] // 8, 8, x.shape[1]), axis=0)


def relay_kernel(fused, *refs):
    if fused:
        (xin, cot, mask, w_in, w_mid, w_out) = refs[:6]
        narrow_in, wide_in = refs[6:12], refs[12:15]
        (bo, ig, gout, vout) = refs[15:19]
        rest = refs[19:]
    else:
        (xin, cot, mask, wfull, wother, v640_in, v1280_in, vx_in, bo, ig, gout, vout) = refs[:12]
        rest = refs[12:]
    (W, WX, POOL, A1, S1, A2, S2, N2, A3, S3, N3, U, GM, GH, XR, ST, TG, V640, V1280, VX, AC, VS) = rest[:22]
    (l_in, l_w, o_s, x_s, x_r, ha_s, ha_r, hg_s, hg_r) = rest[22:31]
    if fused:
        (VF, VG, CR, KEEP, GIVE, YR, ZR, YX, VR, g_s, gg_r, vg_r, ga_r, gc_r, wx_r, wc_r, r_s, rc_s, rc_r, ry_r, rz_r, yx_s, fy_r, fc_r, vr_s, vr_r) = rest[31:]

    sec = lax.axis_index("section")
    seq = lax.axis_index("seq")
    ten = lax.axis_index("tensor")
    y = seq // 2
    core = lax.rem(seq, 2)
    at_core = (sec, y * 2 + (1 - core), ten)
    at_y = (sec, (1 - y) * 2 + core, ten)
    at_diag = (sec, (1 - y) * 2 + (1 - core), ten)
    at_x = (1 - sec, seq, ten)
    up, down = (sec, seq, ten + 1), (sec, seq, ten - 1)
    behind, ahead = (sec, seq - 1, ten), (sec, seq + 1, ten)
    first = sec == 0

    def remote(src, dst, send, recv, where):
        return pltpu.make_async_remote_copy(src_ref=src, dst_ref=dst, send_sem=send, recv_sem=recv, device_id=where, device_id_type=MESH)

    def left(send, count, width=None):
        lines = VG.at[pl.ds(0, count)] if width else POOL.at[pl.ds(0, count), :]
        remote(lines, lines, send, x_r.at[0], at_x).wait_send()

    def rows(base, m, r=0, n=LEN):
        return pl.ds(pl.multiple_of(base + m * LEN + r, 16), n)

    def load_in(m, h, ref, into, sem):
        pltpu.make_async_copy(ref.at[m, 0, :, pl.ds(h * H, H)], into, sem).start()

    def loaded(into, sem):
        pltpu.make_async_copy(into, into, sem).wait()

    if fused:
        own_rows = pl.ds(pl.multiple_of(ten * PART, 16), PART)
        own = [pltpu.make_async_copy(w_in.at[:, pl.ds(h * H, H)], W.at[h, own_rows, :], l_w.at[h]) for h in range(2)]
        own += [pltpu.make_async_copy(w_out.at[:, pl.ds(h * H, H)], W.at[2 + h, own_rows, :], l_w.at[2 + h]) for h in range(2)]
        own += [pltpu.make_async_copy(w_mid, W.at[pl.ds(4, 5), own_rows, :], l_w.at[4])]
        partners = [at_core, at_y, at_diag]
        others = [(s, d) for s in range(2) for d in range(SHARDS) if s or d]
        partners += [(lax.rem(sec + s, 2), seq, lax.rem(ten + d, SHARDS)) for s, d in others]
    else:
        own = [pltpu.make_async_copy(wfull, W, l_w.at[0]), pltpu.make_async_copy(wother, WX, l_w.at[1])]
        partners = [at_core, at_diag, at_x]
    for copy in own:
        copy.start()
    for m in range(MICRO):
        for h in range(2):
            load_in(m, h, xin, POOL.at[pl.ds(E_AT + h * ROWS + m * LEN, LEN), :], l_in.at[0])
            load_in(m, h, cot, U.at[h, pl.ds(m * LEN, LEN), :], l_in.at[1])

    if fused:
        VF[...] = jnp.zeros_like(VF)
        for i, ref in enumerate(narrow_in):
            VF[i : i + 1, 0:PART] = ref[...].astype(f32)
        for i, ref in enumerate(wide_in):
            for half in range(2):
                VF[6 + 3 * half + i : 7 + 3 * half + i, 0:PART] = ref[:, half * PART : (half + 1) * PART].astype(f32)
        VG[sec * SHARDS + ten] = VF[...].astype(bf16)

    barrier = pltpu.get_barrier_semaphore()
    for partner in partners:
        pl.semaphore_signal(barrier, inc=1, device_id=partner, device_id_type=MESH)
    pl.semaphore_wait(barrier, len(partners))

    def piece(ref, b, s, half):
        return ref.at[b, pl.ds(pl.multiple_of(s * PART + half * HALF, 16), HALF), :]

    UP, DOWN, Y_, CORE_, X_, XC_, V_, G_ = range(8)

    def gz(b, s, to_up):
        spot = piece(W, b, s, core)
        return remote(spot, spot, g_s.at[UP if to_up else DOWN], ga_r.at[b, s], up if to_up else down)

    def gy(b, s):
        spot = piece(W, b, s, core)
        return remote(spot, spot, g_s.at[Y_], ga_r.at[b, s], at_y)

    def gc(b, s):
        spot = piece(W, b, s, core)
        return remote(spot, spot, g_s.at[CORE_], gc_r.at[b], at_core)

    def gc_here(b):
        lines = W.at[b, pl.ds(0, (SHARDS - 1) * HALF), :]
        remote(lines, lines, g_s.at[CORE_], gc_r.at[b], at_core).wait_recv()

    def wanted(b):
        return b // 2 == 1 - sec

    def gx(b, s):
        k = lax.rem(b, 2)
        return remote(piece(W, b, s, core), piece(WX, k, s, core), g_s.at[X_], wx_r.at[k], at_x)

    def gx_here(k):
        lines = WX.at[k, pl.ds(0, SHARDS * HALF), :]
        remote(lines, lines, g_s.at[X_], wx_r.at[k], at_x).wait_recv()

    def gxc(k, s):
        spot = piece(WX, k, s, core)
        return remote(spot, spot, g_s.at[XC_], wc_r.at[0], at_core)

    def gv(i):
        s, d = others[i]
        return remote(VG.at[sec * SHARDS + ten], VG.at[sec * SHARDS + ten], g_s.at[V_], vg_r.at[0], (lax.rem(sec + s, 2), seq, lax.rem(ten + d, SHARDS)))

    def gg(s):
        return remote(piece(W, jnp.where(first, LAST, GUEST), s, core), piece(W, jnp.where(first, GUEST, LAST), s, core), g_s.at[G_], gg_r.at[s], at_x)

    def turn(j):
        return jnp.where(first, j, jnp.where(j < GUEST_TURN, j, jnp.where(j == GUEST_TURN, GUEST, j - 1)))

    turns = jnp.where(first, BLOCKS, BLOCKS + 1)
    mine = lambda b: jnp.where(b < LAST, lax.rem(b, 2) == y, jnp.logical_not(first))
    def send_own(j):
        b = turn(j)

        @pl.when(b == GUEST)
        def _():
            gg(ten).wait_recv()

        @pl.when(jnp.logical_and(mine(b), ten < SHARDS - 1))
        def _():
            gz(b, ten, True).start()

        @pl.when(jnp.logical_and(mine(b), ten > 0))
        def _():
            gz(b, ten, False).start()

        @pl.when(wanted(b))
        def _():
            gx(b, ten).start()

    def gather_begin():
        for j in range(2):
            own[j].wait()
            send_own(j)
        for copy in own[2:]:
            copy.wait()

        @pl.when(first)
        def _():
            gg(ten).start()

        for i in range(len(others)):
            gv(i).start()
        for j in range(2, LEAD):
            send_own(j)

    def gather_step(k):
        @pl.when(k + LEAD < turns)
        def _():
            send_own(k + LEAD)

        for d in range(1, SHARDS):
            j = k - (d - 1)
            b = turn(j)
            ok = jnp.logical_and(j >= 0, j < turns)
            for above in (False, True):
                s = ten + d if above else ten - d
                there = jnp.logical_and(ok, s < SHARDS if above else s >= 0)
                onward = (ten > 0) if above else (ten < SHARDS - 1)

                @pl.when(jnp.logical_and(there, mine(b)))
                def _():
                    gz(b, s, True).wait_recv()

                    @pl.when(onward)
                    def _():
                        gz(b, s, not above).start()

                    @pl.when(b < LAST)
                    def _():
                        gy(b, s).start()

                    @pl.when(b < GUEST)
                    def _():
                        gc(b, s).start()

                    @pl.when(b == GUEST)
                    def _():
                        gg(s).start()

                    @pl.when(wanted(b))
                    def _():
                        gx(b, s).start()

        for d in range(1, SHARDS):
            j = k - d - Y_LAG
            b = turn(j)
            ok = jnp.logical_and(j >= 0, j < turns)
            for above in (False, True):
                s = ten + d if above else ten - d
                there = jnp.logical_and(ok, s < SHARDS if above else s >= 0)

                @pl.when(jnp.logical_and(there, jnp.logical_not(mine(b))))
                def _():
                    @pl.when(b < LAST)
                    def _():
                        gy(b, s).wait_recv()

                    @pl.when(b == LAST)
                    def _():
                        gg(s).wait_recv()

                    gc(b, s).start()

                    @pl.when(wanted(b))
                    def _():
                        gx(b, s).start()

        j = k - C_LAG
        b = turn(j)

        @pl.when(jnp.logical_and(jnp.logical_and(j >= 0, j < turns), b < GUEST))
        def _():
            gc_here(b)

        @pl.when(jnp.logical_and(k >= X_STEP, k < X_STEP + 2))
        def _():
            gx_here(k - X_STEP)
            for s in range(SHARDS):
                gxc(k - X_STEP, s).start()

    def others_blocks():
        lines = POOL.at[pl.ds(0, 2 * SHARDS * HALF), :]
        remote(lines, lines, g_s.at[XC_], wc_r.at[0], at_core).wait_recv()

    def gather_drain():
        left(g_s.at[V_], len(others), True)
        left(g_s.at[Y_], 4 * (SHARDS - 1) * HALF)
        left(g_s.at[CORE_], BLOCKS * (SHARDS - 1) * HALF)
        left(g_s.at[X_], 2 * SHARDS * HALF)
        left(g_s.at[XC_], 2 * SHARDS * HALF)
        for who, count, pieces in ((0, 4, 1), (1, 6, SHARDS - 1)):

            @pl.when(sec == who)
            def _():
                left(g_s.at[G_], pieces * HALF)

            for z in range(SHARDS):

                @pl.when(jnp.logical_and(sec == who, ten == z))
                def _():
                    if z < SHARDS - 1:
                        left(g_s.at[UP], count * (z + 1) * HALF)
                    if z > 0:
                        left(g_s.at[DOWN], count * (SHARDS - z) * HALF)

    def vectors():
        lines = VG.at[pl.ds(0, len(others))]
        remote(lines, lines, g_s.at[V_], vg_r.at[0], at_x).wait_recv()
        line = lax.broadcasted_iota(jnp.int32, (2 * 128, H), 0)
        col = lax.broadcasted_iota(jnp.int32, (2 * 128, H), 1)

        def pick(offset):
            return jnp.where(col == line + offset, 1.0, 0.0).astype(bf16)

        narrow = jnp.zeros((16, H), f32)
        wide = [[jnp.zeros((16, H), f32) for _ in range(4)] for _ in range(2)]
        for s in range(SHARDS):
            inner = pick(s * PART)
            narrow = narrow + dot(VG[sec * SHARDS + s], inner, NN)
            for who in range(2):
                held = VG[(sec if who == 0 else 1 - sec) * SHARDS + s]
                for h in range(2):
                    for k in range(2):
                        put = pick(s * 2 * PART + k * PART - h * H)
                        wide[who][h * 2 + k] = wide[who][h * 2 + k] + dot(held, put, NN)
        V640[...] = narrow
        for who, into in ((0, V1280), (1, VX)):
            for h in range(2):
                into[h, 0:3, :] = wide[who][h * 2][6:9] + wide[who][h * 2 + 1][9:12]

    def halo(ref, sends, recvs, m, reach, start):
        fwd = remote(ref.at[m, pl.ds(2 * LEN - reach, reach), :], ref.at[m, pl.ds(LEN - reach, reach), :], sends.at[0], recvs.at[m, 0], ahead)
        bwd = remote(ref.at[m, pl.ds(LEN, reach), :], ref.at[m, pl.ds(2 * LEN, reach), :], sends.at[1], recvs.at[m, 1], behind)

        @pl.when(seq < 3)
        def _():
            fwd.start() if start else bwd.wait_recv()

        @pl.when(seq > 0)
        def _():
            bwd.start() if start else fwd.wait_recv()

    def halo_drain(sends):
        for s, reach in ((0, 2 * SPAN_0), (1, 2 * SPAN_1)):

            @pl.when(jnp.logical_and(sec == s, seq < 3))
            def _():
                left(sends.at[0], MICRO * reach)

            @pl.when(jnp.logical_and(sec == s, seq > 0))
            def _():
                left(sends.at[1], MICRO * reach)

    def x_send(m, src):
        return remote(src.at[rows(0, m), :], XR.at[rows(0, m), :], x_s.at[0], x_r.at[m], at_x)

    def stage_first(m):
        def tile(i):
            r = i * WIDE
            at = rows(0, m, r, WIDE)
            x = [POOL[rows(E_AT + h * ROWS, m, r, WIDE), :].astype(f32) for h in range(2)]
            mean, inverse = row_stats(x, 2 * H)
            ST[at, 0:1] = mean
            ST[at, 1:2] = inverse
            for h in range(2):
                v = (x[h] - mean) * inverse * V1280[h, 1:2, :] + V1280[h, 2:3, :]
                phi, slope = gelu_slope(v)
                A1[h, at, :] = (v * phi).astype(bf16)
                S1[h, at, :] = slope.astype(bf16)

        unroll(LEN // WIDE, tile)

    def stage_a(m, reach):
        here = rows(0, m)
        TG[0:LEN, :] = dot(A1[0, here, :], W[0], NT) + dot(A1[1, here, :], W[1], NT)

        def tile2(i):
            r = i * TILE
            at = rows(0, m, r, TILE)
            x = TG[pl.ds(r, TILE), :] + V640[0:1, :]
            mean, inverse = row_stats([x], H)
            normed = (x - mean) * inverse
            v = normed * V640[2:3, :] + V640[3:4, :]
            phi, slope = gelu_slope(v)
            A2[m, pl.ds(pl.multiple_of(LEN + r, 16), TILE), :] = (v * phi).astype(bf16)
            S2[at, :] = slope.astype(bf16)
            N2[at, :] = normed.astype(bf16)
            ST[at, 2:3] = inverse

        unroll(LEN // TILE, tile2)
        halo(A2, ha_s, ha_r, m, reach, True)

    def stage_b(m, span):
        halo(A2, ha_s, ha_r, m, 2 * span, False)
        taps = [A2[m, pl.ds(LEN + (t - 2) * span, LEN), :] for t in range(5)]
        TG[0:LEN, :] = dot(jnp.concatenate(taps, axis=1), jnp.concatenate([W[4 + t] for t in range(5)], axis=1), NT)

        def tile(i):
            r = i * TILE
            at = rows(0, m, r, TILE)
            x = TG[pl.ds(r, TILE), :] + V640[1:2, :]
            mean, inverse = row_stats([x], H)
            normed = (x - mean) * inverse
            v = normed * V640[4:5, :] + V640[5:6, :]
            phi, slope = gelu_slope(v)
            A3[at, :] = (v * phi).astype(bf16)
            S3[at, :] = slope.astype(bf16)
            N3[at, :] = normed.astype(bf16)
            ST[at, 3:4] = inverse

        unroll(LEN // TILE, tile)

    def stage_out(m):
        here = rows(0, m)
        for h in range(2):
            mixed = dot(A3[here, :], W[2 + h], NN) + V1280[h, 0:1, :]
            POOL[rows(LV_AT + h * ROWS, m), :] = (POOL[rows(E_AT + h * ROWS, m), :].astype(f32) + mixed).astype(bf16)
            out_bo(m, h).start()

    def out_bo(m, h):
        return pltpu.make_async_copy(POOL.at[rows(LV_AT + h * ROWS, m), :], bo.at[m, :, pl.ds(h * H, H)], o_s.at[0])

    def out_ig(m, h):
        return pltpu.make_async_copy(S1.at[h, rows(0, m), :], ig.at[m, :, pl.ds(h * H, H)], o_s.at[1])

    def stage_x(m):
        x_send(m, A3).wait_recv()
        for h in range(2):
            at = rows(E_AT + h * ROWS, m)
            mixed = dot(XR[rows(0, m), :], WX[h], NN) + VX[h, 0:1, :]
            POOL[at, :] = (POOL[at, :].astype(f32) + mixed).astype(bf16)

    def stage_n(m):
        def tile(i):
            r = i * WIDE
            at = rows(0, m, r, WIDE)
            x = [POOL[rows(LV_AT + h * ROWS, m, r, WIDE), :].astype(f32) for h in range(2)]
            mean, inverse = row_stats(x, 2 * H)
            ST[at, 4:5] = mean
            ST[at, 5:6] = inverse
            for h in range(2):
                v = (x[h] - mean) * inverse * VX[h, 1:2, :] + VX[h, 2:3, :]
                POOL[rows(SX_AT + h * ROWS, m, r, WIDE), :] = gelu_slope(v)[1].astype(bf16)

        unroll(LEN // WIDE, tile)

    def stage_q(m):
        x_send(m, GH).wait_recv()
        for h in range(2):
            TG[h * LEN : (h + 1) * LEN, :] = dot(XR[rows(0, m), :], WX[h], NN)

        def tile(i):
            r = i * WIDE
            at = rows(0, m, r, WIDE)
            mean, inverse = ST[at, 4:5], ST[at, 5:6]
            ys, normeds = [], []
            for h in range(2):
                slope = POOL[rows(SX_AT + h * ROWS, m, r, WIDE), :].astype(f32)
                ys.append(TG[pl.ds(h * LEN + r, WIDE), :] * slope)
                normeds.append((POOL[rows(LV_AT + h * ROWS, m, r, WIDE), :].astype(f32) - mean) * inverse)
            grads = norm_back(ys, normeds, inverse, [VX[h, 1:2, :] for h in range(2)], 2 * H)
            for h in range(2):
                U[h, at, :] = (U[h, at, :].astype(f32) + grads[h]).astype(bf16)

        unroll(LEN // WIDE, tile)

    def back_three(m):
        here = rows(0, m)
        return dot(U[0, here, :], W[2], NT) + dot(U[1, here, :], W[3], NT)

    def stage_back_three(m):
        full_ = back_three(m)
        high = full_.astype(bf16)
        POOL[rows(SX_AT, m), :] = high
        POOL[rows(SX_AT + ROWS, m), :] = (full_ - high.astype(f32)).astype(bf16)

    def stage_p1(m, reach, kept_):
        if kept_:
            back = POOL[rows(SX_AT, m), :].astype(f32) + POOL[rows(SX_AT + ROWS, m), :].astype(f32)
        else:
            back = back_three(m)
        at = rows(0, m)
        y_ = back * S3[at, :].astype(f32)
        normed = N3[at, :].astype(f32)
        (grad,) = norm_back([y_], [normed], ST[at, 3:4], [V640[4:5, :]], H)
        low = grad.astype(bf16)
        GM[m, LEN : 2 * LEN, :] = low
        halo(GM, hg_s, hg_r, m, reach, True)
        AC[4] += eights(y_ * normed)
        AC[5] += eights(y_)
        AC[1] += eights(low.astype(f32))

    def stage_p2(m, span, relay):
        halo(GM, hg_s, hg_r, m, 2 * span, False)
        taps = [GM[m, pl.ds(LEN - (t - 2) * span, LEN), :] for t in range(5)]
        TG[0:LEN, :] = dot(jnp.concatenate(taps, axis=1), jnp.concatenate([W[4 + t] for t in range(5)]), NN)

        def tile(i):
            r = i * TILE
            at = rows(0, m, r, TILE)
            y_ = TG[pl.ds(r, TILE), :] * S2[at, :].astype(f32)
            normed = N2[at, :].astype(f32)
            (grad,) = norm_back([y_], [normed], ST[at, 2:3], [V640[2:3, :]], H)
            low = grad.astype(bf16)
            GH[at, :] = low
            AC[2] += eights(y_ * normed)
            AC[3] += eights(y_)
            AC[0] += eights(low.astype(f32))

        unroll(LEN // TILE, tile)
        if relay:
            x_send(m, GH).start()

    def stage_p3(m):
        for h in range(2):
            TG[h * LEN : (h + 1) * LEN, :] = dot(GH[rows(0, m), :], W[h], NN)

        def tile(i):
            r = i * WIDE
            at = rows(0, m, r, WIDE)
            mean, inverse = ST[at, 0:1], ST[at, 1:2]
            ys, normeds = [], []
            for h in range(2):
                ys.append(TG[pl.ds(h * LEN + r, WIDE), :] * S1[h, at, :].astype(f32))
                normeds.append((POOL[rows(E_AT + h * ROWS, m, r, WIDE), :].astype(f32) - mean) * inverse)
            grads = norm_back(ys, normeds, inverse, [V1280[h, 1:2, :] for h in range(2)], 2 * H)
            for h in range(2):
                S1[h, at, :] = (U[h, at, :].astype(f32) + grads[h]).astype(bf16)
                AC[6 + h] += eights(U[h, at, :].astype(f32))
                AC[8 + h] += eights(ys[h] * normeds[h])
                AC[10 + h] += eights(ys[h])

        unroll(LEN // WIDE, tile)
        for h in range(2):
            out_ig(m, h).start()

    def prepare():
        AC[...] = jnp.zeros_like(AC)
        for ref in (A2, GM):

            @pl.when(seq == 0)
            def _():
                for m in range(MICRO):
                    ref[m, 0:LEN, :] = jnp.zeros((LEN, H), bf16)

            @pl.when(seq == 3)
            def _():
                for m in range(MICRO):
                    ref[m, 2 * LEN : 3 * LEN, :] = jnp.zeros((LEN, H), bf16)

        for m in range(MICRO):
            ST[m * LEN : (m + 1) * LEN, 6:7] = jnp.transpose(jnp.broadcast_to(mask[m].astype(f32), (128, LEN)))[:, 0:1]
        loaded(POOL.at[pl.ds(E_AT, 2 * ROWS), :], l_in.at[0])
        loaded(U, l_in.at[1])

        def masked(m):
            at = rows(0, m)
            keep = ST[at, 6:7]
            for h in range(2):
                U[h, at, :] = (U[h, at, :].astype(f32) * keep).astype(bf16)

        loop(MICRO, masked)

    SPAN_0, SPAN_1 = DILATION_BASE, 2 * DILATION_BASE
    span = DILATION_BASE * (1 + sec)
    early = 0
    if fused:
        gather_begin()
        prepare()
        early = MICRO

        def step(k):
            gather_step(k)

            @pl.when(k == F_STEP)
            def _():
                vectors()

            @pl.when(jnp.logical_and(first, jnp.logical_and(k >= F_STEP, k < F_STEP + MICRO)))
            def _():
                stage_first(k - F_STEP)

            @pl.when(jnp.logical_and(first, jnp.logical_and(k >= A_STEP, k < A_STEP + MICRO)))
            def _():
                stage_a(k - A_STEP, 2 * SPAN_0)

        loop(BLOCKS + 1 + C_LAG, step)
    else:
        for copy in own:
            copy.wait()
        for src, dst in ((v640_in, V640), (v1280_in, V1280), (vx_in, VX)):
            dst[...] = src[...]
        prepare()

    @pl.when(first)
    def _():
        def firsts(m):
            stage_first(m)
            stage_a(m, 2 * SPAN_0)

        if early == 0:
            loop(MICRO, firsts)

        def leave(m):
            stage_b(m, SPAN_0)
            x_send(m, A3).start()
            stage_out(m)

        loop(MICRO, leave)
        if fused:
            others_blocks()
        loop(MICRO, stage_n)

        def backward(m):
            stage_q(m)
            stage_p1(m, 2 * SPAN_0, False)

            @pl.when(m < MICRO - LATE_P2)
            def _():
                stage_p2(m, SPAN_0, False)

            @pl.when(m < MICRO - LATE_P3)
            def _():
                stage_p3(m)

        loop(MICRO, backward)

    @pl.when(jnp.logical_not(first))
    def _():
        if fused:
            others_blocks()
        loop(MICRO, stage_back_three)

        def both(k):
            @pl.when(k < MICRO)
            def _():
                stage_x(k)
                stage_first(k)
                stage_a(k, 2 * SPAN_1)

            @pl.when(jnp.logical_and(k >= 1, k <= MICRO))
            def _():
                stage_b(k - 1, SPAN_1)
                stage_p1(k - 1, 2 * SPAN_1, True)

            @pl.when(k == MICRO + 1)
            def _():
                loop(MICRO - LATE_P3, stage_p3)

            @pl.when(k >= 2)
            def _():
                stage_p2(k - 2, SPAN_1, True)

        loop(MICRO + 2, both)

    def last_grad_hidden():
        @pl.when(first)
        def _():
            loop(LATE_P2, lambda m: stage_p2(m + MICRO - LATE_P2, SPAN_0, False))

    def small_gradients():
        for i in range(12):
            VS[0, i : i + 1, :] = jnp.sum(AC[i], axis=0, keepdims=True)
        VS[0, 12:16, :] = jnp.zeros((4, H), f32)

    def relay_drain():
        left(x_s.at[0], ROWS)
        halo_drain(ha_s)
        halo_drain(hg_s)
        for i in range(2):
            lines = POOL.at[pl.ds(0, 2 * ROWS), :]
            pltpu.make_async_copy(lines, lines, o_s.at[i]).wait()

    def gradient(b):
        @pl.when(b < 2)
        def _():
            TG[...] = dot(GH[...], A1[b], TN)

        @pl.when(jnp.logical_and(b >= 2, b < 4))
        def _():
            TG[...] = dot(A3[...], U[b - 2], TN)

        @pl.when(b >= 4)
        def _():
            at = pl.ds(pl.multiple_of(LEN + (b - 6) * span, 64), LEN)
            TG[...] = dot(jnp.concatenate([GM[m, LEN : 2 * LEN, :] for m in range(MICRO)]), jnp.concatenate([A2[m, at, :] for m in range(MICRO)]), TN)

    if not fused:
        last_grad_hidden()
        loop(LATE_P3, lambda m: stage_p3(m + MICRO - LATE_P3))

        @pl.when(jnp.logical_not(first))
        def _():
            loop(MICRO, stage_out)

        small_gradients()
        relay_drain()

        def whole(b):
            gradient(b)
            out = pltpu.make_async_copy(TG, gout.at[b], l_w.at[0])
            out.start()
            out.wait()

        loop(BLOCKS, whole)
        vout[...] = VS[0]
        return

    kind = lambda p: lax.rem(p + 2, 3)
    slot = lambda p: p // 3
    over_tensor_first = lambda p: kind(p) == 2
    zslot = lambda p: slot(p) + jnp.where(over_tensor_first(p), 3, 0)
    owned = lambda p: jnp.logical_or(over_tensor_first(p), kind(p) == y)
    block = lambda p: jnp.where(p < 7, p + 2, p - 7)
    outer = jnp.logical_or(ten == 0, ten == SHARDS - 1)
    low_side = ten < SHARDS // 2
    FAR, NEAR = jnp.where(low_side, 3, 0), jnp.where(low_side, 2, 1)

    def half_of(half):
        return pl.ds(pl.multiple_of(half * HALF, 16), HALF)

    def part(p, s):
        return CR.at[p, pl.ds(pl.multiple_of(s * HALF, 16), HALF), :]

    def kept(p, s):
        return KEEP.at[lax.rem(p, KEEP_SLOTS), s * HALF : (s + 1) * HALF, :]

    def final(p, half):
        return gout.at[block(p), half_of(half), :]

    def rc(p):
        return remote(GIVE.at[lax.rem(p, GIVE_SLOTS)], CR.at[p], rc_s.at[lax.rem(p, GIVE_SLOTS)], rc_r.at[p], at_core)

    R_Y, R_Z, R_FY, R_FC, R_OUT = range(5)

    def ry(p):
        return remote(CR.at[p], YR.at[slot(p)], r_s.at[R_Y], ry_r.at[slot(p)], at_y)

    def rz(p, s, idx, to):
        return remote(part(p, s), ZR.at[zslot(p), idx], r_s.at[R_Z], rz_r.at[zslot(p), idx], (sec, seq, to))

    def yx(p):
        return remote(part(p, ten), YX.at[slot(p)], yx_s.at[slot(p)], fy_r.at[p], at_y)

    def fy(p):
        return remote(part(p, ten), final(p, core), r_s.at[R_FY], fy_r.at[p], at_y)

    def fc(p, src):
        return remote(src, final(p, core), r_s.at[R_FC], fc_r.at[0], at_core)

    def out_g(p):
        return pltpu.make_async_copy(part(p, ten), final(p, core), r_s.at[R_OUT])

    def add(ref, *others_):
        total = ref[...].astype(f32)
        for other in others_:
            total = total + other[...].astype(f32)
        ref[...] = total.astype(bf16)

    def compute(p):
        @pl.when(p >= GIVE_SLOTS)
        def _():
            rc(p - GIVE_SLOTS).wait_send()

        gradient(block(p))
        for s in range(SHARDS):
            theirs = TG[pl.ds(pl.multiple_of(s * PART + (1 - core) * HALF, 16), HALF), :]
            GIVE[lax.rem(p, GIVE_SLOTS), s * HALF : (s + 1) * HALF, :] = theirs.astype(bf16)
        rc(p).start()
        for s in range(SHARDS):
            kept(p, s)[...] = TG[pl.ds(pl.multiple_of(s * PART + core * HALF, 16), HALF), :].astype(bf16)

    def over_core(p):
        rc(p).wait_recv()
        for s in range(SHARDS):
            add(part(p, s), kept(p, s))

        @pl.when(jnp.logical_not(owned(p)))
        def _():
            ry(p).start()

    def over_y(p):
        @pl.when(owned(p))
        def _():
            ry(p).wait_recv()
            for s in range(SHARDS):
                add(part(p, s), YR.at[slot(p), s * HALF : (s + 1) * HALF, :])

    def chain_one(p):
        @pl.when(jnp.logical_and(owned(p), outer))
        def _():
            for k in range(3):
                s = jnp.where(low_side, 3 - k, k)
                idx = jnp.where(low_side, s - 1, s)
                rz(p, s, idx, jnp.where(low_side, 1, 2)).start()

        @pl.when(jnp.logical_and(owned(p), jnp.logical_not(outer)))
        def _():
            s = jnp.where(low_side, 0, 3)
            rz(p, s, 0, s).start()

    def chain_two(p):
        @pl.when(jnp.logical_and(owned(p), jnp.logical_not(outer)))
        def _():
            for s, idx in ((FAR, jnp.where(low_side, 2, 0)), (NEAR, 1)):
                rz(p, s, idx, s).wait_recv()
                add(part(p, s), ZR.at[zslot(p), idx])
                rz(p, s, 3, s).start()

    def chain_end(p):
        @pl.when(owned(p))
        def _():
            idx, at_z = jnp.where(ten == 2, 2, 0), lax.rem(ten + 1, SHARDS)
            rz(p, ten, idx, at_z).wait_recv()
            rz(p, ten, 3, at_z).wait_recv()
            add(part(p, ten), ZR.at[zslot(p), idx], ZR.at[zslot(p), 3])

            @pl.when(over_tensor_first(p))
            def _():
                yx(p).start()

            @pl.when(jnp.logical_not(over_tensor_first(p)))
            def _():
                fy(p).start()
                fc(p, part(p, ten)).start()
                out_g(p).start()

    def settle(p):
        @pl.when(over_tensor_first(p))
        def _():
            yx(p).wait()
            add(part(p, ten), YX.at[slot(p)])
            fc(p, part(p, ten)).start()
            out_g(p).start()

        @pl.when(jnp.logical_not(owned(p)))
        def _():
            fy(p).wait_recv()
            fc(p, final(p, core)).start()

    def vector_round(i):
        pair, far = ten + 1 - 2 * lax.rem(ten, 2), lax.rem(ten + 2, SHARDS)
        where_seq = jnp.where(i == 0, y * 2 + 1 - core, jnp.where(i == 1, (1 - y) * 2 + core, seq))
        where_ten = jnp.where(i == 2, pair, jnp.where(i == 3, far, ten))
        return remote(VS.at[i], VR.at[i], vr_s.at[i], vr_r.at[i], (sec, where_seq, where_ten))

    def sums(t):
        @pl.when(t == BLOCKS - 2)
        def _():
            last_grad_hidden()

        for stage, lag, first_kind in SCHEDULE:
            p = t - lag
            fits = jnp.logical_and(p >= 0, p < BLOCKS)
            if first_kind is not None:
                fits = jnp.logical_and(fits, over_tensor_first(p) if first_kind else jnp.logical_not(over_tensor_first(p)))

            @pl.when(fits)
            def _():
                dict(compute=compute, core=over_core, y=over_y, one=chain_one, two=chain_two, end=chain_end, settle=settle)[stage](p)

        late = t - BLOCKS

        @pl.when(jnp.logical_and(late >= 0, late < LATE_P3))
        def _():
            stage_p3(late + MICRO - LATE_P3)

        @pl.when(jnp.logical_and(jnp.logical_not(first), jnp.logical_and(late >= 0, late < MICRO)))
        def _():
            stage_out(late)

        i = late - LATE_P3

        @pl.when(i == 0)
        def _():
            small_gradients()

        @pl.when(jnp.logical_and(i > 0, i <= 4))
        def _():
            vector_round(i - 1).wait()
            VS[i] = VS[i - 1] + VR[i - 1]

        @pl.when(jnp.logical_and(i >= 0, i < 4))
        def _():
            vector_round(i).start()

    loop(BLOCKS + LAST_LAG, sums)
    vout[...] = VS[4]

    lines = POOL.at[pl.ds(0, BLOCKS * HALF), :]
    remote(lines, lines, r_s.at[R_FC], fc_r.at[0], at_core).wait()
    relay_drain()
    gather_drain()
    loop(GIVE_SLOTS, lambda i: rc(i).wait_send())
    left(r_s.at[R_Y], 3 * SHARDS * HALF)
    left(r_s.at[R_Z], 6 * 3 * HALF)
    left(r_s.at[R_FY], 3 * HALF)
    lines = POOL.at[pl.ds(0, 6 * HALF), :]
    pltpu.make_async_copy(lines, lines, r_s.at[R_OUT]).wait()


def relay(block_input, cotangent, mask, weights, vectors, fused):
    hbm = pl.BlockSpec(memory_space=pl.ANY)
    vmem = pl.BlockSpec(memory_space=pltpu.VMEM)
    dma = lambda *shape: pltpu.SemaphoreType.DMA(shape)
    low = lambda *shape: pltpu.VMEM(shape, bf16)
    full = lambda *shape: pltpu.VMEM(shape, f32)
    scratch = [
        low(BLOCKS + 1 if fused else BLOCKS, H, H),
        low(2, H, H),
        low(POOL_ROWS, H),
        low(2, ROWS, H),
        low(2, ROWS, H),
        low(MICRO, 3 * LEN, H),
        low(ROWS, H),
        low(ROWS, H),
        low(ROWS, H),
        low(ROWS, H),
        low(ROWS, H),
        low(2, ROWS, H),
        low(MICRO, 3 * LEN, H),
        low(ROWS, H),
        low(ROWS, H),
        full(ROWS, 8),
        full(H, H),
        full(16, H),
        full(2, 8, H),
        full(2, 8, H),
        full(12, 8, H),
        full(5, 16, H),
        dma(2),
        dma(5),
        dma(2),
        dma(1),
        dma(MICRO),
        dma(2),
        dma(MICRO, 2),
        dma(2),
        dma(MICRO, 2),
    ]
    if fused:
        scratch += [
            full(16, 256),
            low(2 * SHARDS, 16, 256),
            low(BLOCKS, SHARDS * HALF, H),
            low(KEEP_SLOTS, SHARDS * HALF, H),
            low(GIVE_SLOTS, SHARDS * HALF, H),
            low(3, SHARDS * HALF, H),
            low(6, 4, HALF, H),
            low(3, HALF, H),
            full(4, 16, H),
            dma(8),
            dma(SHARDS),
            dma(1),
            dma(BLOCKS + 1, SHARDS),
            dma(BLOCKS),
            dma(2),
            dma(1),
            dma(5),
            dma(GIVE_SLOTS),
            dma(BLOCKS),
            dma(3),
            dma(6, 4),
            dma(3),
            dma(BLOCKS),
            dma(1),
            dma(4),
            dma(4),
        ]
    outs = (
        jax.ShapeDtypeStruct((MICRO, LEN, 2 * H), bf16),
        jax.ShapeDtypeStruct((MICRO, LEN, 2 * H), bf16),
        jax.ShapeDtypeStruct((BLOCKS, PART, H), bf16) if fused else jax.ShapeDtypeStruct((BLOCKS, H, H), f32),
        jax.ShapeDtypeStruct((16, H), f32),
    )
    in_specs = [hbm, hbm, vmem] + [hbm] * len(weights) + [vmem] * len(vectors)
    return pl.pallas_call(
        functools.partial(relay_kernel, fused),
        out_shape=outs,
        in_specs=in_specs,
        out_specs=(hbm, hbm, hbm, vmem),
        scratch_shapes=scratch,
        compiler_params=pltpu.CompilerParams(collective_id=0, has_side_effects=True, vmem_limit_bytes=62 * 2**20),
        cost_estimate=pl.CostEstimate(flops=25_000_000_000, bytes_accessed=20_000_000, transcendentals=4_000_000),
        name="relay",
    )(block_input, cotangent, mask, *weights, *vectors)


def unpack_kernel(bo, ig, grads, small, bo_out, ig_out, in_out, mid_out, out_out, *rest):
    vectors, (B, G, F, sems) = rest[:9], rest[9:]
    ten = lax.axis_index("tensor")
    load = pltpu.make_async_copy(grads, G, sems.at[2, 0])
    load.start()
    arrays = [(k, m, src, dst) for k, (src, dst) in enumerate(((bo, bo_out), (ig, ig_out))) for m in range(MICRO)]
    arrive = [pltpu.make_async_copy(src.at[m], B.at[k, m], sems.at[k, m]) for k, m, src, dst in arrays]
    leave = [pltpu.make_async_copy(B.at[k, m], dst.at[0, m, 0], sems.at[4 + k, m]) for k, m, src, dst in arrays]
    for copy in arrive:
        copy.start()
    for z in range(SHARDS):

        @pl.when(ten == z)
        def _():
            for row, ref in zip((0, 1, 2, 3, 4, 5), vectors[:6]):
                ref[...] = small[row : row + 1, z * PART : (z + 1) * PART]
            for i, ref in enumerate(vectors[6:]):
                row, at = 6 + 2 * i + z // 2, z % 2 * 2 * PART
                ref[...] = small[row : row + 1, at : at + 2 * PART]

    load.wait()
    F[...] = G[...].astype(f32)
    outs = [pltpu.make_async_copy(F.at[h + 2 * k], ref.at[:, pl.ds(h * H, H)], sems.at[3, 2 * k + h]) for k, ref in enumerate((in_out, out_out)) for h in range(2)]
    outs += [pltpu.make_async_copy(F.at[pl.ds(4, 5)], mid_out, sems.at[2, 1])]
    for out in outs:
        out.start()
    for came, copy in zip(arrive, leave):
        came.wait()
        copy.start()
    for copy in leave + outs:
        copy.wait()


def unpacked(block_out, input_grad, grads, small):
    hbm, vmem = pl.BlockSpec(memory_space=pl.ANY), pl.BlockSpec(memory_space=pltpu.VMEM)
    like = lambda *shape: jax.ShapeDtypeStruct(shape, f32)
    rows_like = jax.ShapeDtypeStruct((1, MICRO, 1, LEN, 2 * H), bf16)
    (block_out, input_grad, grad_in, grad_mid, grad_out, *vectors) = pl.pallas_call(
        unpack_kernel,
        out_shape=[rows_like, rows_like, like(PART, 2 * H), like(5, PART, H), like(PART, 2 * H)] + [like(1, PART)] * 6 + [like(1, 2 * PART)] * 3,
        in_specs=[hbm, hbm, hbm, vmem],
        out_specs=[hbm] * 5 + [vmem] * 9,
        scratch_shapes=[pltpu.VMEM((2, MICRO, LEN, 2 * H), bf16), pltpu.VMEM((BLOCKS, PART, H), bf16), pltpu.VMEM((BLOCKS, PART, H), f32), pltpu.SemaphoreType.DMA((6, MICRO))],
        compiler_params=pltpu.CompilerParams(vmem_limit_bytes=62 * 2**20),
        name="unpack",
    )(block_out, input_grad, grads, small)
    (bias_in, bias_mid, gain_second, shift_second, gain_third, shift_third, bias_out, gain_first, shift_first) = vectors
    return (
        block_out,
        input_grad,
        grad_in.T[None],
        bias_in,
        grad_mid.transpose(0, 2, 1)[None],
        bias_mid,
        grad_out[None],
        bias_out,
        gain_first,
        shift_first,
        gain_second,
        shift_second,
        gain_third,
        shift_third,
    )


def packed_weights(conv_in, conv_mid, conv_out):
    channels = conv_out.shape[0]
    halves = lambda m: m.reshape(channels, 2, H).transpose(1, 0, 2)
    return jnp.concatenate([halves(conv_in.T), halves(conv_out), conv_mid.transpose(0, 2, 1)])


def local(*args):
    block_input, cotangent, mask = args[:3]
    (conv_in, bias_in, conv_mid, bias_mid, conv_out, bias_out, gain_first, shift_first, gain_second, shift_second, gain_third, shift_third) = (a[0] for a in args[3:])
    ten, sec = lax.axis_index("tensor"), lax.axis_index("section")
    shards = lax.axis_size("tensor")
    fused = shards == SHARDS
    channels = conv_out.shape[0]
    narrow = (bias_in, bias_mid, gain_second, shift_second, gain_third, shift_third)
    wide = (bias_out, gain_first, shift_first)
    if fused:
        weights = (conv_in.T, conv_mid.transpose(0, 2, 1), conv_out)
        block_out, input_grad, grads, small = relay(block_input, cotangent, mask, weights, tuple(v[None] for v in narrow + wide), True)
        return unpacked(block_out, input_grad, grads, small)
    else:
        mine = packed_weights(conv_in, conv_mid, conv_out)
        whole = lax.all_gather(mine, "tensor", axis=1, tiled=True)
        swap = [(0, 1), (1, 0)]
        give = jnp.where(sec == 0, whole[2:4], whole[0:2])
        other = lax.ppermute(give, "section", swap)
        v_narrow = lax.all_gather(jnp.stack(narrow), "tensor", axis=1, tiled=True)
        v_wide = lax.all_gather(jnp.stack(wide), "tensor", axis=1, tiled=True)
        v640 = jnp.pad(v_narrow.astype(f32), ((0, 10), (0, 0)))
        v1280 = jnp.pad(v_wide.astype(f32).reshape(3, 2, H).transpose(1, 0, 2), ((0, 0), (0, 5), (0, 0)))
        vx = lax.ppermute(v1280, "section", swap)
        block_out, input_grad, grads, small = relay(block_input, cotangent, mask, (whole, other), (v640, v1280, vx), False)
        grads = lax.psum(lax.psum_scatter(grads, "tensor", scatter_dimension=1, tiled=True), "seq")
        small = lax.psum(small, ("seq", "tensor"))
    grad_in = grads[0:2].transpose(0, 2, 1).reshape(2 * H, channels)
    grad_out = grads[2:4].transpose(1, 0, 2).reshape(channels, 2 * H)
    grad_mid = grads[4:9].transpose(0, 2, 1)
    thin = lax.dynamic_slice_in_dim(small[0:6], ten * channels, channels, 1)
    thick = lax.dynamic_slice_in_dim(small[6:12].reshape(3, 2 * H), ten * 2 * channels, 2 * channels, 1)
    shape = (1, MICRO, 1, LEN, 2 * H)
    return (
        block_out.reshape(shape),
        input_grad.reshape(shape),
        grad_in[None],
        thin[0:1],
        grad_mid[None],
        thin[1:2],
        grad_out[None],
        thick[0:1],
        thick[1:2],
        thick[2:3],
        thin[2:3],
        thin[3:4],
        thin[4:5],
        thin[5:6],
    )


def solution(mesh):
    in_specs = (
        P(None, "tensor", "seq", None),
        P(None, "tensor", "seq", None),
        P(None, "tensor", "seq"),
        P("section", None, "tensor"),
        P("section", "tensor"),
        P("section", None, None, "tensor"),
        P("section", "tensor"),
        P("section", "tensor", None),
        P("section", "tensor"),
        P("section", "tensor"),
        P("section", "tensor"),
        P("section", "tensor"),
        P("section", "tensor"),
        P("section", "tensor"),
        P("section", "tensor"),
    )
    out_specs = (
        P("section", None, "tensor", "seq", None),
        P("section", None, "tensor", "seq", None),
        P("section", None, "tensor"),
        P("section", "tensor"),
        P("section", None, None, "tensor"),
        P("section", "tensor"),
        P("section", "tensor", None),
        P("section", "tensor"),
        P("section", "tensor"),
        P("section", "tensor"),
        P("section", "tensor"),
        P("section", "tensor"),
        P("section", "tensor"),
        P("section", "tensor"),
    )
    return jax.shard_map(local, mesh=mesh, in_specs=in_specs, out_specs=out_specs, check_vma=False)
```

```python
import functools

import jax
import jax.numpy as jnp
from jax import lax
from jax.experimental import pallas as pl
from jax.experimental.pallas import tpu as pltpu
from jax.sharding import PartitionSpec as P

DILATION_BASE = 64
EPS = 1e-05
ROOT_HALF = 0.7071067811865476
INVERSE_ROOT_TWO_PI = 0.3989422804014327
MESH = pl.DeviceIdType.MESH
f32 = jnp.float32
bf16 = jnp.bfloat16

MICRO = 4
LEN = 256
H = 640
ROWS = MICRO * LEN
SHARDS = 4
PART = H // SHARDS
HALF = PART // 2
BLOCKS = 9
LAST = BLOCKS - 1
GUEST, GUEST_TURN = BLOCKS, 3
TILE = 256
WIDE = 128
Y_LAG, C_LAG = 1, 6
X_STEP = 9
F_STEP = 2
A_STEP = C_LAG + 1
EARLY_A = 2
LEAD = 3
NN = (((1,), (0,)), ((), ()))
NT = (((1,), (1,)), ((), ()))
TN = (((0,), (0,)), ((), ()))

E_AT, SX_AT, LV_AT, POOL_ROWS = 0, 2 * ROWS, 4 * ROWS, 6 * ROWS
KEEP_SLOTS, GIVE_SLOTS = 3, 3
SCHEDULE = (
    ("two", 6, False),
    ("compute", 0, None),
    ("settle", 12, True),
    ("core", 1, None),
    ("end", 8, True),
    ("settle", 12, False),
    ("two", 3, True),
    ("one", 1, True),
    ("end", 8, False),
    ("y", 4, False),
    ("one", 4, False),
)
LAST_LAG = 12
LATE_P2, LATE_P3 = 2, 3


def dot(a, b, dims):
    return lax.dot_general(a, b, dims, preferred_element_type=f32)


def loop(count, body):
    def step(i, carry):
        body(i)
        return carry

    lax.fori_loop(0, count, step, 0)


def unroll(count, body):
    for i in range(count):
        body(i)


def row_stats(parts, width):
    mean = sum(jnp.sum(x, axis=-1, keepdims=True) for x in parts) / width
    spread = sum(jnp.sum(x * x, axis=-1, keepdims=True) for x in parts) / width - mean * mean
    return mean, lax.rsqrt(spread + EPS)


def gelu_slope(v):
    phi = 0.5 * (1.0 + lax.erf(v * ROOT_HALF))
    return phi, phi + v * (jnp.exp(-0.5 * v * v) * INVERSE_ROOT_TWO_PI)


def norm_back(ys, normeds, inverse, gains, width):
    scaled = [y * g for y, g in zip(ys, gains)]
    total = sum(jnp.sum(s, axis=-1, keepdims=True) for s in scaled) / width
    along = sum(jnp.sum(s * n, axis=-1, keepdims=True) for s, n in zip(scaled, normeds)) / width
    return [inverse * (s - total - n * along) for s, n in zip(scaled, normeds)]


def eights(x):
    return jnp.sum(x.reshape(x.shape[0] // 8, 8, x.shape[1]), axis=0)


def relay_kernel(fused, *refs):
    if fused:
        (xin, cot, mask, w_in, w_mid, w_out) = refs[:6]
        narrow_in, wide_in = refs[6:12], refs[12:15]
        (bo, ig, gout, vout) = refs[15:19]
        rest = refs[19:]
    else:
        (xin, cot, mask, wfull, wother, v640_in, v1280_in, vx_in, bo, ig, gout, vout) = refs[:12]
        rest = refs[12:]
    (W, WX, POOL, A1, S1, A2, S2, N2, A3, S3, N3, U, GM, GH, XR, ST, TG, V640, V1280, VX, AC, VS) = rest[:22]
    (l_in, l_w, o_s, x_s, x_r, ha_s, ha_r, hg_s, hg_r) = rest[22:31]
    if fused:
        (VF, VG, CR, KEEP, GIVE, YR, ZR, YX, VR, g_s, gg_r, vg_r, ga_r, gc_r, wx_r, wc_r, r_s, rc_s, rc_r, ry_r, rz_r, yx_s, fy_r, fc_r, vr_s, vr_r) = rest[31:]

    sec = lax.axis_index("section")
    seq = lax.axis_index("seq")
    ten = lax.axis_index("tensor")
    y = seq // 2
    core = lax.rem(seq, 2)
    at_core = (sec, y * 2 + (1 - core), ten)
    at_y = (sec, (1 - y) * 2 + core, ten)
    at_diag = (sec, (1 - y) * 2 + (1 - core), ten)
    at_x = (1 - sec, seq, ten)
    up, down = (sec, seq, ten + 1), (sec, seq, ten - 1)
    behind, ahead = (sec, seq - 1, ten), (sec, seq + 1, ten)
    first = sec == 0

    def remote(src, dst, send, recv, where):
        return pltpu.make_async_remote_copy(src_ref=src, dst_ref=dst, send_sem=send, recv_sem=recv, device_id=where, device_id_type=MESH)

    def left(send, count, width=None):
        lines = VG.at[pl.ds(0, count)] if width else POOL.at[pl.ds(0, count), :]
        remote(lines, lines, send, x_r.at[0], at_x).wait_send()

    def rows(base, m, r=0, n=LEN):
        return pl.ds(pl.multiple_of(base + m * LEN + r, 16), n)

    def load_in(m, h, ref, into, sem):
        pltpu.make_async_copy(ref.at[m, 0, :, pl.ds(h * H, H)], into, sem).start()

    def loaded(into, sem):
        pltpu.make_async_copy(into, into, sem).wait()

    if fused:
        own_rows = pl.ds(pl.multiple_of(ten * PART, 16), PART)
        own = [pltpu.make_async_copy(w_in.at[:, pl.ds(h * H, H)], W.at[h, own_rows, :], l_w.at[h]) for h in range(2)]
        own += [pltpu.make_async_copy(w_out.at[:, pl.ds(h * H, H)], W.at[2 + h, own_rows, :], l_w.at[2 + h]) for h in range(2)]
        own += [pltpu.make_async_copy(w_mid, W.at[pl.ds(4, 5), own_rows, :], l_w.at[4])]
        partners = [at_core, at_y, at_diag]
        others = [(s, d) for s in range(2) for d in range(SHARDS) if s or d]
        partners += [(lax.rem(sec + s, 2), seq, lax.rem(ten + d, SHARDS)) for s, d in others]
    else:
        own = [pltpu.make_async_copy(wfull, W, l_w.at[0]), pltpu.make_async_copy(wother, WX, l_w.at[1])]
        partners = [at_core, at_diag, at_x]
    for copy in own:
        copy.start()
    for m in range(MICRO):
        for h in range(2):
            load_in(m, h, xin, POOL.at[pl.ds(E_AT + h * ROWS + m * LEN, LEN), :], l_in.at[0])
            load_in(m, h, cot, U.at[h, pl.ds(m * LEN, LEN), :], l_in.at[1])

    if fused:
        VF[...] = jnp.zeros_like(VF)
        for i, ref in enumerate(narrow_in):
            VF[i : i + 1, 0:PART] = ref[...].astype(f32)
        for i, ref in enumerate(wide_in):
            for half in range(2):
                VF[6 + 3 * half + i : 7 + 3 * half + i, 0:PART] = ref[:, half * PART : (half + 1) * PART].astype(f32)
        VG[sec * SHARDS + ten] = VF[...].astype(bf16)

    barrier = pltpu.get_barrier_semaphore()
    for partner in partners:
        pl.semaphore_signal(barrier, inc=1, device_id=partner, device_id_type=MESH)
    pl.semaphore_wait(barrier, len(partners))

    def piece(ref, b, s, half):
        return ref.at[b, pl.ds(pl.multiple_of(s * PART + half * HALF, 16), HALF), :]

    UP, DOWN, Y_, CORE_, X_, XC_, V_, G_ = range(8)

    def gz(b, s, to_up):
        spot = piece(W, b, s, core)
        return remote(spot, spot, g_s.at[UP if to_up else DOWN], ga_r.at[b, s], up if to_up else down)

    def gy(b, s):
        spot = piece(W, b, s, core)
        return remote(spot, spot, g_s.at[Y_], ga_r.at[b, s], at_y)

    def gc(b, s):
        spot = piece(W, b, s, core)
        return remote(spot, spot, g_s.at[CORE_], gc_r.at[b], at_core)

    def gc_here(b):
        lines = W.at[b, pl.ds(0, (SHARDS - 1) * HALF), :]
        remote(lines, lines, g_s.at[CORE_], gc_r.at[b], at_core).wait_recv()

    def wanted(b):
        return b // 2 == 1 - sec

    def gx(b, s):
        k = lax.rem(b, 2)
        return remote(piece(W, b, s, core), piece(WX, k, s, core), g_s.at[X_], wx_r.at[k], at_x)

    def gx_here(k):
        lines = WX.at[k, pl.ds(0, SHARDS * HALF), :]
        remote(lines, lines, g_s.at[X_], wx_r.at[k], at_x).wait_recv()

    def gxc(k, s):
        spot = piece(WX, k, s, core)
        return remote(spot, spot, g_s.at[XC_], wc_r.at[0], at_core)

    def gv(i):
        s, d = others[i]
        return remote(VG.at[sec * SHARDS + ten], VG.at[sec * SHARDS + ten], g_s.at[V_], vg_r.at[0], (lax.rem(sec + s, 2), seq, lax.rem(ten + d, SHARDS)))

    def gg(s):
        return remote(piece(W, jnp.where(first, LAST, GUEST), s, core), piece(W, jnp.where(first, GUEST, LAST), s, core), g_s.at[G_], gg_r.at[s], at_x)

    def turn(j):
        return jnp.where(first, j, jnp.where(j < GUEST_TURN, j, jnp.where(j == GUEST_TURN, GUEST, j - 1)))

    turns = jnp.where(first, BLOCKS, BLOCKS + 1)
    mine = lambda b: jnp.where(b < LAST, lax.rem(b, 2) == y, jnp.logical_not(first))
    def send_own(j):
        b = turn(j)

        @pl.when(b == GUEST)
        def _():
            gg(ten).wait_recv()

        @pl.when(jnp.logical_and(mine(b), ten < SHARDS - 1))
        def _():
            gz(b, ten, True).start()

        @pl.when(jnp.logical_and(mine(b), ten > 0))
        def _():
            gz(b, ten, False).start()

        @pl.when(wanted(b))
        def _():
            gx(b, ten).start()

    def gather_begin():
        for j in range(2):
            own[j].wait()
            send_own(j)
        for copy in own[2:]:
            copy.wait()

        @pl.when(first)
        def _():
            gg(ten).start()

        for i in range(len(others)):
            gv(i).start()
        for j in range(2, LEAD):
            send_own(j)

    def gather_step(k):
        @pl.when(k + LEAD < turns)
        def _():
            send_own(k + LEAD)

        for d in range(1, SHARDS):
            j = k - (d - 1)
            b = turn(j)
            ok = jnp.logical_and(j >= 0, j < turns)
            for above in (False, True):
                s = ten + d if above else ten - d
                there = jnp.logical_and(ok, s < SHARDS if above else s >= 0)
                onward = (ten > 0) if above else (ten < SHARDS - 1)

                @pl.when(jnp.logical_and(there, mine(b)))
                def _():
                    gz(b, s, True).wait_recv()

                    @pl.when(onward)
                    def _():
                        gz(b, s, not above).start()

                    @pl.when(b < LAST)
                    def _():
                        gy(b, s).start()

                    @pl.when(b < GUEST)
                    def _():
                        gc(b, s).start()

                    @pl.when(b == GUEST)
                    def _():
                        gg(s).start()

                    @pl.when(wanted(b))
                    def _():
                        gx(b, s).start()

        for d in range(1, SHARDS):
            j = k - d - Y_LAG
            b = turn(j)
            ok = jnp.logical_and(j >= 0, j < turns)
            for above in (False, True):
                s = ten + d if above else ten - d
                there = jnp.logical_and(ok, s < SHARDS if above else s >= 0)

                @pl.when(jnp.logical_and(there, jnp.logical_not(mine(b))))
                def _():
                    @pl.when(b < LAST)
                    def _():
                        gy(b, s).wait_recv()

                    @pl.when(b == LAST)
                    def _():
                        gg(s).wait_recv()

                    gc(b, s).start()

                    @pl.when(wanted(b))
                    def _():
                        gx(b, s).start()

        j = k - C_LAG
        b = turn(j)

        @pl.when(jnp.logical_and(jnp.logical_and(j >= 0, j < turns), b < GUEST))
        def _():
            gc_here(b)

        @pl.when(jnp.logical_and(k >= X_STEP, k < X_STEP + 2))
        def _():
            gx_here(k - X_STEP)
            for s in range(SHARDS):
                gxc(k - X_STEP, s).start()

    def others_blocks():
        lines = POOL.at[pl.ds(0, 2 * SHARDS * HALF), :]
        remote(lines, lines, g_s.at[XC_], wc_r.at[0], at_core).wait_recv()

    def gather_drain():
        left(g_s.at[V_], len(others), True)
        left(g_s.at[Y_], 4 * (SHARDS - 1) * HALF)
        left(g_s.at[CORE_], BLOCKS * (SHARDS - 1) * HALF)
        left(g_s.at[X_], 2 * SHARDS * HALF)
        left(g_s.at[XC_], 2 * SHARDS * HALF)
        for who, count, pieces in ((0, 4, 1), (1, 6, SHARDS - 1)):

            @pl.when(sec == who)
            def _():
                left(g_s.at[G_], pieces * HALF)

            for z in range(SHARDS):

                @pl.when(jnp.logical_and(sec == who, ten == z))
                def _():
                    if z < SHARDS - 1:
                        left(g_s.at[UP], count * (z + 1) * HALF)
                    if z > 0:
                        left(g_s.at[DOWN], count * (SHARDS - z) * HALF)

    def vectors():
        lines = VG.at[pl.ds(0, len(others))]
        remote(lines, lines, g_s.at[V_], vg_r.at[0], at_x).wait_recv()
        line = lax.broadcasted_iota(jnp.int32, (2 * 128, H), 0)
        col = lax.broadcasted_iota(jnp.int32, (2 * 128, H), 1)

        def pick(offset):
            return jnp.where(col == line + offset, 1.0, 0.0).astype(bf16)

        narrow = jnp.zeros((16, H), f32)
        wide = [[jnp.zeros((16, H), f32) for _ in range(4)] for _ in range(2)]
        for s in range(SHARDS):
            inner = pick(s * PART)
            narrow = narrow + dot(VG[sec * SHARDS + s], inner, NN)
            for who in range(2):
                held = VG[(sec if who == 0 else 1 - sec) * SHARDS + s]
                for h in range(2):
                    for k in range(2):
                        put = pick(s * 2 * PART + k * PART - h * H)
                        wide[who][h * 2 + k] = wide[who][h * 2 + k] + dot(held, put, NN)
        V640[...] = narrow
        for who, into in ((0, V1280), (1, VX)):
            for h in range(2):
                into[h, 0:3, :] = wide[who][h * 2][6:9] + wide[who][h * 2 + 1][9:12]

    def halo(ref, sends, recvs, m, reach, start):
        fwd = remote(ref.at[m, pl.ds(2 * LEN - reach, reach), :], ref.at[m, pl.ds(LEN - reach, reach), :], sends.at[0], recvs.at[m, 0], ahead)
        bwd = remote(ref.at[m, pl.ds(LEN, reach), :], ref.at[m, pl.ds(2 * LEN, reach), :], sends.at[1], recvs.at[m, 1], behind)

        @pl.when(seq < 3)
        def _():
            fwd.start() if start else bwd.wait_recv()

        @pl.when(seq > 0)
        def _():
            bwd.start() if start else fwd.wait_recv()

    def halo_drain(sends):
        for s, reach in ((0, 2 * SPAN_0), (1, 2 * SPAN_1)):

            @pl.when(jnp.logical_and(sec == s, seq < 3))
            def _():
                left(sends.at[0], MICRO * reach)

            @pl.when(jnp.logical_and(sec == s, seq > 0))
            def _():
                left(sends.at[1], MICRO * reach)

    def x_send(m, src):
        return remote(src.at[rows(0, m), :], XR.at[rows(0, m), :], x_s.at[0], x_r.at[m], at_x)

    def stage_first(m):
        def tile(i):
            r = i * WIDE
            at = rows(0, m, r, WIDE)
            x = [POOL[rows(E_AT + h * ROWS, m, r, WIDE), :].astype(f32) for h in range(2)]
            mean, inverse = row_stats(x, 2 * H)
            ST[at, 0:1] = mean
            ST[at, 1:2] = inverse
            for h in range(2):
                v = (x[h] - mean) * inverse * V1280[h, 1:2, :] + V1280[h, 2:3, :]
                phi, slope = gelu_slope(v)
                A1[h, at, :] = (v * phi).astype(bf16)
                S1[h, at, :] = slope.astype(bf16)

        unroll(LEN // WIDE, tile)

    def stage_a(m, reach):
        here = rows(0, m)
        TG[0:LEN, :] = dot(A1[0, here, :], W[0], NT) + dot(A1[1, here, :], W[1], NT)

        def tile2(i):
            r = i * TILE
            at = rows(0, m, r, TILE)
            x = TG[pl.ds(r, TILE), :] + V640[0:1, :]
            mean, inverse = row_stats([x], H)
            normed = (x - mean) * inverse
            v = normed * V640[2:3, :] + V640[3:4, :]
            phi, slope = gelu_slope(v)
            A2[m, pl.ds(pl.multiple_of(LEN + r, 16), TILE), :] = (v * phi).astype(bf16)
            S2[at, :] = slope.astype(bf16)
            N2[at, :] = normed.astype(bf16)
            ST[at, 2:3] = inverse

        unroll(LEN // TILE, tile2)
        halo(A2, ha_s, ha_r, m, reach, True)

    def stage_b(m, span):
        halo(A2, ha_s, ha_r, m, 2 * span, False)
        taps = [A2[m, pl.ds(LEN + (t - 2) * span, LEN), :] for t in range(5)]
        TG[0:LEN, :] = dot(jnp.concatenate(taps, axis=1), jnp.concatenate([W[4 + t] for t in range(5)], axis=1), NT)

        def tile(i):
            r = i * TILE
            at = rows(0, m, r, TILE)
            x = TG[pl.ds(r, TILE), :] + V640[1:2, :]
            mean, inverse = row_stats([x], H)
            normed = (x - mean) * inverse
            v = normed * V640[4:5, :] + V640[5:6, :]
            phi, slope = gelu_slope(v)
            A3[at, :] = (v * phi).astype(bf16)
            S3[at, :] = slope.astype(bf16)
            N3[at, :] = normed.astype(bf16)
            ST[at, 3:4] = inverse

        unroll(LEN // TILE, tile)

    def stage_out(m):
        here = rows(0, m)
        for h in range(2):
            mixed = dot(A3[here, :], W[2 + h], NN) + V1280[h, 0:1, :]
            POOL[rows(LV_AT + h * ROWS, m), :] = (POOL[rows(E_AT + h * ROWS, m), :].astype(f32) + mixed).astype(bf16)
            out_bo(m, h).start()

    def out_bo(m, h):
        return pltpu.make_async_copy(POOL.at[rows(LV_AT + h * ROWS, m), :], bo.at[m, :, pl.ds(h * H, H)], o_s.at[0])

    def out_ig(m, h):
        return pltpu.make_async_copy(S1.at[h, rows(0, m), :], ig.at[m, :, pl.ds(h * H, H)], o_s.at[1])

    def stage_x(m):
        x_send(m, A3).wait_recv()
        for h in range(2):
            at = rows(E_AT + h * ROWS, m)
            mixed = dot(XR[rows(0, m), :], WX[h], NN) + VX[h, 0:1, :]
            POOL[at, :] = (POOL[at, :].astype(f32) + mixed).astype(bf16)

    def stage_n(m):
        def tile(i):
            r = i * WIDE
            at = rows(0, m, r, WIDE)
            x = [POOL[rows(LV_AT + h * ROWS, m, r, WIDE), :].astype(f32) for h in range(2)]
            mean, inverse = row_stats(x, 2 * H)
            ST[at, 4:5] = mean
            ST[at, 5:6] = inverse
            for h in range(2):
                v = (x[h] - mean) * inverse * VX[h, 1:2, :] + VX[h, 2:3, :]
                POOL[rows(SX_AT + h * ROWS, m, r, WIDE), :] = gelu_slope(v)[1].astype(bf16)

        unroll(LEN // WIDE, tile)

    def stage_q(m):
        x_send(m, GH).wait_recv()
        for h in range(2):
            TG[h * LEN : (h + 1) * LEN, :] = dot(XR[rows(0, m), :], WX[h], NN)

        def tile(i):
            r = i * WIDE
            at = rows(0, m, r, WIDE)
            mean, inverse = ST[at, 4:5], ST[at, 5:6]
            ys, normeds = [], []
            for h in range(2):
                slope = POOL[rows(SX_AT + h * ROWS, m, r, WIDE), :].astype(f32)
                ys.append(TG[pl.ds(h * LEN + r, WIDE), :] * slope)
                normeds.append((POOL[rows(LV_AT + h * ROWS, m, r, WIDE), :].astype(f32) - mean) * inverse)
            grads = norm_back(ys, normeds, inverse, [VX[h, 1:2, :] for h in range(2)], 2 * H)
            for h in range(2):
                U[h, at, :] = (U[h, at, :].astype(f32) + grads[h]).astype(bf16)

        unroll(LEN // WIDE, tile)

    def back_three(m):
        here = rows(0, m)
        return dot(U[0, here, :], W[2], NT) + dot(U[1, here, :], W[3], NT)

    def stage_back_three(m):
        full_ = back_three(m)
        high = full_.astype(bf16)
        POOL[rows(SX_AT, m), :] = high
        POOL[rows(SX_AT + ROWS, m), :] = (full_ - high.astype(f32)).astype(bf16)

    def stage_p1(m, reach, kept_):
        if kept_:
            back = POOL[rows(SX_AT, m), :].astype(f32) + POOL[rows(SX_AT + ROWS, m), :].astype(f32)
        else:
            back = back_three(m)
        at = rows(0, m)
        y_ = back * S3[at, :].astype(f32)
        normed = N3[at, :].astype(f32)
        (grad,) = norm_back([y_], [normed], ST[at, 3:4], [V640[4:5, :]], H)
        low = grad.astype(bf16)
        GM[m, LEN : 2 * LEN, :] = low
        halo(GM, hg_s, hg_r, m, reach, True)
        AC[4] += eights(y_ * normed)
        AC[5] += eights(y_)
        AC[1] += eights(low.astype(f32))

    def stage_p2(m, span, relay):
        halo(GM, hg_s, hg_r, m, 2 * span, False)
        taps = [GM[m, pl.ds(LEN - (t - 2) * span, LEN), :] for t in range(5)]
        TG[0:LEN, :] = dot(jnp.concatenate(taps, axis=1), jnp.concatenate([W[4 + t] for t in range(5)]), NN)

        def tile(i):
            r = i * TILE
            at = rows(0, m, r, TILE)
            y_ = TG[pl.ds(r, TILE), :] * S2[at, :].astype(f32)
            normed = N2[at, :].astype(f32)
            (grad,) = norm_back([y_], [normed], ST[at, 2:3], [V640[2:3, :]], H)
            low = grad.astype(bf16)
            GH[at, :] = low
            AC[2] += eights(y_ * normed)
            AC[3] += eights(y_)
            AC[0] += eights(low.astype(f32))

        unroll(LEN // TILE, tile)
        if relay:
            x_send(m, GH).start()

    def stage_p3(m):
        for h in range(2):
            TG[h * LEN : (h + 1) * LEN, :] = dot(GH[rows(0, m), :], W[h], NN)

        def tile(i):
            r = i * WIDE
            at = rows(0, m, r, WIDE)
            mean, inverse = ST[at, 0:1], ST[at, 1:2]
            ys, normeds = [], []
            for h in range(2):
                ys.append(TG[pl.ds(h * LEN + r, WIDE), :] * S1[h, at, :].astype(f32))
                normeds.append((POOL[rows(E_AT + h * ROWS, m, r, WIDE), :].astype(f32) - mean) * inverse)
            grads = norm_back(ys, normeds, inverse, [V1280[h, 1:2, :] for h in range(2)], 2 * H)
            for h in range(2):
                S1[h, at, :] = (U[h, at, :].astype(f32) + grads[h]).astype(bf16)
                AC[6 + h] += eights(U[h, at, :].astype(f32))
                AC[8 + h] += eights(ys[h] * normeds[h])
                AC[10 + h] += eights(ys[h])

        unroll(LEN // WIDE, tile)
        for h in range(2):
            out_ig(m, h).start()

    def prepare():
        AC[...] = jnp.zeros_like(AC)
        for ref in (A2, GM):

            @pl.when(seq == 0)
            def _():
                for m in range(MICRO):
                    ref[m, 0:LEN, :] = jnp.zeros((LEN, H), bf16)

            @pl.when(seq == 3)
            def _():
                for m in range(MICRO):
                    ref[m, 2 * LEN : 3 * LEN, :] = jnp.zeros((LEN, H), bf16)

        for m in range(MICRO):
            ST[m * LEN : (m + 1) * LEN, 6:7] = jnp.transpose(jnp.broadcast_to(mask[m].astype(f32), (128, LEN)))[:, 0:1]
        loaded(POOL.at[pl.ds(E_AT, 2 * ROWS), :], l_in.at[0])
        loaded(U, l_in.at[1])

        def masked(m):
            at = rows(0, m)
            keep = ST[at, 6:7]
            for h in range(2):
                U[h, at, :] = (U[h, at, :].astype(f32) * keep).astype(bf16)

        loop(MICRO, masked)

    SPAN_0, SPAN_1 = DILATION_BASE, 2 * DILATION_BASE
    span = DILATION_BASE * (1 + sec)
    early = 0
    if fused:
        gather_begin()
        prepare()
        early = MICRO

        def step(k):
            gather_step(k)

            @pl.when(k == F_STEP)
            def _():
                vectors()

            @pl.when(jnp.logical_and(first, jnp.logical_and(k >= F_STEP, k < F_STEP + MICRO)))
            def _():
                stage_first(k - F_STEP)

            @pl.when(jnp.logical_and(first, jnp.logical_and(k >= A_STEP, k < A_STEP + EARLY_A)))
            def _():
                stage_a(k - A_STEP, 2 * SPAN_0)

        loop(BLOCKS + 1 + C_LAG, step)
    else:
        for copy in own:
            copy.wait()
        for src, dst in ((v640_in, V640), (v1280_in, V1280), (vx_in, VX)):
            dst[...] = src[...]
        prepare()

    @pl.when(first)
    def _():
        def firsts(m):
            stage_first(m)
            stage_a(m, 2 * SPAN_0)

        if early == 0:
            loop(MICRO, firsts)

        def leave(m):
            stage_b(m, SPAN_0)
            x_send(m, A3).start()
            if early:

                @pl.when(m + EARLY_A < MICRO)
                def _():
                    stage_a(m + EARLY_A, 2 * SPAN_0)

            stage_out(m)

        loop(MICRO, leave)
        if fused:
            others_blocks()
        loop(MICRO, stage_n)

        def backward(m):
            stage_q(m)
            stage_p1(m, 2 * SPAN_0, False)

            @pl.when(m < MICRO - LATE_P2)
            def _():
                stage_p2(m, SPAN_0, False)

            @pl.when(m < MICRO - LATE_P3)
            def _():
                stage_p3(m)

        loop(MICRO, backward)

    @pl.when(jnp.logical_not(first))
    def _():
        if fused:
            others_blocks()
        loop(MICRO, stage_back_three)

        def both(k):
            @pl.when(k < MICRO)
            def _():
                stage_x(k)
                stage_first(k)
                stage_a(k, 2 * SPAN_1)

            @pl.when(jnp.logical_and(k >= 1, k <= MICRO))
            def _():
                stage_b(k - 1, SPAN_1)
                stage_p1(k - 1, 2 * SPAN_1, True)

            @pl.when(k == MICRO + 1)
            def _():
                loop(MICRO - LATE_P3, stage_p3)

            @pl.when(k >= 2)
            def _():
                stage_p2(k - 2, SPAN_1, True)

        loop(MICRO + 2, both)

    def last_grad_hidden():
        @pl.when(first)
        def _():
            loop(LATE_P2, lambda m: stage_p2(m + MICRO - LATE_P2, SPAN_0, False))

    def small_gradients():
        for i in range(12):
            VS[0, i : i + 1, :] = jnp.sum(AC[i], axis=0, keepdims=True)
        VS[0, 12:16, :] = jnp.zeros((4, H), f32)

    def relay_drain():
        left(x_s.at[0], ROWS)
        halo_drain(ha_s)
        halo_drain(hg_s)
        for i in range(2):
            lines = POOL.at[pl.ds(0, 2 * ROWS), :]
            pltpu.make_async_copy(lines, lines, o_s.at[i]).wait()

    def gradient(b):
        @pl.when(b < 2)
        def _():
            TG[...] = dot(GH[...], A1[b], TN)

        @pl.when(jnp.logical_and(b >= 2, b < 4))
        def _():
            TG[...] = dot(A3[...], U[b - 2], TN)

        @pl.when(b >= 4)
        def _():
            at = pl.ds(pl.multiple_of(LEN + (b - 6) * span, 64), LEN)
            TG[...] = dot(jnp.concatenate([GM[m, LEN : 2 * LEN, :] for m in range(MICRO)]), jnp.concatenate([A2[m, at, :] for m in range(MICRO)]), TN)

    if not fused:
        last_grad_hidden()
        loop(LATE_P3, lambda m: stage_p3(m + MICRO - LATE_P3))

        @pl.when(jnp.logical_not(first))
        def _():
            loop(MICRO, stage_out)

        small_gradients()
        relay_drain()

        def whole(b):
            gradient(b)
            out = pltpu.make_async_copy(TG, gout.at[b], l_w.at[0])
            out.start()
            out.wait()

        loop(BLOCKS, whole)
        vout[...] = VS[0]
        return

    kind = lambda p: lax.rem(p + 2, 3)
    slot = lambda p: p // 3
    over_tensor_first = lambda p: kind(p) == 2
    zslot = lambda p: slot(p) + jnp.where(over_tensor_first(p), 3, 0)
    owned = lambda p: jnp.logical_or(over_tensor_first(p), kind(p) == y)
    block = lambda p: jnp.where(p < 7, p + 2, p - 7)
    outer = jnp.logical_or(ten == 0, ten == SHARDS - 1)
    low_side = ten < SHARDS // 2
    FAR, NEAR = jnp.where(low_side, 3, 0), jnp.where(low_side, 2, 1)

    def half_of(half):
        return pl.ds(pl.multiple_of(half * HALF, 16), HALF)

    def part(p, s):
        return CR.at[p, pl.ds(pl.multiple_of(s * HALF, 16), HALF), :]

    def kept(p, s):
        return KEEP.at[lax.rem(p, KEEP_SLOTS), s * HALF : (s + 1) * HALF, :]

    def final(p, half):
        return gout.at[block(p), half_of(half), :]

    def rc(p):
        return remote(GIVE.at[lax.rem(p, GIVE_SLOTS)], CR.at[p], rc_s.at[lax.rem(p, GIVE_SLOTS)], rc_r.at[p], at_core)

    R_Y, R_Z, R_FY, R_FC, R_OUT = range(5)

    def ry(p):
        return remote(CR.at[p], YR.at[slot(p)], r_s.at[R_Y], ry_r.at[slot(p)], at_y)

    def rz(p, s, idx, to):
        return remote(part(p, s), ZR.at[zslot(p), idx], r_s.at[R_Z], rz_r.at[zslot(p), idx], (sec, seq, to))

    def yx(p):
        return remote(part(p, ten), YX.at[slot(p)], yx_s.at[slot(p)], fy_r.at[p], at_y)

    def fy(p):
        return remote(part(p, ten), final(p, core), r_s.at[R_FY], fy_r.at[p], at_y)

    def fc(p, src):
        return remote(src, final(p, core), r_s.at[R_FC], fc_r.at[0], at_core)

    def out_g(p):
        return pltpu.make_async_copy(part(p, ten), final(p, core), r_s.at[R_OUT])

    def add(ref, *others_):
        total = ref[...].astype(f32)
        for other in others_:
            total = total + other[...].astype(f32)
        ref[...] = total.astype(bf16)

    def compute(p):
        @pl.when(p >= GIVE_SLOTS)
        def _():
            rc(p - GIVE_SLOTS).wait_send()

        gradient(block(p))
        for s in range(SHARDS):
            theirs = TG[pl.ds(pl.multiple_of(s * PART + (1 - core) * HALF, 16), HALF), :]
            GIVE[lax.rem(p, GIVE_SLOTS), s * HALF : (s + 1) * HALF, :] = theirs.astype(bf16)
        rc(p).start()
        for s in range(SHARDS):
            kept(p, s)[...] = TG[pl.ds(pl.multiple_of(s * PART + core * HALF, 16), HALF), :].astype(bf16)

    def over_core(p):
        rc(p).wait_recv()
        for s in range(SHARDS):
            add(part(p, s), kept(p, s))

        @pl.when(jnp.logical_not(owned(p)))
        def _():
            ry(p).start()

    def over_y(p):
        @pl.when(owned(p))
        def _():
            ry(p).wait_recv()
            for s in range(SHARDS):
                add(part(p, s), YR.at[slot(p), s * HALF : (s + 1) * HALF, :])

    def chain_one(p):
        @pl.when(jnp.logical_and(owned(p), outer))
        def _():
            for k in range(3):
                s = jnp.where(low_side, 3 - k, k)
                idx = jnp.where(low_side, s - 1, s)
                rz(p, s, idx, jnp.where(low_side, 1, 2)).start()

        @pl.when(jnp.logical_and(owned(p), jnp.logical_not(outer)))
        def _():
            s = jnp.where(low_side, 0, 3)
            rz(p, s, 0, s).start()

    def chain_two(p):
        @pl.when(jnp.logical_and(owned(p), jnp.logical_not(outer)))
        def _():
            for s, idx in ((FAR, jnp.where(low_side, 2, 0)), (NEAR, 1)):
                rz(p, s, idx, s).wait_recv()
                add(part(p, s), ZR.at[zslot(p), idx])
                rz(p, s, 3, s).start()

    def chain_end(p):
        @pl.when(owned(p))
        def _():
            idx, at_z = jnp.where(ten == 2, 2, 0), lax.rem(ten + 1, SHARDS)
            rz(p, ten, idx, at_z).wait_recv()
            rz(p, ten, 3, at_z).wait_recv()
            add(part(p, ten), ZR.at[zslot(p), idx], ZR.at[zslot(p), 3])

            @pl.when(over_tensor_first(p))
            def _():
                yx(p).start()

            @pl.when(jnp.logical_not(over_tensor_first(p)))
            def _():
                fy(p).start()
                fc(p, part(p, ten)).start()
                out_g(p).start()

    def settle(p):
        @pl.when(over_tensor_first(p))
        def _():
            yx(p).wait()
            add(part(p, ten), YX.at[slot(p)])
            fc(p, part(p, ten)).start()
            out_g(p).start()

        @pl.when(jnp.logical_not(owned(p)))
        def _():
            fy(p).wait_recv()
            fc(p, final(p, core)).start()

    def vector_round(i):
        pair, far = ten + 1 - 2 * lax.rem(ten, 2), lax.rem(ten + 2, SHARDS)
        where_seq = jnp.where(i == 0, y * 2 + 1 - core, jnp.where(i == 1, (1 - y) * 2 + core, seq))
        where_ten = jnp.where(i == 2, pair, jnp.where(i == 3, far, ten))
        return remote(VS.at[i], VR.at[i], vr_s.at[i], vr_r.at[i], (sec, where_seq, where_ten))

    def sums(t):
        @pl.when(t == BLOCKS - 2)
        def _():
            last_grad_hidden()

        for stage, lag, first_kind in SCHEDULE:
            p = t - lag
            fits = jnp.logical_and(p >= 0, p < BLOCKS)
            if first_kind is not None:
                fits = jnp.logical_and(fits, over_tensor_first(p) if first_kind else jnp.logical_not(over_tensor_first(p)))

            @pl.when(fits)
            def _():
                dict(compute=compute, core=over_core, y=over_y, one=chain_one, two=chain_two, end=chain_end, settle=settle)[stage](p)

        late = t - BLOCKS

        @pl.when(jnp.logical_and(late >= 0, late < LATE_P3))
        def _():
            stage_p3(late + MICRO - LATE_P3)

        @pl.when(jnp.logical_and(jnp.logical_not(first), jnp.logical_and(late >= 0, late < MICRO)))
        def _():
            stage_out(late)

        i = late - LATE_P3

        @pl.when(i == 0)
        def _():
            small_gradients()

        @pl.when(jnp.logical_and(i > 0, i <= 4))
        def _():
            vector_round(i - 1).wait()
            VS[i] = VS[i - 1] + VR[i - 1]

        @pl.when(jnp.logical_and(i >= 0, i < 4))
        def _():
            vector_round(i).start()

    loop(BLOCKS + LAST_LAG, sums)
    vout[...] = VS[4]

    lines = POOL.at[pl.ds(0, BLOCKS * HALF), :]
    remote(lines, lines, r_s.at[R_FC], fc_r.at[0], at_core).wait()
    relay_drain()
    gather_drain()
    loop(GIVE_SLOTS, lambda i: rc(i).wait_send())
    left(r_s.at[R_Y], 3 * SHARDS * HALF)
    left(r_s.at[R_Z], 6 * 3 * HALF)
    left(r_s.at[R_FY], 3 * HALF)
    lines = POOL.at[pl.ds(0, 6 * HALF), :]
    pltpu.make_async_copy(lines, lines, r_s.at[R_OUT]).wait()


def relay(block_input, cotangent, mask, weights, vectors, fused):
    hbm = pl.BlockSpec(memory_space=pl.ANY)
    vmem = pl.BlockSpec(memory_space=pltpu.VMEM)
    dma = lambda *shape: pltpu.SemaphoreType.DMA(shape)
    low = lambda *shape: pltpu.VMEM(shape, bf16)
    full = lambda *shape: pltpu.VMEM(shape, f32)
    scratch = [
        low(BLOCKS + 1 if fused else BLOCKS, H, H),
        low(2, H, H),
        low(POOL_ROWS, H),
        low(2, ROWS, H),
        low(2, ROWS, H),
        low(MICRO, 3 * LEN, H),
        low(ROWS, H),
        low(ROWS, H),
        low(ROWS, H),
        low(ROWS, H),
        low(ROWS, H),
        low(2, ROWS, H),
        low(MICRO, 3 * LEN, H),
        low(ROWS, H),
        low(ROWS, H),
        full(ROWS, 8),
        full(H, H),
        full(16, H),
        full(2, 8, H),
        full(2, 8, H),
        full(12, 8, H),
        full(5, 16, H),
        dma(2),
        dma(5),
        dma(2),
        dma(1),
        dma(MICRO),
        dma(2),
        dma(MICRO, 2),
        dma(2),
        dma(MICRO, 2),
    ]
    if fused:
        scratch += [
            full(16, 256),
            low(2 * SHARDS, 16, 256),
            low(BLOCKS, SHARDS * HALF, H),
            low(KEEP_SLOTS, SHARDS * HALF, H),
            low(GIVE_SLOTS, SHARDS * HALF, H),
            low(3, SHARDS * HALF, H),
            low(6, 4, HALF, H),
            low(3, HALF, H),
            full(4, 16, H),
            dma(8),
            dma(SHARDS),
            dma(1),
            dma(BLOCKS + 1, SHARDS),
            dma(BLOCKS),
            dma(2),
            dma(1),
            dma(5),
            dma(GIVE_SLOTS),
            dma(BLOCKS),
            dma(3),
            dma(6, 4),
            dma(3),
            dma(BLOCKS),
            dma(1),
            dma(4),
            dma(4),
        ]
    outs = (
        jax.ShapeDtypeStruct((MICRO, LEN, 2 * H), bf16),
        jax.ShapeDtypeStruct((MICRO, LEN, 2 * H), bf16),
        jax.ShapeDtypeStruct((BLOCKS, PART, H), bf16) if fused else jax.ShapeDtypeStruct((BLOCKS, H, H), f32),
        jax.ShapeDtypeStruct((16, H), f32),
    )
    in_specs = [hbm, hbm, vmem] + [hbm] * len(weights) + [vmem] * len(vectors)
    return pl.pallas_call(
        functools.partial(relay_kernel, fused),
        out_shape=outs,
        in_specs=in_specs,
        out_specs=(hbm, hbm, hbm, vmem),
        scratch_shapes=scratch,
        compiler_params=pltpu.CompilerParams(collective_id=0, has_side_effects=True, vmem_limit_bytes=62 * 2**20),
        cost_estimate=pl.CostEstimate(flops=25_000_000_000, bytes_accessed=20_000_000, transcendentals=4_000_000),
        name="relay",
    )(block_input, cotangent, mask, *weights, *vectors)


def unpack_kernel(bo, ig, grads, small, bo_out, ig_out, in_out, mid_out, out_out, *rest):
    vectors, (B, G, F, sems) = rest[:9], rest[9:]
    ten = lax.axis_index("tensor")
    load = pltpu.make_async_copy(grads, G, sems.at[2, 0])
    load.start()
    arrays = [(k, m, src, dst) for k, (src, dst) in enumerate(((bo, bo_out), (ig, ig_out))) for m in range(MICRO)]
    arrive = [pltpu.make_async_copy(src.at[m], B.at[k, m], sems.at[k, m]) for k, m, src, dst in arrays]
    leave = [pltpu.make_async_copy(B.at[k, m], dst.at[0, m, 0], sems.at[4 + k, m]) for k, m, src, dst in arrays]
    for copy in arrive:
        copy.start()
    for z in range(SHARDS):

        @pl.when(ten == z)
        def _():
            for row, ref in zip((0, 1, 2, 3, 4, 5), vectors[:6]):
                ref[...] = small[row : row + 1, z * PART : (z + 1) * PART]
            for i, ref in enumerate(vectors[6:]):
                row, at = 6 + 2 * i + z // 2, z % 2 * 2 * PART
                ref[...] = small[row : row + 1, at : at + 2 * PART]

    load.wait()
    F[...] = G[...].astype(f32)
    outs = [pltpu.make_async_copy(F.at[h + 2 * k], ref.at[:, pl.ds(h * H, H)], sems.at[3, 2 * k + h]) for k, ref in enumerate((in_out, out_out)) for h in range(2)]
    outs += [pltpu.make_async_copy(F.at[pl.ds(4, 5)], mid_out, sems.at[2, 1])]
    for out in outs:
        out.start()
    for came, copy in zip(arrive, leave):
        came.wait()
        copy.start()
    for copy in leave + outs:
        copy.wait()


def unpacked(block_out, input_grad, grads, small):
    hbm, vmem = pl.BlockSpec(memory_space=pl.ANY), pl.BlockSpec(memory_space=pltpu.VMEM)
    like = lambda *shape: jax.ShapeDtypeStruct(shape, f32)
    rows_like = jax.ShapeDtypeStruct((1, MICRO, 1, LEN, 2 * H), bf16)
    (block_out, input_grad, grad_in, grad_mid, grad_out, *vectors) = pl.pallas_call(
        unpack_kernel,
        out_shape=[rows_like, rows_like, like(PART, 2 * H), like(5, PART, H), like(PART, 2 * H)] + [like(1, PART)] * 6 + [like(1, 2 * PART)] * 3,
        in_specs=[hbm, hbm, hbm, vmem],
        out_specs=[hbm] * 5 + [vmem] * 9,
        scratch_shapes=[pltpu.VMEM((2, MICRO, LEN, 2 * H), bf16), pltpu.VMEM((BLOCKS, PART, H), bf16), pltpu.VMEM((BLOCKS, PART, H), f32), pltpu.SemaphoreType.DMA((6, MICRO))],
        compiler_params=pltpu.CompilerParams(vmem_limit_bytes=62 * 2**20),
        name="unpack",
    )(block_out, input_grad, grads, small)
    (bias_in, bias_mid, gain_second, shift_second, gain_third, shift_third, bias_out, gain_first, shift_first) = vectors
    return (
        block_out,
        input_grad,
        grad_in.T[None],
        bias_in,
        grad_mid.transpose(0, 2, 1)[None],
        bias_mid,
        grad_out[None],
        bias_out,
        gain_first,
        shift_first,
        gain_second,
        shift_second,
        gain_third,
        shift_third,
    )


def packed_weights(conv_in, conv_mid, conv_out):
    channels = conv_out.shape[0]
    halves = lambda m: m.reshape(channels, 2, H).transpose(1, 0, 2)
    return jnp.concatenate([halves(conv_in.T), halves(conv_out), conv_mid.transpose(0, 2, 1)])


def local(*args):
    block_input, cotangent, mask = args[:3]
    (conv_in, bias_in, conv_mid, bias_mid, conv_out, bias_out, gain_first, shift_first, gain_second, shift_second, gain_third, shift_third) = (a[0] for a in args[3:])
    ten, sec = lax.axis_index("tensor"), lax.axis_index("section")
    shards = lax.axis_size("tensor")
    fused = shards == SHARDS
    channels = conv_out.shape[0]
    narrow = (bias_in, bias_mid, gain_second, shift_second, gain_third, shift_third)
    wide = (bias_out, gain_first, shift_first)
    if fused:
        weights = (conv_in.T, conv_mid.transpose(0, 2, 1), conv_out)
        block_out, input_grad, grads, small = relay(block_input, cotangent, mask, weights, tuple(v[None] for v in narrow + wide), True)
        return unpacked(block_out, input_grad, grads, small)
    else:
        mine = packed_weights(conv_in, conv_mid, conv_out)
        whole = lax.all_gather(mine, "tensor", axis=1, tiled=True)
        swap = [(0, 1), (1, 0)]
        give = jnp.where(sec == 0, whole[2:4], whole[0:2])
        other = lax.ppermute(give, "section", swap)
        v_narrow = lax.all_gather(jnp.stack(narrow), "tensor", axis=1, tiled=True)
        v_wide = lax.all_gather(jnp.stack(wide), "tensor", axis=1, tiled=True)
        v640 = jnp.pad(v_narrow.astype(f32), ((0, 10), (0, 0)))
        v1280 = jnp.pad(v_wide.astype(f32).reshape(3, 2, H).transpose(1, 0, 2), ((0, 0), (0, 5), (0, 0)))
        vx = lax.ppermute(v1280, "section", swap)
        block_out, input_grad, grads, small = relay(block_input, cotangent, mask, (whole, other), (v640, v1280, vx), False)
        grads = lax.psum(lax.psum_scatter(grads, "tensor", scatter_dimension=1, tiled=True), "seq")
        small = lax.psum(small, ("seq", "tensor"))
    grad_in = grads[0:2].transpose(0, 2, 1).reshape(2 * H, channels)
    grad_out = grads[2:4].transpose(1, 0, 2).reshape(channels, 2 * H)
    grad_mid = grads[4:9].transpose(0, 2, 1)
    thin = lax.dynamic_slice_in_dim(small[0:6], ten * channels, channels, 1)
    thick = lax.dynamic_slice_in_dim(small[6:12].reshape(3, 2 * H), ten * 2 * channels, 2 * channels, 1)
    shape = (1, MICRO, 1, LEN, 2 * H)
    return (
        block_out.reshape(shape),
        input_grad.reshape(shape),
        grad_in[None],
        thin[0:1],
        grad_mid[None],
        thin[1:2],
        grad_out[None],
        thick[0:1],
        thick[1:2],
        thick[2:3],
        thin[2:3],
        thin[3:4],
        thin[4:5],
        thin[5:6],
    )


def solution(mesh):
    in_specs = (
        P(None, "tensor", "seq", None),
        P(None, "tensor", "seq", None),
        P(None, "tensor", "seq"),
        P("section", None, "tensor"),
        P("section", "tensor"),
        P("section", None, None, "tensor"),
        P("section", "tensor"),
        P("section", "tensor", None),
        P("section", "tensor"),
        P("section", "tensor"),
        P("section", "tensor"),
        P("section", "tensor"),
        P("section", "tensor"),
        P("section", "tensor"),
        P("section", "tensor"),
    )
    out_specs = (
        P("section", None, "tensor", "seq", None),
        P("section", None, "tensor", "seq", None),
        P("section", None, "tensor"),
        P("section", "tensor"),
        P("section", None, None, "tensor"),
        P("section", "tensor"),
        P("section", "tensor", None),
        P("section", "tensor"),
        P("section", "tensor"),
        P("section", "tensor"),
        P("section", "tensor"),
        P("section", "tensor"),
        P("section", "tensor"),
        P("section", "tensor"),
    )
    return jax.shard_map(local, mesh=mesh, in_specs=in_specs, out_specs=out_specs, check_vma=False)
```
